256 devices in a mesh: context: 32 (over z, x), dp: 8 (over y, core).
Axes of the slice: x: 4, y: 4, z: 8, core: 2. Of those that a mesh axis runs over, the one named last changes fastest.
Arguments:
- bases: int32 [8, 16384], P('dp', 'context'), may hold values from 0 to 3
- organism: int32 [8], P('dp'), may hold values from 0 to 1, as said below
- embed_weight: bfloat16 [60, 768], replicated, may hold values from -1.5 to 1.5
- conv_weight: bfloat16 [768, 3840], P('context'), may hold values from -0.21875 to 0.21875
- deep_weight: bfloat16 [1536, 3840], P('context'), may hold values from -0.09375 to 0.09375
- human_head: bfloat16 [1536, 5888], P(None, 'context'), may hold values from -0.15625 to 0.15625
- mouse_head: bfloat16 [1536, 1024], P(None, 'context'), may hold values from -0.15625 to 0.15625
- human_cotangent: bfloat16 [8, 128, 5888], P('dp', None, 'context'), may hold values from -0.59765625 to 0.59765625
- mouse_cotangent: bfloat16 [8, 128, 1024], P('dp', None, 'context'), may hold values from -0.59765625 to 0.59765625
Outputs:
- grad_embed: float32 [60, 768], replicated
- grad_conv: float32 [768, 3840], P('context')
- grad_deep: float32 [1536, 3840], P('context')
- grad_human: float32 [1536, 5888], P('dp', 'context')
- grad_mouse: float32 [1536, 1024], P('dp', 'context')
- first_delta: float32 [8, 16384, 768], P('dp', 'context')
The draws below stay inside these ranges and needn't reach their ends.
Inputs may be any that keep to these rules, and one draw needn't show every extreme that they name: `organism`: exactly half of the 8 windows are mouse windows.
All inputs are finite; a program needn't handle non-finite values.
Results may differ from the reference program's by a relative error of at most 0.035.
Values may be sent and summed in bfloat16 or wider, within the bound.
A program may use at most 128 MiB of HBM per device.

```python
import jax
import jax.numpy as jnp
from jax import lax

WIDTH = 768
DEEP = 1536
HUMAN_TRACKS = 5888
MOUSE_TRACKS = 1024
EMBED_SPAN = 15
CONV_SPAN = 5
POOL = 128
BATCH = 8
LENGTH = 16384
COARSE = 128


def draw_organism(key, part):
    key = jax.random.fold_in(key, 11)
    order = jax.random.permutation(key, BATCH)
    return (order % 2).astype(jnp.int32)


def plant(values, key, low, largest):
    longest = values.shape.index(max(values.shape))
    spots = []
    for shift in (0, 1):
        where = [jax.random.randint(jax.random.fold_in(key, axis), (), 0, length) for axis, length in enumerate(values.shape)]
        where[longest] = (where[longest] + shift) % values.shape[longest]
        spots.append(tuple(where))
    return values.at[spots[0]].set(low).at[spots[1]].set(largest)


def steps_of(key, dims, shards, low, top_value):
    def one(position, parts):
        draws = jax.random.uniform(jax.random.fold_in(jax.random.fold_in(key, 6), position), (parts,), jnp.float32, low / len(shards), top_value / len(shards))
        return jnp.repeat(jnp.exp(draws), dims[position] // parts).reshape((-1,) + (1,) * (len(dims) - position - 1))

    loudness = one(*shards[0])
    for cut in shards[1:]:
        loudness = loudness * one(*cut)
    return loudness


def scatter_about(own_key, dims, spread, limit, cuts=(), kind=jnp.bfloat16):
    entries = jax.random.normal(own_key, dims, jnp.float32) * spread
    if len(cuts) > 0:
        entries = steps_of(own_key, dims, cuts, -0.22, 0.18) * entries
    return jnp.clip(entries, min=-limit, max=limit).astype(kind)


def setup_inputs(seed: int = 0) -> dict:
    seeds = jax.random.split(jax.random.key(seed), 10)
    bases = plant(jax.random.randint(seeds[0], (BATCH, LENGTH), 0, 4), jax.random.fold_in(seeds[0], 1), 0, 3).astype(jnp.int32)
    organism = draw_organism(jax.random.fold_in(seeds[9], 71), 0)
    embed_weight = scatter_about(seeds[2], (EMBED_SPAN * 4, WIDTH), EMBED_SPAN ** -0.5, 1.5)
    conv_weight = scatter_about(seeds[3], (WIDTH, CONV_SPAN * WIDTH), WIDTH ** -0.5, 0.21875, ((0, 32),))
    deep_weight = scatter_about(seeds[4], (DEEP, CONV_SPAN * WIDTH), (CONV_SPAN * WIDTH) ** -0.5, 0.09375, ((0, 32),))
    human_head = scatter_about(seeds[5], (DEEP, HUMAN_TRACKS), DEEP ** -0.5, 0.15625, ((1, 32),))
    mouse_head = scatter_about(seeds[6], (DEEP, MOUSE_TRACKS), DEEP ** -0.5, 0.15625, ((1, 32),))
    human_cotangent = scatter_about(seeds[7], (BATCH, COARSE, HUMAN_TRACKS), 0.1, 0.59765625, ((0, 8), (2, 32)))
    mouse_cotangent = scatter_about(seeds[8], (BATCH, COARSE, MOUSE_TRACKS), 0.1, 0.59765625, ((0, 8), (2, 32)))
    return dict(bases=bases, organism=organism, embed_weight=embed_weight, conv_weight=conv_weight, deep_weight=deep_weight, human_head=human_head, mouse_head=mouse_head, human_cotangent=human_cotangent, mouse_cotangent=mouse_cotangent)


SLOPE = 0.7978845608028654
CUBIC = 0.044715
EPSILON = 1e-06

def gelu_value(value):
    return 0.5 * value * (1.0 + jnp.tanh(SLOPE * (value + CUBIC * value * value * value)))

def gelu_slope(value):
    tangent = jnp.tanh(SLOPE * (value + CUBIC * value * value * value))
    return 0.5 * (1.0 + tangent) + 0.5 * value * (1.0 - tangent * tangent) * SLOPE * (1.0 + 3.0 * CUBIC * value * value)

def normalize(source):
    values = source.astype(jnp.float32)
    factor = lax.rsqrt(lax.optimization_barrier(jnp.mean(values * values, axis=-1, keepdims=True)) + EPSILON)
    return (values * factor, factor)

def norm_back(upstream, normed, factor):
    return factor * (upstream - normed * lax.optimization_barrier(jnp.mean(upstream * normed, axis=-1, keepdims=True)))

def conv_forward(source, weight, span):
    half = span // 2
    length, channels = source.shape
    padded = jnp.pad(source, ((half, half), (0, 0)))
    total = jnp.zeros((length, weight.shape[0]), jnp.float32)
    for offset in range(span):
        block = weight[:, offset * channels:(offset + 1) * channels]
        total = total + jnp.dot(padded[offset:offset + length], block.T, preferred_element_type=jnp.float32)
    return total

def conv_weight_grad(delta, source, span):
    half = span // 2
    length = source.shape[0]
    padded = jnp.pad(source, ((half, half), (0, 0)))
    blocks = [jnp.dot(delta.T, padded[offset:offset + length], preferred_element_type=jnp.float32) for offset in range(span)]
    return jnp.concatenate(blocks, axis=1)

def conv_input_grad(delta, weight, span):
    half = span // 2
    length = delta.shape[0]
    channels = weight.shape[1] // span
    padded = jnp.pad(delta, ((half, half), (0, 0)))
    total = jnp.zeros((length, channels), jnp.float32)
    for offset in range(span):
        block = weight[:, offset * channels:(offset + 1) * channels]
        total = total + jnp.dot(padded[2 * half - offset:2 * half - offset + length], block, preferred_element_type=jnp.float32)
    return total

def reference(bases, organism, embed_weight, conv_weight, deep_weight, human_head, mouse_head, human_cotangent, mouse_cotangent):
    reach = EMBED_SPAN // 2

    def window(carry, inputs):
        embed_sum, conv_sum, deep_sum, human_sum, mouse_sum = carry
        sites, label, human_cot, mouse_cot = inputs
        padded_sites = jnp.pad(sites, (reach, reach), constant_values=-1)
        codes = jnp.arange(4, dtype=jnp.int32)
        onehot = (padded_sites[:, None] == codes[None, :]).astype(jnp.bfloat16)
        length = sites.shape[0]
        first = jnp.zeros((length, WIDTH), jnp.float32)
        for offset in range(EMBED_SPAN):
            first = first + jnp.dot(onehot[offset:offset + length], embed_weight[4 * offset:4 * offset + 4], preferred_element_type=jnp.float32)
        first = first.astype(jnp.bfloat16)
        normed, factor = normalize(first)
        active = gelu_value(normed).astype(jnp.bfloat16)
        mixed = conv_forward(active, conv_weight, CONV_SPAN)
        pooled = (first.astype(jnp.float32) + gelu_value(mixed)).reshape(-1, POOL, WIDTH).mean(axis=1).astype(jnp.bfloat16)
        deep_normed, deep_factor = normalize(pooled)
        deep_active = gelu_value(deep_normed).astype(jnp.bfloat16)
        features = conv_forward(deep_active, deep_weight, CONV_SPAN).astype(jnp.bfloat16)
        human_logit = jnp.dot(features, human_head, preferred_element_type=jnp.float32)
        mouse_logit = jnp.dot(features, mouse_head, preferred_element_type=jnp.float32)
        is_human = (label == 0).astype(jnp.float32)
        human_delta = (is_human * human_cot.astype(jnp.float32) * jax.nn.sigmoid(human_logit)).astype(jnp.bfloat16)
        mouse_delta = ((1.0 - is_human) * mouse_cot.astype(jnp.float32) * jax.nn.sigmoid(mouse_logit)).astype(jnp.bfloat16)
        human_sum = human_sum + jnp.dot(features.T, human_delta, preferred_element_type=jnp.float32)
        mouse_sum = mouse_sum + jnp.dot(features.T, mouse_delta, preferred_element_type=jnp.float32)
        feature_delta = (jnp.dot(human_delta, human_head.T, preferred_element_type=jnp.float32) + jnp.dot(mouse_delta, mouse_head.T, preferred_element_type=jnp.float32)).astype(jnp.bfloat16)
        deep_sum = deep_sum + conv_weight_grad(feature_delta, deep_active, CONV_SPAN)
        deep_back = conv_input_grad(feature_delta, deep_weight, CONV_SPAN)
        pool_delta = norm_back(deep_back * gelu_slope(deep_normed), deep_normed, deep_factor)
        block_delta = jnp.repeat(pool_delta, POOL, axis=0) / POOL
        fine_delta = (block_delta * gelu_slope(mixed)).astype(jnp.bfloat16)
        conv_sum = conv_sum + conv_weight_grad(fine_delta, active, CONV_SPAN)
        conv_back = conv_input_grad(fine_delta, conv_weight, CONV_SPAN)
        first_delta = block_delta + norm_back(conv_back * gelu_slope(normed), normed, factor)
        onehot_wide = onehot.astype(jnp.float32)
        blocks = [jnp.dot(onehot_wide[offset:offset + length].T, first_delta, precision=lax.Precision.HIGHEST, preferred_element_type=jnp.float32) for offset in range(EMBED_SPAN)]
        embed_sum = embed_sum + jnp.concatenate(blocks, axis=0)
        return ((embed_sum, conv_sum, deep_sum, human_sum, mouse_sum), first_delta)
    start = (jnp.zeros((EMBED_SPAN * 4, WIDTH), jnp.float32), jnp.zeros((WIDTH, CONV_SPAN * WIDTH), jnp.float32), jnp.zeros((DEEP, CONV_SPAN * WIDTH), jnp.float32), jnp.zeros((DEEP, HUMAN_TRACKS), jnp.float32), jnp.zeros((DEEP, MOUSE_TRACKS), jnp.float32))
    totals, deltas = lax.scan(window, start, (bases, organism, human_cotangent, mouse_cotangent))
    return (totals[0], totals[1], totals[2], totals[3], totals[4], deltas)
```

```python
import jax
import jax.numpy as jnp
from jax import lax
from jax.experimental import pallas as pl
from jax.experimental.pallas import tpu as pltpu
from jax.sharding import PartitionSpec as P

F32 = jnp.float32
BF = jnp.bfloat16
MESH = pl.DeviceIdType.MESH

WIDTH = 768
SPAN = 5
NZ, NX, NY = 8, 4, 4
ND = 8
ROWS = 512
OFF = 16
EXT = ROWS + 2 * OFF
WIDE = 640
HALF = 1920
SPLIT = 1024

SLOPE = 0.7978845608028654
CUBIC = 0.044715
EPSILON = 1e-06


def gelu_both(value):
    square = value * value
    tangent = jnp.tanh(SLOPE * (value + CUBIC * square * value))
    half = 0.5 * (1.0 + tangent)
    slope = half + 0.5 * value * (1.0 - tangent * tangent) * SLOPE * (1.0 + 3.0 * CUBIC * square)
    return value * half, slope


def gelu_value(value):
    return 0.5 * value * (1.0 + jnp.tanh(SLOPE * (value + CUBIC * value * value * value)))


def gelu_slope(value):
    return gelu_both(value)[1]


def dot(a, b, ca=1, cb=0):
    return lax.dot_general(a, b, (((ca,), (cb,)), ((), ())), preferred_element_type=F32)


def loop(count, body, unroll=1):
    def step(i, carry):
        body(i)
        return carry

    lax.fori_loop(0, count, step, 0, unroll=unroll)


def kernel(
    bases, embed, cw, dw, hm, cot,
    o_ge, o_gc, o_gd, o_gh, o_gm, o_fd,
    hl, hr, e_ref, et_ref, embp, fpad, first, nm_ref, gn_ref, fac_ref, acols, wg, wf, mixed, ah,
    pbuf, dn_ref, dpad, df_ref, dcols, ft, dtx, fxs, fbs, fxr, fzs, fzr, fdx, fkx, dw2, dbp, dbs, dxr, dzs, dzr,
    dax, pd_ref, fdp, fdc, fdt,
    ga, gb, gar, gbr, ha, hb, har, hbr, zs, zr, fin,
    fdl, fhl, ep, er, ex, ey, eg,
    s_h, r_h, s_w, r_w, s_p, r_p, s_f, r_f, s_rf, r_rf, s_rd, r_rd, s_d, r_d, s_g, r_g, s_e, r_e, s_o,
):
    c = lax.axis_index("context")
    d = lax.axis_index("dp")
    z, x = c // NX, c % NX
    y, k = d // 2, d % 2
    sends = []

    def zp(i):
        return lax.rem(z + i + NZ, NZ)

    def xp(i):
        return lax.rem(x + i + NX, NX)

    def dpp(i):
        return lax.rem(d + i + ND, ND)

    def yp(i):
        return lax.rem(y + i + NY, NY)

    def send(src, dst, ss, rs, **to):
        copy = pltpu.make_async_remote_copy(
            src_ref=src, dst_ref=dst, send_sem=ss, recv_sem=rs, device_id=to, device_id_type=MESH
        )
        copy.start()
        sends.append(copy)

    def wait(dst, rs):
        pltpu.make_async_remote_copy(
            src_ref=dst, dst_ref=dst, send_sem=rs, recv_sem=rs, device_id={"context": zp(1) * NX + x}, device_id_type=MESH
        ).wait_recv()

    barrier = pltpu.get_barrier_semaphore()
    for i in range(1, NZ):
        pl.semaphore_signal(barrier, inc=1, device_id={"context": zp(i) * NX + x}, device_id_type=MESH)
    for i in range(1, NX):
        pl.semaphore_signal(barrier, inc=1, device_id={"context": z * NX + xp(i)}, device_id_type=MESH)
    for i in range(1, ND):
        pl.semaphore_signal(barrier, inc=1, device_id={"dp": dpp(i)}, device_id_type=MESH)
    right, left = lax.rem(c + 1, NZ * NX), lax.rem(c + NZ * NX - 1, NZ * NX)
    pl.semaphore_signal(barrier, inc=1, device_id={"context": right}, device_id_type=MESH)
    pl.semaphore_signal(barrier, inc=1, device_id={"context": left}, device_id_type=MESH)
    wg[z, x] = cw[...]
    pl.semaphore_wait(barrier, NZ - 1 + NX - 1 + ND - 1 + 2)

    mine = pl.multiple_of(HALF * k, 128)
    other = pl.multiple_of(HALF * (1 - k), 128)
    c0 = pl.ds(mine, SPLIT)
    c1 = pl.ds(pl.multiple_of(mine + SPLIT, 128), HALF - SPLIT)
    o0 = pl.ds(other, SPLIT)
    o1 = pl.ds(pl.multiple_of(other + SPLIT, 128), HALF - SPLIT)
    sib = 2 * y + 1 - k

    def blk1(q):
        return wg.at[zp(-q), x, :, c1]

    def to_z(i):
        return dict(context=zp(i) * NX + x)

    def to_x(i):
        return dict(context=z * NX + xp(i))

    send(bases.at[:, pl.ds(ROWS - 128, 128)], hl, s_h.at[0], r_h.at[0], context=right)
    send(bases.at[:, pl.ds(0, 128)], hr, s_h.at[1], r_h.at[1], context=left)
    for i in range(1, NX):
        send(wg.at[z, x, :, c0], wg.at[z, x, :, c0], s_w.at[0, i], r_w.at[0, i], **to_x(i))
    send(blk1(0), blk1(0), s_w.at[1, 1], r_w.at[1, 1], **to_z(1))
    send(blk1(0), blk1(0), s_w.at[2, 1], r_w.at[2, 1], **to_z(-1))
    for i in range(1, NX):
        send(blk1(0), blk1(0), s_w.at[4 + i, 0], r_w.at[4 + i, 0], **to_x(i))

    rows60 = lax.broadcasted_iota(jnp.int32, (64, 60), 0)
    cols60 = lax.broadcasted_iota(jnp.int32, (64, 60), 1)
    place = jnp.where(cols60 == 4 * (15 - rows60 % 16) + rows60 // 16, 1.0, 0.0).astype(BF)
    embp[...] = dot(place, embed[...]).astype(BF)
    wait(hl, r_h.at[0])
    wait(hr, r_h.at[1])
    before = jnp.where(c == 0, -1, hl[...])
    after = jnp.where(c == NZ * NX - 1, -1, hr[...])
    line = jnp.concatenate([before, bases[...], after], axis=1)
    rolled = pltpu.roll(jnp.broadcast_to(line, (16, ROWS + 256)), 648, 1, stride=1, stride_axis=0)
    for j in range(4):
        e_ref[16 * j : 16 * j + 16, :] = jnp.where(rolled[:, :WIDE] == j, 1.0, 0.0).astype(BF)
    for i in range(WIDE // 128):
        block = e_ref[:, 128 * i : 128 * i + 128].astype(F32)
        et_ref[128 * i : 128 * i + 128, :] = block.T.astype(BF)
    fpad[0:8, :] = jnp.zeros((8, WIDTH), F32)

    def embed_step(i):
        r0 = pl.multiple_of(i * 32, 32)
        values = dot(et_ref[pl.ds(r0, 32), :], embp[...]).astype(BF)
        first[pl.ds(r0, 32), :] = values
        values = values.astype(F32)
        factor = lax.rsqrt(jnp.mean(values * values, axis=1, keepdims=True) + EPSILON)
        normed = values * factor
        value, slope = gelu_both(normed)
        spot = lax.broadcasted_iota(jnp.int32, (32, WIDTH), 0) + (c * ROWS + r0 - OFF)
        inside = jnp.logical_and(spot >= 0, spot < ROWS * NZ * NX)
        value = jnp.where(inside, value, 0.0)
        fpad[pl.ds(r0 + 8, 32), :] = value.astype(BF).astype(F32)
        nm_ref[pl.ds(r0, 32), :] = normed
        gn_ref[pl.ds(r0, 32), :] = slope
        fac_ref[pl.ds(r0, 32), :] = jnp.broadcast_to(factor, (32, 128))

    loop(WIDE // 32, embed_step)

    def ring1_up(s):
        wait(blk1(s), r_w.at[1, s])
        if s < 4:
            send(blk1(s), blk1(s), s_w.at[1, s + 1], r_w.at[1, s + 1], **to_z(1))
        spread1(s)

    def ring1_down(s):
        q = NZ - s
        wait(blk1(q), r_w.at[2, s])
        if s < 3:
            send(blk1(q), blk1(q), s_w.at[2, s + 1], r_w.at[2, s + 1], **to_z(-1))
        spread1(q)

    def spread1(q):
        for i in range(1, NX):
            send(blk1(q), blk1(q), s_w.at[4 + i, q], r_w.at[4 + i, q], **to_x(i))
        send(blk1(q), blk1(q), s_w.at[8, q], r_w.at[8, q], dp=sib)

    def blk0(q, cols=c0):
        return wg.at[zp(-q), :, :, cols]

    def ring0_up(s):
        wait(blk0(s), r_w.at[3, s])
        if s < 4:
            send(blk0(s), blk0(s), s_w.at[3, s + 1], r_w.at[3, s + 1], **to_z(1))
        send(blk0(s), blk0(s), s_w.at[10, s], r_w.at[10, s], dp=sib)

    def ring0_down(s):
        q = NZ - s
        wait(blk0(q), r_w.at[4, s])
        if s < 3:
            send(blk0(q), blk0(q), s_w.at[4, s + 1], r_w.at[4, s + 1], **to_z(-1))
        send(blk0(q), blk0(q), s_w.at[10, q], r_w.at[10, q], dp=sib)

    ring1_up(1)
    ring1_down(1)
    for i in range(1, NX):
        here = wg.at[z, xp(-i), :, c0]
        wait(here, r_w.at[0, i])
        send(here, here, s_w.at[9, i], r_w.at[9, i], dp=sib)
    send(blk0(0), blk0(0), s_w.at[3, 1], r_w.at[3, 1], **to_z(1))
    send(blk0(0), blk0(0), s_w.at[4, 1], r_w.at[4, 1], **to_z(-1))
    ring1_up(2)
    ring1_down(2)

    def shift_step(i):
        r0 = pl.multiple_of(i * 32, 32)
        block = fpad[pl.ds(r0, 48), :]
        for t in range(SPAN):
            acols[t, pl.ds(r0, 32), :] = block[t + 6 : t + 38].astype(BF)

    loop(EXT // 32, shift_step)
    ring1_up(3)
    ring1_down(3)
    ring0_up(1)
    ring0_down(1)
    ring1_up(4)
    ring0_up(2)
    ring0_down(2)
    ring0_up(3)
    ring0_down(3)
    ring0_up(4)
    for i in range(1, NX):
        for q in range(NZ):
            here = wg.at[zp(-q), xp(-i), :, c1]
            wait(here, r_w.at[4 + i, q])
        here = wg.at[:, xp(-i), :, c1]
        send(here, here, s_w.at[11, i], r_w.at[11, i], dp=sib)
    own_cols = pl.ds(pl.multiple_of((WIDTH // 2) * k, 128), WIDTH // 2)
    sib_cols = pl.ds(pl.multiple_of((WIDTH // 2) * (1 - k), 128), WIDTH // 2)
    local = []
    for t in range(SPAN):
        dst = ah.at[pl.ds(0, ROWS), pl.ds(384 * t, 384)]
        copy = pltpu.make_async_copy(acols.at[t, pl.ds(OFF, ROWS), own_cols], dst, s_o.at[t])
        copy.start()
        local.append(copy)
        send(
            acols.at[t, pl.ds(OFF, ROWS), sib_cols], ah.at[pl.ds(ROWS, ROWS), pl.ds(384 * t, 384)],
            s_d.at[4, t], r_d.at[4, t], dp=sib,
        )
    ah[:, pl.ds(HALF, 128)] = jnp.zeros((2 * ROWS, 128), BF)
    for q in range(1, NZ):
        wait(wg.at[zp(-q), x, :, o1], r_w.at[8, q])
        wait(blk0(q, o0), r_w.at[10, q])
    for i in range(1, NX):
        wait(wg.at[z, xp(-i), :, o0], r_w.at[9, i])
        wait(wg.at[:, xp(-i), :, o1], r_w.at[11, i])

    def pack_step(i):
        zz, half = i // 2, 2 * (i % 2)
        pair = jnp.concatenate([wg[zz, half].astype(F32), wg[zz, half + 1].astype(F32)], axis=0)
        wf[pl.ds(pl.multiple_of(48 * i, 16), 48), :] = pair.astype(BF)

    loop(16, pack_step)

    def conv_step(i):
        o0_ = pl.multiple_of(i * 256, 256)
        total = dot(acols[0], wf[pl.ds(o0_, 256), 0:WIDTH], 1, 1)
        for t in range(1, SPAN):
            total = total + dot(acols[t], wf[pl.ds(o0_, 256), WIDTH * t : WIDTH * (t + 1)], 1, 1)
        mixed[:, pl.ds(o0_, 256)] = total

    loop(3, conv_step)

    for t in range(4):
        def pool_step(i, total):
            r0 = pl.multiple_of(OFF + 128 * t + 32 * i, 16)
            part = first[pl.ds(r0, 32), :].astype(F32) + gelu_value(mixed[pl.ds(r0, 32), :])
            return total + part.reshape(4, 8, WIDTH).sum(axis=0)

        total = lax.fori_loop(0, 4, pool_step, jnp.zeros((8, WIDTH), F32))
        row = (jnp.sum(total, axis=0, keepdims=True) / 128.0).astype(BF).astype(F32)
        pbuf[z, x, t : t + 1, :] = row[:, :384]
        pbuf[z, x, 4 + t : 5 + t, :] = row[:, 384:]

    def relay_gather(buf, ss, rs, between=None):
        for i in range(1, NZ):
            send(buf.at[z, x], buf.at[z, x], ss.at[i], rs.at[i], **to_z(i))
        if between is not None:
            between()
        for i in range(1, NZ):
            wait(buf.at[zp(-i), x], rs.at[i])
        for i in range(1, NX):
            send(buf.at[:, x], buf.at[:, x], ss.at[7 + i], rs.at[7 + i], **to_x(i))

    def relay_finish(buf, rs):
        for i in range(1, NX):
            wait(buf.at[:, xp(-i)], rs.at[7 + i])

    relay_gather(pbuf, s_p, r_p)

    def slope_step(i):
        r0 = pl.multiple_of(i * 32, 32)
        mixed[pl.ds(r0, 32), :] = gelu_slope(mixed[pl.ds(r0, 32), :])

    loop(EXT // 32, slope_step)
    for t in range(SPAN):
        dw2[48 * t : 48 * t + 48, :] = dw[:, WIDTH * t : WIDTH * (t + 1)]
    zero8 = jnp.zeros((8, WIDTH), F32)
    dn_ref[0:8, :] = zero8
    dn_ref[136:144, :] = zero8
    dpad[0:8, :] = zero8
    dpad[136:144, :] = zero8
    dbp[0:8, :] = zero8
    dbp[136:144, :] = zero8
    df_ref[...] = jnp.ones((144, 128), F32)
    relay_finish(pbuf, r_p)

    def coarse_step(i):
        zz, half = i // 2, 2 * (i % 2)
        v0, v1 = pbuf[zz, half], pbuf[zz, half + 1]
        top = jnp.concatenate([v0[:4], v1[:4]], axis=0)
        bottom = jnp.concatenate([v0[4:], v1[4:]], axis=0)
        values = jnp.concatenate([top, bottom], axis=1)
        factor = lax.rsqrt(jnp.mean(values * values, axis=1, keepdims=True) + EPSILON)
        normed = values * factor
        r0 = pl.multiple_of(8 * i + 8, 8)
        dn_ref[pl.ds(r0, 8), :] = normed
        df_ref[pl.ds(r0, 8), :] = jnp.broadcast_to(factor, (8, 128))
        dpad[pl.ds(r0, 8), :] = gelu_value(normed).astype(BF).astype(F32)

    loop(16, coarse_step)
    block = dpad[...]
    for t in range(SPAN):
        dcols[t] = block[t + 6 : t + 134].astype(BF)
    total = dot(dw[:, 0:WIDTH], dcols[0], 1, 1)
    for t in range(1, SPAN):
        total = total + dot(dw[:, WIDTH * t : WIDTH * (t + 1)], dcols[t], 1, 1)
    ft[z, x] = total.astype(BF)
    dax[pl.ds(pl.multiple_of(d * 128, 128), 128), :] = dcols[2]

    def dp_slot(ref, i, size):
        return ref.at[pl.ds(pl.multiple_of(i * size, 16), size)]

    def coarse_background():
        for i in range(1, ND):
            send(dcols.at[2], dp_slot(dax, d, 128), s_d.at[0, i], r_d.at[0, i], dp=dpp(i))

    relay_gather(ft, s_f, r_f, coarse_background)
    relay_finish(ft, r_f)

    feats = ft[...].reshape(1536, 128)
    logit = dot(hm[...], feats, 0, 0)
    delta = (cot[...].astype(F32) * jax.nn.sigmoid(logit)).astype(BF)
    dtx[d] = delta
    fbs[...] = dot(hm[...], delta).astype(BF).reshape(NZ, NX, 48, 128)
    for i in range(1, NX):
        send(fbs.at[:, xp(i)], fxr.at[i], s_rf.at[i], r_rf.at[i], **to_x(i))
    for i in range(1, ND):
        send(dtx.at[d], dtx.at[d], s_d.at[1, i], r_d.at[1, i], dp=dpp(i))
        send(ft.at[dpp(i)], fxs.at[d], s_d.at[2, i], r_d.at[2, i], dp=dpp(i))
    fxs[d] = ft[d]

    def finish_rs(own, got, zsrc, zgot, ss, rs):
        for i in range(1, NX):
            wait(got.at[i], rs.at[i])
        zsrc[...] = (
            own[:, x].astype(F32) + got[1].astype(F32) + got[2].astype(F32) + got[3].astype(F32)
        ).astype(BF)
        for i in range(1, NZ):
            send(zsrc.at[zp(i)], zgot.at[i], ss.at[3 + i], rs.at[3 + i], **to_z(i))

    def finish_sum(zsrc, zgot, rs):
        total = zsrc[z].astype(F32)
        for i in range(1, NZ):
            wait(zgot.at[i], rs.at[3 + i])
        for i in range(1, NZ):
            total = total + zgot[i].astype(F32)
        return total

    finish_rs(fbs, fxr, fzs, fzr, s_rf, r_rf)
    fdelta = finish_sum(fzs, fzr, r_rf).astype(BF)
    fdx[d] = fdelta
    for i in range(1, ND):
        send(fdx.at[d], fdx.at[d], s_d.at[3, i], r_d.at[3, i], dp=dpp(i))

    lanes = lax.broadcasted_iota(jnp.int32, (48, 128), 1)

    def shifted(values):
        wide = values.astype(F32)
        parts = []
        for t in range(SPAN):
            move = t - 2
            if move == 0:
                parts.append(wide)
                continue
            turned = pltpu.roll(wide, move % 128, 1)
            keep = lanes >= move if move > 0 else lanes < 128 + move
            parts.append(jnp.where(keep, turned, 0.0))
        return jnp.concatenate(parts, axis=0).astype(BF)

    back = dot(shifted(fdelta), dw2[...], 0, 0)
    dbp[8:136, :] = back

    def piece_step(i):
        block = dbp[pl.ds(pl.multiple_of(8 * i, 8), 24), :]
        zz, half = i // 2, 2 * (i % 2)
        for j, low in ((0, 6), (1, 10)):
            rows = block[low : low + 8]
            dbs[zz, half + j] = jnp.concatenate([rows[:, :384], rows[:, 384:]], axis=0).astype(BF)

    loop(16, piece_step)
    for i in range(1, NX):
        send(dbs.at[:, xp(i)], dxr.at[i], s_rd.at[i], r_rd.at[i], **to_x(i))
    finish_rs(dbs, dxr, dzs, dzr, s_rd, r_rd)

    for i in range(1, ND):
        wait(dtx.at[dpp(-i)], r_d.at[1, i])
        wait(fxs.at[dpp(-i)], r_d.at[2, i])
    total = jnp.zeros((192, 256), F32)
    for i in range(ND):
        total = total + dot(fxs[i].reshape(192, 128), dtx[i], 1, 1)
    o_gh[...] = total[:, :184]
    o_gm[...] = total[:, 192:224]

    deep_back = finish_sum(dzs, dzr, r_rd)
    deep_back = jnp.concatenate([deep_back[:8], deep_back[8:]], axis=1)
    r0 = pl.multiple_of(8 * (c // 2), 8)

    def own_rows(ref):
        block = ref[pl.ds(r0, 24), :]
        return jnp.where(c % 2 == 0, block[6:14], block[10:18])

    dnormed = own_rows(dn_ref)
    dfactor = own_rows(df_ref)[:, :1]
    v = deep_back * gelu_slope(dnormed)
    pd_ref[...] = dfactor * (v - dnormed * jnp.mean(v * dnormed, axis=1, keepdims=True)) / 128.0

    fdp[0:8, :] = zero8
    fdp[EXT + 8 : EXT + 16, :] = zero8

    def fine_step(i):
        r0 = pl.multiple_of(i * 16, 16)
        row = pd_ref[pl.ds((r0 + 112) // 128 + 1, 1), :]
        fine = (mixed[pl.ds(r0, 16), :] * row).astype(BF).astype(F32)
        fdp[pl.ds(r0 + 8, 16), :] = fine

    loop(EXT // 16, fine_step, unroll=2)
    for i in range(4):
        block = fdp[OFF + 8 + 128 * i : OFF + 136 + 128 * i, :]
        fdt[0, :, 128 * i : 128 * i + 128] = block.T.astype(BF)
    send(fdt.at[0], fdt.at[1], s_g.at[0, 0], r_g.at[0, 0], dp=sib)

    def back_shift(i):
        r0 = pl.multiple_of(i * 32, 32)
        block = fdp[pl.ds(r0, 48), :]
        for t in range(SPAN):
            fdc[t, pl.ds(r0, 32), :] = block[10 - t : 42 - t].astype(BF)

    loop(EXT // 32, back_shift)
    for copy in local:
        copy.wait()
    for t in range(SPAN):
        wait(ah.at[pl.ds(ROWS, ROWS), pl.ds(384 * t, 384)], r_d.at[4, t])
    wait(fdt.at[1], r_g.at[0, 0])

    def grad_chunk(low):
        cols = pl.ds(pl.multiple_of(low, 256), 256)
        return dot(fdt[0], ah[pl.ds(0, ROWS), cols]) + dot(fdt[1], ah[pl.ds(ROWS, ROWS), cols])

    def by_x(total, xx):
        return jnp.concatenate(
            [total[24 * (4 * zz + xx) : 24 * (4 * zz + xx) + 24] for zz in range(NZ)], axis=0
        ).astype(BF)

    def beta_step(i):
        total = grad_chunk(512 * i + 256)
        for xx in range(NX):
            gb[xx, i] = by_x(total, xx)

    loop(NY, beta_step)
    for i in range(1, NX):
        send(gb.at[xp(i)], gbr.at[i], s_g.at[1, i], r_g.at[1, i], **to_x(i))

    def alpha_step(i):
        yy = lax.rem(y + i + 1, NY)
        total = grad_chunk(512 * yy)
        for xx in range(NX):
            ga[yy, xx] = by_x(total, xx)

    for i in range(NY):
        alpha_step(i)
        if i < NY - 1:
            send(ga.at[yp(i + 1)], gar.at[i + 1], s_g.at[2, i + 1], r_g.at[2, i + 1], dp=2 * yp(i + 1) + k)

    def back_step(i):
        cols = 256 * i
        total = dot(fdc[0], wf[:, cols : cols + 256])
        for t in range(1, SPAN):
            total = total + dot(fdc[t], wf[:, WIDTH * t + cols : WIDTH * t + cols + 256])
        fdp[0:EXT, cols : cols + 256] = total

    for i in range(3):
        back_step(i)

    fhl[0, EXT:WIDE, :] = jnp.zeros((WIDE - EXT, WIDTH), BF)
    fhl[1, EXT:WIDE, :] = jnp.zeros((WIDE - EXT, WIDTH), BF)

    def delta_step(i):
        r0 = pl.multiple_of(i * 16, 16)
        row = pd_ref[pl.ds((r0 + 112) // 128 + 1, 1), :]
        normed = nm_ref[pl.ds(r0, 16), :]
        w = fdp[pl.ds(r0, 16), :] * gn_ref[pl.ds(r0, 16), :]
        factor = fac_ref[pl.ds(r0, 16), :][:, :1]
        value = row + factor * (w - normed * jnp.mean(w * normed, axis=1, keepdims=True))
        value = jnp.where(jnp.logical_and(r0 >= OFF, r0 < OFF + ROWS), value, 0.0)
        fdl[pl.ds(r0, 16), :] = value
        high = value.astype(BF)
        fhl[0, pl.ds(r0, 16), :] = high
        fhl[1, pl.ds(r0, 16), :] = (value - high.astype(F32)).astype(BF)

    loop(EXT // 16, delta_step, unroll=2)
    out_copy = pltpu.make_async_copy(fdl.at[pl.ds(OFF, ROWS)], o_fd, s_o.at[5])
    out_copy.start()
    ep[...] = (dot(e_ref[...], fhl[0]) + dot(e_ref[...], fhl[1])).reshape(NZ, 8, WIDTH)
    for i in range(1, NZ):
        send(ep.at[zp(i)], er.at[i], s_e.at[0, i], r_e.at[0, i], **to_z(i))

    def sum_pieces(count, step_rows, own, got, put):
        def body(i):
            rows = pl.ds(pl.multiple_of(i * step_rows, 16), step_rows)
            total = own(rows).astype(F32)
            for j in range(1, 4):
                total = total + got(j, rows).astype(F32)
            put(rows, total)

        loop(count, body)

    for i in range(1, NY):
        wait(gar.at[i], r_g.at[2, i])
    for xx in range(NX):
        def put_a(rows, total, xx=xx):
            ha[xx, rows, :] = total.astype(BF)

        sum_pieces(4, 48, lambda rows, xx=xx: ga[y, xx, rows, :], lambda j, rows, xx=xx: gar[j, xx, rows, :], put_a)
    for i in range(1, NX):
        send(ha.at[xp(i)], har.at[i], s_g.at[3, i], r_g.at[3, i], **to_x(i))
    for i in range(1, NX):
        wait(gbr.at[i], r_g.at[1, i])
    for yy in range(NY):
        def put_b(rows, total, yy=yy):
            hb[yy, rows, :] = total.astype(BF)

        sum_pieces(4, 48, lambda rows, yy=yy: gb[x, yy, rows, :], lambda j, rows, yy=yy: gbr[j, yy, rows, :], put_b)
    for i in range(1, NY):
        send(hb.at[yp(i)], hbr.at[i], s_g.at[4, i], r_g.at[4, i], dp=2 * yp(i) + k)

    total = ep[z]
    for i in range(1, NZ):
        wait(er.at[i], r_e.at[0, i])
    for i in range(1, NZ):
        total = total + er[i]
    ex[x] = total
    for i in range(1, NX):
        send(ex.at[x], ex.at[x], s_e.at[1, i], r_e.at[1, i], **to_x(i))

    for i in range(1, ND):
        wait(dp_slot(dax, dpp(-i), 128), r_d.at[0, i])
        wait(fdx.at[dpp(-i)], r_d.at[3, i])
    for i in range(ND):
        fkx[:, 128 * i : 128 * i + 128] = shifted(fdx[i])
    deep_total = dot(fkx[...], dax[...])
    for t in range(SPAN):
        o_gd[:, WIDTH * t : WIDTH * (t + 1)] = deep_total[48 * t : 48 * t + 48]

    for i in range(1, NX):
        wait(ex.at[xp(-i)], r_e.at[1, i])
    ey[d] = (ex[0] + ex[1]) + (ex[2] + ex[3])
    for i in range(1, ND):
        send(ey.at[d], ey.at[d], s_e.at[2, i], r_e.at[2, i], dp=dpp(i))

    for i in range(1, NX):
        wait(har.at[i], r_g.at[3, i])
    for i in range(1, NY):
        wait(hbr.at[i], r_g.at[4, i])

    def third_step(i):
        rows = pl.ds(pl.multiple_of(i * 48, 16), 48)
        left_half = ha[x, rows, :].astype(F32)
        right_half = hb[y, rows, :].astype(F32)
        for j in range(1, 4):
            left_half = left_half + har[j, rows, :].astype(F32)
            right_half = right_half + hbr[j, rows, :].astype(F32)
        zs[2 * i] = jnp.concatenate([left_half[:24], right_half[:24]], axis=0).astype(BF)
        zs[2 * i + 1] = jnp.concatenate([left_half[24:], right_half[24:]], axis=0).astype(BF)

    loop(4, third_step)
    for i in range(1, NZ):
        send(zs.at[zp(i)], zr.at[i], s_g.at[5, i], r_g.at[5, i], **to_z(i))

    total = ey[d]
    for i in range(1, ND):
        wait(ey.at[dpp(-i)], r_e.at[2, i])
    total = ey[0]
    for i in range(1, ND):
        total = total + ey[i]
    eg[z] = total
    for i in range(1, NZ):
        send(eg.at[z], eg.at[z], s_e.at[3, i], r_e.at[3, i], **to_z(i))

    total = zs[z].astype(F32)
    for i in range(1, NZ):
        wait(zr.at[i], r_g.at[5, i])
    for i in range(1, NZ):
        total = total + zr[i].astype(F32)
    fin[d] = total
    for i in range(1, ND):
        send(fin.at[d], fin.at[d], s_g.at[6, i], r_g.at[6, i], dp=dpp(i))
    for i in range(1, NZ):
        wait(eg.at[zp(-i)], r_e.at[3, i])
    o_ge[...] = eg[...].reshape(64, WIDTH)
    for i in range(1, ND):
        wait(fin.at[dpp(-i)], r_g.at[6, i])
    for i in range(ND):
        for t in range(4):
            tile = 4 * (i // 2) + t
            if tile >= 15:
                continue
            column = 128 * (6 * (tile // 3) + 3 * (i % 2) + tile % 3)
            part = fin[i, 24 * (t // 2) : 24 * (t // 2) + 24, 128 * (t % 2) : 128 * (t % 2) + 128]
            o_gc[:, column : column + 128] = part

    out_copy.wait()
    for copy in sends:
        copy.wait_send()


def shards(bases, organism, embed_weight, conv_weight, deep_weight, human_head, mouse_head, human_cotangent, mouse_cotangent):
    gap = jnp.zeros((1536, 8), BF)
    hm = jnp.concatenate([human_head, gap, mouse_head, jnp.zeros((1536, 32), BF)], axis=1)
    is_human = (organism == 0).astype(BF)[:, None, None]
    cots = jnp.concatenate(
        [
            human_cotangent * is_human,
            jnp.zeros((1, 128, 8), BF),
            mouse_cotangent * (1 - is_human),
            jnp.zeros((1, 128, 32), BF),
        ],
        axis=2,
    )
    cot = cots[0].T
    vmem, dma = pltpu.VMEM, pltpu.SemaphoreType.DMA
    scratch = [
        vmem((1, 128), jnp.int32), vmem((1, 128), jnp.int32),
        vmem((64, WIDE), BF), vmem((WIDE, 64), BF), vmem((64, WIDTH), BF),
        vmem((WIDE + 8, WIDTH), F32), vmem((WIDE, WIDTH), BF), vmem((WIDE, WIDTH), F32),
        vmem((WIDE, WIDTH), F32), vmem((WIDE, 128), F32), vmem((SPAN, EXT, WIDTH), BF),
        vmem((NZ, NX, 24, 3840), BF), vmem((WIDTH, 3840), BF), vmem((EXT, WIDTH), F32),
        vmem((2 * ROWS, 2048), BF),
        vmem((NZ, NX, 8, 384), F32), vmem((144, WIDTH), F32), vmem((144, WIDTH), F32), vmem((144, 128), F32),
        vmem((SPAN, 128, WIDTH), BF), vmem((NZ, NX, 48, 128), BF),
        vmem((ND, 256, 128), BF), vmem((ND, 4, 48, 128), BF),
        vmem((NZ, NX, 48, 128), BF), vmem((4, NZ, 48, 128), BF), vmem((NZ, 48, 128), BF), vmem((NZ, 48, 128), BF),
        vmem((ND, 48, 128), BF), vmem((240, 1024), BF), vmem((240, WIDTH), BF), vmem((144, WIDTH), F32),
        vmem((NZ, NX, 16, 384), BF), vmem((4, NZ, 16, 384), BF), vmem((NZ, 16, 384), BF), vmem((NZ, 16, 384), BF),
        vmem((1024, WIDTH), BF), vmem((8, WIDTH), F32),
        vmem((EXT + 16, WIDTH), F32), vmem((SPAN, EXT, WIDTH), BF), vmem((2, WIDTH, ROWS), BF),
        vmem((NY, NX, 192, 256), BF), vmem((NX, NY, 192, 256), BF),
        vmem((4, NX, 192, 256), BF), vmem((4, NY, 192, 256), BF),
        vmem((NX, 192, 256), BF), vmem((NY, 192, 256), BF), vmem((4, 192, 256), BF), vmem((4, 192, 256), BF),
        vmem((NZ, 48, 256), BF), vmem((NZ, 48, 256), BF), vmem((ND, 48, 256), F32),
        vmem((EXT, WIDTH), F32), vmem((2, WIDE, WIDTH), BF),
        vmem((NZ, 8, WIDTH), F32), vmem((NZ, 8, WIDTH), F32), vmem((NX, 8, WIDTH), F32),
        vmem((ND, 8, WIDTH), F32), vmem((NZ, 8, WIDTH), F32),
        dma((2,)), dma((2,)), dma((12, 8)), dma((12, 8)), dma((11,)), dma((11,)), dma((11,)), dma((11,)),
        dma((11,)), dma((11,)), dma((11,)), dma((11,)), dma((5, 8)), dma((5, 8)), dma((7, 8)), dma((7, 8)),
        dma((4, 8)), dma((4, 8)), dma((6,)),
    ]
    spec = pl.BlockSpec(memory_space=pltpu.VMEM)
    ge, gc, gd, gh, gm, fd = pl.pallas_call(
        kernel,
        out_shape=(
            jax.ShapeDtypeStruct((64, WIDTH), F32),
            jax.ShapeDtypeStruct((24, 3840), F32),
            jax.ShapeDtypeStruct((48, 3840), F32),
            jax.ShapeDtypeStruct((192, 184), F32),
            jax.ShapeDtypeStruct((192, 32), F32),
            jax.ShapeDtypeStruct((ROWS, WIDTH), F32),
        ),
        in_specs=[spec] * 6,
        out_specs=(spec, spec, spec, spec, spec, pl.BlockSpec(memory_space=pl.ANY)),
        scratch_shapes=scratch,
        compiler_params=pltpu.CompilerParams(
            collective_id=0, has_side_effects=True, vmem_limit_bytes=60 * 1024 * 1024
        ),
        cost_estimate=pl.CostEstimate(flops=10_000_000_000, bytes_accessed=8_000_000, transcendentals=2_000_000),
    )(bases, embed_weight, conv_weight, deep_weight, hm, cot)
    grad_embed = ge.reshape(4, 16, WIDTH)[:, :0:-1].transpose(1, 0, 2).reshape(60, WIDTH)
    return grad_embed, gc, gd, gh, gm, fd[None]


def solution(mesh):
    return jax.shard_map(
        shards,
        mesh=mesh,
        in_specs=(
            P("dp", "context"),
            P("dp"),
            P(),
            P("context", None),
            P("context", None),
            P(None, "context"),
            P(None, "context"),
            P("dp", None, "context"),
            P("dp", None, "context"),
        ),
        out_specs=(
            P(),
            P("context", None),
            P("context", None),
            P("dp", "context"),
            P("dp", "context"),
            P("dp", "context", None),
        ),
        check_vma=False,
    )
```

```python
import jax
import jax.numpy as jnp
from jax import lax
from jax.experimental import pallas as pl
from jax.experimental.pallas import tpu as pltpu
from jax.sharding import PartitionSpec as P

F32 = jnp.float32
BF = jnp.bfloat16
MESH = pl.DeviceIdType.MESH

WIDTH = 768
SPAN = 5
NZ, NX, NY = 8, 4, 4
ND = 8
ROWS = 512
OFF = 16
EXT = ROWS + 2 * OFF
WIDE = 640
HALF = 1920
SPLIT = 1024

SLOPE = 0.7978845608028654
CUBIC = 0.044715
EPSILON = 1e-06


def gelu_both(value):
    square = value * value
    tangent = jnp.tanh(SLOPE * (value + CUBIC * square * value))
    half = 0.5 * (1.0 + tangent)
    slope = half + 0.5 * value * (1.0 - tangent * tangent) * SLOPE * (1.0 + 3.0 * CUBIC * square)
    return value * half, slope


def gelu_value(value):
    return 0.5 * value * (1.0 + jnp.tanh(SLOPE * (value + CUBIC * value * value * value)))


def gelu_slope(value):
    return gelu_both(value)[1]


def dot(a, b, ca=1, cb=0):
    return lax.dot_general(a, b, (((ca,), (cb,)), ((), ())), preferred_element_type=F32)


def loop(count, body, unroll=1):
    def step(i, carry):
        body(i)
        return carry

    lax.fori_loop(0, count, step, 0, unroll=unroll)


def kernel(
    i_bases, organism, i_embed, i_cw, i_dw, i_head_h, i_head_m, i_cot_h, i_cot_m,
    q_ge, q_gc, q_gd, q_gh, q_gm, o_fd,
    bases, embed, dw, head_h, head_m, cot_h, cot_m, o_ge, o_gc, o_gd, o_gh, o_gm,
    hm, hmt, cot, hl, hr, e_ref, et_ref, embp, fpad, first, nm_ref, gn_ref, fac_ref, acols, wg, wf, mixed, ah,
    pbuf, dn_ref, dpad, df_ref, dcols, ft, dtx, fxs, fbs, fxr, fzs, fzr, fdx, fkx, dw2, dbp, dbs, dxr, dzs, dzr,
    dax, pd_ref, fdp, fdc, fdt,
    ga, gb, gar, gbr, ha, hb, har, hbr, zs, zr, fin,
    fdl, fhl, ep, er, ex, ey, eg,
    s_h, r_h, s_w, r_w, s_p, r_p, s_f, r_f, s_rf, r_rf, s_rd, r_rd, s_d, r_d, s_g, r_g, s_e, r_e, s_o, s_i,
):
    c = lax.axis_index("context")
    d = lax.axis_index("dp")
    z, x = c // NX, c % NX
    y, k = d // 2, d % 2
    sends = []

    def zp(i):
        return lax.rem(z + i + NZ, NZ)

    def xp(i):
        return lax.rem(x + i + NX, NX)

    def dpp(i):
        return lax.rem(d + i + ND, ND)

    def yp(i):
        return lax.rem(y + i + NY, NY)

    def send(src, dst, ss, rs, **to):
        copy = pltpu.make_async_remote_copy(
            src_ref=src, dst_ref=dst, send_sem=ss, recv_sem=rs, device_id=to, device_id_type=MESH
        )
        copy.start()
        sends.append(copy)

    def wait(dst, rs):
        pltpu.make_async_remote_copy(
            src_ref=dst, dst_ref=dst, send_sem=rs, recv_sem=rs, device_id={"context": zp(1) * NX + x}, device_id_type=MESH
        ).wait_recv()

    barrier = pltpu.get_barrier_semaphore()
    for i in range(1, NZ):
        pl.semaphore_signal(barrier, inc=1, device_id={"context": zp(i) * NX + x}, device_id_type=MESH)
    for i in range(1, NX):
        pl.semaphore_signal(barrier, inc=1, device_id={"context": z * NX + xp(i)}, device_id_type=MESH)
    for i in range(1, ND):
        pl.semaphore_signal(barrier, inc=1, device_id={"dp": dpp(i)}, device_id_type=MESH)
    right, left = lax.rem(c + 1, NZ * NX), lax.rem(c + NZ * NX - 1, NZ * NX)
    pl.semaphore_signal(barrier, inc=1, device_id={"context": right}, device_id_type=MESH)
    pl.semaphore_signal(barrier, inc=1, device_id={"context": left}, device_id_type=MESH)
    loads = []
    for i, (src, dst) in enumerate(
        (
            (i_cw, wg.at[z, x]), (i_bases, bases), (i_embed, embed), (i_head_h, head_h),
            (i_head_m, head_m), (i_cot_h, cot_h), (i_cot_m, cot_m), (i_dw, dw),
        )
    ):
        load = pltpu.make_async_copy(src, dst, s_i.at[i])
        load.start()
        loads.append(load)
    stores = []

    def store(src, dst):
        out = pltpu.make_async_copy(src, dst, s_i.at[8 + len(stores)])
        out.start()
        stores.append(out)

    loads[0].wait()
    loads[1].wait()
    pl.semaphore_wait(barrier, NZ - 1 + NX - 1 + ND - 1 + 2)

    mine = pl.multiple_of(HALF * k, 128)
    other = pl.multiple_of(HALF * (1 - k), 128)
    c0 = pl.ds(mine, SPLIT)
    c1 = pl.ds(pl.multiple_of(mine + SPLIT, 128), HALF - SPLIT)
    o0 = pl.ds(other, SPLIT)
    o1 = pl.ds(pl.multiple_of(other + SPLIT, 128), HALF - SPLIT)
    sib = 2 * y + 1 - k

    def blk1(q):
        return wg.at[zp(-q), x, :, c1]

    def to_z(i):
        return dict(context=zp(i) * NX + x)

    def to_x(i):
        return dict(context=z * NX + xp(i))

    send(bases.at[:, pl.ds(ROWS - 128, 128)], hl, s_h.at[0], r_h.at[0], context=right)
    send(bases.at[:, pl.ds(0, 128)], hr, s_h.at[1], r_h.at[1], context=left)
    for i in range(1, NX):
        send(wg.at[z, x, :, c0], wg.at[z, x, :, c0], s_w.at[0, i], r_w.at[0, i], **to_x(i))
    send(blk1(0), blk1(0), s_w.at[1, 1], r_w.at[1, 1], **to_z(1))
    send(blk1(0), blk1(0), s_w.at[2, 1], r_w.at[2, 1], **to_z(-1))
    for i in range(1, NX):
        send(blk1(0), blk1(0), s_w.at[4 + i, 0], r_w.at[4 + i, 0], **to_x(i))

    rows60 = lax.broadcasted_iota(jnp.int32, (64, 60), 0)
    cols60 = lax.broadcasted_iota(jnp.int32, (64, 60), 1)
    place = jnp.where(cols60 == 4 * (15 - rows60 % 16) + rows60 // 16, 1.0, 0.0).astype(BF)
    loads[2].wait()
    embp[...] = dot(place, embed[...]).astype(BF)
    wait(hl, r_h.at[0])
    wait(hr, r_h.at[1])
    before = jnp.where(c == 0, -1, hl[...])
    after = jnp.where(c == NZ * NX - 1, -1, hr[...])
    line = jnp.concatenate([before, bases[...], after], axis=1)
    rolled = pltpu.roll(jnp.broadcast_to(line, (16, ROWS + 256)), 648, 1, stride=1, stride_axis=0)
    for j in range(4):
        e_ref[16 * j : 16 * j + 16, :] = jnp.where(rolled[:, :WIDE] == j, 1.0, 0.0).astype(BF)
    for i in range(WIDE // 128):
        block = e_ref[:, 128 * i : 128 * i + 128].astype(F32)
        et_ref[128 * i : 128 * i + 128, :] = block.T.astype(BF)
    fpad[0:8, :] = jnp.zeros((8, WIDTH), F32)
    fpad[EXT + 8 : EXT + 16, :] = jnp.zeros((8, WIDTH), F32)

    def embed_step(i):
        r0 = pl.multiple_of(i * 32, 32)
        values = dot(et_ref[pl.ds(r0, 32), :], embp[...]).astype(BF)
        first[pl.ds(r0, 32), :] = values
        values = values.astype(F32)
        factor = lax.rsqrt(jnp.mean(values * values, axis=1, keepdims=True) + EPSILON)
        normed = values * factor
        value, slope = gelu_both(normed)
        spot = lax.broadcasted_iota(jnp.int32, (32, WIDTH), 0) + (c * ROWS + r0 - OFF)
        inside = jnp.logical_and(spot >= 0, spot < ROWS * NZ * NX)
        value = jnp.where(inside, value, 0.0)
        fpad[pl.ds(r0 + 8, 32), :] = value.astype(BF).astype(F32)
        nm_ref[pl.ds(r0, 32), :] = normed
        gn_ref[pl.ds(r0, 32), :] = slope
        fac_ref[pl.ds(r0, 32), :] = jnp.broadcast_to(factor, (32, 128))

    def head_rows():
        for load in loads[3:]:
            load.wait()
        hmt[0:176, :] = head_h[0:176, :]
        last = jnp.concatenate([head_h[176:184, :].astype(F32), jnp.zeros((8, 1536), F32)], axis=0)
        hmt[176:192, :] = last.astype(BF)
        hmt[192:224, :] = head_m[...]
        hmt[224:256, :] = jnp.zeros((32, 1536), BF)
        human = (organism[0] == 0).astype(F32)
        cot[0:184, :] = cot_h[...].astype(F32) * human
        cot[184:192, :] = jnp.zeros((8, 128), F32)
        cot[192:224, :] = cot_m[...].astype(F32) * (1.0 - human)
        cot[224:256, :] = jnp.zeros((32, 128), F32)

    def head_turn(i):
        cols = pl.ds(pl.multiple_of(128 * i, 128), 128)
        hm[cols, :] = hmt[:, cols].astype(F32).T.astype(BF)

    def ring1_up(s):
        wait(blk1(s), r_w.at[1, s])
        if s < 4:
            send(blk1(s), blk1(s), s_w.at[1, s + 1], r_w.at[1, s + 1], **to_z(1))
        spread1(s)

    def ring1_down(s):
        q = NZ - s
        wait(blk1(q), r_w.at[2, s])
        if s < 3:
            send(blk1(q), blk1(q), s_w.at[2, s + 1], r_w.at[2, s + 1], **to_z(-1))
        spread1(q)

    def spread1(q):
        for i in range(1, NX):
            send(blk1(q), blk1(q), s_w.at[4 + i, q], r_w.at[4 + i, q], **to_x(i))
        send(blk1(q), blk1(q), s_w.at[8, q], r_w.at[8, q], dp=sib)

    def blk0(q, cols):
        return wg.at[zp(-q), :, :, cols]

    def chunk(low, h):
        return pl.ds(pl.multiple_of(low + 256 * h, 128), 256)

    def ring0(s, h):
        for down in range(2):
            if s == 4 and down:
                continue
            q, row = (NZ - s if down else s), 12 + 4 * down + h
            part = blk0(q, chunk(mine, h))
            wait(part, r_w.at[row, s])
            if s < 4 - down:
                send(part, part, s_w.at[row, s + 1], r_w.at[row, s + 1], **to_z(-1 if down else 1))
            send(part, part, s_w.at[20 + h, q], r_w.at[20 + h, q], dp=sib)

    def embed_some(low, high):
        def body(i):
            embed_step(i + low)

        loop(high - low, body)

    def shift_step(i):
        r0 = pl.multiple_of(i * 32, 32)
        block = fpad[pl.ds(r0, 48), :]
        for t in range(SPAN):
            acols[t, pl.ds(r0, 32), :] = block[t + 6 : t + 38].astype(BF)

    ring1_up(1)
    ring1_down(1)
    for i in range(1, NX):
        here = wg.at[z, xp(-i), :, c0]
        wait(here, r_w.at[0, i])
        send(here, here, s_w.at[9, i], r_w.at[9, i], dp=sib)
    for h in range(4):
        part = blk0(0, chunk(mine, h))
        send(part, part, s_w.at[12 + h, 1], r_w.at[12 + h, 1], **to_z(1))
        send(part, part, s_w.at[16 + h, 1], r_w.at[16 + h, 1], **to_z(-1))
    embed_some(0, 4)
    ring1_up(2)
    ring1_down(2)
    embed_step(4)
    for s in range(1, 4):
        for h in range(4):
            ring0(s, h)
            embed_step(1 + 4 * s + h)
            if s == 1 and h == 1:
                ring1_up(3)
                ring1_down(3)
            if s == 2 and h == 1:
                ring1_up(4)
    head_rows()
    for h in range(4):
        ring0(4, h)
        if h == 0:
            loop(EXT // 32, shift_step)
        if h == 1:
            loop(12, head_turn)
    for i in range(1, NX):
        for q in range(NZ):
            here = wg.at[zp(-q), xp(-i), :, c1]
            wait(here, r_w.at[4 + i, q])
        here = wg.at[:, xp(-i), :, c1]
        send(here, here, s_w.at[11, i], r_w.at[11, i], dp=sib)
    for q in range(1, NZ):
        wait(wg.at[zp(-q), x, :, o1], r_w.at[8, q])
        for h in range(4):
            wait(blk0(q, chunk(other, h)), r_w.at[20 + h, q])
    for i in range(1, NX):
        wait(wg.at[z, xp(-i), :, o0], r_w.at[9, i])
        wait(wg.at[:, xp(-i), :, o1], r_w.at[11, i])

    def pack_step(i):
        zz, half = i // 2, 2 * (i % 2)
        pair = jnp.concatenate([wg[zz, half].astype(F32), wg[zz, half + 1].astype(F32)], axis=0)
        wf[pl.ds(pl.multiple_of(48 * i, 16), 48), :] = pair.astype(BF)

    loop(16, pack_step)

    own_cols = pl.ds(pl.multiple_of((WIDTH // 2) * k, 128), WIDTH // 2)
    sib_cols = pl.ds(pl.multiple_of((WIDTH // 2) * (1 - k), 128), WIDTH // 2)
    local = []
    for t in range(SPAN):
        dst = ah.at[pl.ds(0, ROWS), pl.ds(384 * t, 384)]
        copy = pltpu.make_async_copy(acols.at[t, pl.ds(OFF, ROWS), own_cols], dst, s_o.at[t])
        copy.start()
        local.append(copy)
        send(
            acols.at[t, pl.ds(OFF, ROWS), sib_cols], ah.at[pl.ds(ROWS, ROWS), pl.ds(384 * t, 384)],
            s_d.at[4, t], r_d.at[4, t], dp=sib,
        )
    ah[:, pl.ds(HALF, 128)] = jnp.zeros((2 * ROWS, 128), BF)
    def conv_step(i):
        o0_ = pl.multiple_of(i * 256, 256)
        total = dot(acols[0], wf[pl.ds(o0_, 256), 0:WIDTH], 1, 1)
        for t in range(1, SPAN):
            total = total + dot(acols[t], wf[pl.ds(o0_, 256), WIDTH * t : WIDTH * (t + 1)], 1, 1)
        mixed[:, pl.ds(o0_, 256)] = total

    loop(3, conv_step)

    pooled = []
    for t in range(4):
        def pool_step(i, total):
            r0 = pl.multiple_of(OFF + 128 * t + 32 * i, 16)
            part = first[pl.ds(r0, 32), :].astype(F32) + gelu_value(mixed[pl.ds(r0, 32), :])
            return total + part.reshape(4, 8, WIDTH).sum(axis=0)

        total = lax.fori_loop(0, 4, pool_step, jnp.zeros((8, WIDTH), F32))
        row = jnp.sum(total, axis=0, keepdims=True) / 128.0
        pooled.append(row)

    pieces = [row[:, 256 * m : 256 * m + 256] for m in range(3) for row in pooled]
    pbuf[z, x] = jnp.concatenate(pieces + [jnp.zeros((4, 256), F32)], axis=0).astype(BF)
    near = (1, 7, 2, 6, 3, 5, 4)
    far = (4, 3, 5, 2, 6, 1, 7, 0)

    def relay_gather(buf, ss, rs, between=None):
        own = buf.at[z, x]
        for q in near:
            send(own, own, ss.at[0, q], rs.at[0, q], **to_z(q))
        for i in range(1, NX):
            send(own, own, ss.at[i, 0], rs.at[i, 0], **to_x(i))
        if between is not None:
            between()
        for q in near:
            here = buf.at[zp(-q), x]
            wait(here, rs.at[0, q])
            for i in range(1, NX):
                send(here, here, ss.at[i, q], rs.at[i, q], **to_x(i))

    def relay_finish(buf, rs):
        for q in (0,) + near:
            for i in range(1, NX):
                wait(buf.at[zp(-q), xp(-i)], rs.at[i, q])

    def scatter_start(src, got, ss, rs):
        for q in far:
            for i in range(1, NX):
                send(src.at[zp(q), xp(i)], got.at[i, q], ss.at[i, q], rs.at[i, q], **to_x(i))

    def scatter_turn(src, got, zsrc, zgot, ss, rs):
        for q in far:
            total = src[zp(q), x].astype(F32)
            for i in range(1, NX):
                wait(got.at[i, q], rs.at[i, q])
                total = total + got[i, q].astype(F32)
            if q:
                zsrc[q] = total.astype(BF)
                send(zsrc.at[q], zgot.at[q], ss.at[0, q], rs.at[0, q], **to_z(q))
        return total

    def scatter_finish(total, zgot, rs):
        for q in near:
            wait(zgot.at[q], rs.at[0, q])
            total = total + zgot[q].astype(F32)
        return total

    relay_gather(pbuf, s_p, r_p)

    def slope_step(i):
        r0 = pl.multiple_of(i * 32, 32)
        mixed[pl.ds(r0, 32), :] = gelu_slope(mixed[pl.ds(r0, 32), :])

    loop(EXT // 32, slope_step)
    for t in range(SPAN):
        dw2[48 * t : 48 * t + 48, :] = dw[:, WIDTH * t : WIDTH * (t + 1)]
    zero8 = jnp.zeros((8, WIDTH), F32)
    dn_ref[0:8, :] = zero8
    dn_ref[136:144, :] = zero8
    dpad[0:8, :] = zero8
    dpad[136:144, :] = zero8
    dbp[0:8, :] = zero8
    dbp[136:144, :] = zero8
    df_ref[...] = jnp.ones((144, 128), F32)
    relay_finish(pbuf, r_p)

    def coarse_step(i):
        zz, half = i // 2, 2 * (i % 2)
        v0, v1 = pbuf[zz, half].astype(F32), pbuf[zz, half + 1].astype(F32)
        parts = [jnp.concatenate([v0[4 * m : 4 * m + 4], v1[4 * m : 4 * m + 4]], axis=0) for m in range(3)]
        values = jnp.concatenate(parts, axis=1)
        factor = lax.rsqrt(jnp.mean(values * values, axis=1, keepdims=True) + EPSILON)
        normed = values * factor
        r0 = pl.multiple_of(8 * i + 8, 8)
        dn_ref[pl.ds(r0, 8), :] = normed
        df_ref[pl.ds(r0, 8), :] = jnp.broadcast_to(factor, (8, 128))
        dpad[pl.ds(r0, 8), :] = gelu_value(normed).astype(BF).astype(F32)

    loop(16, coarse_step)
    block = dpad[...]
    for t in range(SPAN):
        dcols[t] = block[t + 6 : t + 134].astype(BF)
    total = dot(dw[:, 0:WIDTH], dcols[0], 1, 1)
    for t in range(1, SPAN):
        total = total + dot(dw[:, WIDTH * t : WIDTH * (t + 1)], dcols[t], 1, 1)
    ft[z, x] = total.astype(BF)
    dax[pl.ds(pl.multiple_of(d * 128, 128), 128), :] = dcols[2]

    def dp_slot(ref, i, size):
        return ref.at[pl.ds(pl.multiple_of(i * size, 16), size)]

    def coarse_background():
        for i in range(1, ND):
            send(dcols.at[2], dp_slot(dax, d, 128), s_d.at[0, i], r_d.at[0, i], dp=dpp(i))

    relay_gather(ft, s_f, r_f, coarse_background)
    relay_finish(ft, r_f)

    feats = ft[...].reshape(1536, 128)
    logit = dot(hmt[...], feats)
    delta = (cot[...] * jax.nn.sigmoid(logit)).astype(BF)
    dtx[d] = delta
    fbs[...] = dot(hm[...], delta).astype(BF).reshape(NZ, NX, 48, 128)
    scatter_start(fbs, fxr, s_rf, r_rf)
    for i in range(1, ND):
        send(dtx.at[d], dtx.at[d], s_d.at[1, i], r_d.at[1, i], dp=dpp(i))
        send(ft.at[dpp(i)], fxs.at[d], s_d.at[2, i], r_d.at[2, i], dp=dpp(i))
    fxs[d] = ft[d]

    own_part = scatter_turn(fbs, fxr, fzs, fzr, s_rf, r_rf)
    fdelta = scatter_finish(own_part, fzr, r_rf).astype(BF)
    fdx[d] = fdelta
    for i in range(1, ND):
        send(fdx.at[d], fdx.at[d], s_d.at[3, i], r_d.at[3, i], dp=dpp(i))

    lanes = lax.broadcasted_iota(jnp.int32, (48, 128), 1)

    def shifted(values):
        wide = values.astype(F32)
        parts = []
        for t in range(SPAN):
            move = t - 2
            if move == 0:
                parts.append(wide)
                continue
            turned = pltpu.roll(wide, move % 128, 1)
            keep = lanes >= move if move > 0 else lanes < 128 + move
            parts.append(jnp.where(keep, turned, 0.0))
        return jnp.concatenate(parts, axis=0).astype(BF)

    back = dot(shifted(fdelta), dw2[...], 0, 0)
    dbp[8:136, :] = back

    def piece_step(i):
        block = dbp[pl.ds(pl.multiple_of(8 * i, 8), 24), :]
        zz, half = i // 2, 2 * (i % 2)
        for j, low in ((0, 6), (1, 10)):
            rows = block[low : low + 8]
            dbs[zz, half + j] = jnp.concatenate([rows[:, :384], rows[:, 384:]], axis=0).astype(BF)

    loop(16, piece_step)
    scatter_start(dbs, dxr, s_rd, r_rd)
    own_part = scatter_turn(dbs, dxr, dzs, dzr, s_rd, r_rd)

    for i in range(1, ND):
        wait(dtx.at[dpp(-i)], r_d.at[1, i])
        wait(fxs.at[dpp(-i)], r_d.at[2, i])
    total = jnp.zeros((256, 192), F32)
    for i in range(ND):
        total = total + dot(dtx[i], fxs[i].reshape(192, 128), 1, 1)
    o_gh[...] = total[:184]
    o_gm[...] = total[192:224]
    store(o_gh, q_gh)
    store(o_gm, q_gm)

    deep_back = scatter_finish(own_part, dzr, r_rd)
    deep_back = jnp.concatenate([deep_back[:8], deep_back[8:]], axis=1)
    r0 = pl.multiple_of(8 * (c // 2), 8)

    def own_rows(ref):
        block = ref[pl.ds(r0, 24), :]
        return jnp.where(c % 2 == 0, block[6:14], block[10:18])

    dnormed = own_rows(dn_ref)
    dfactor = own_rows(df_ref)[:, :1]
    v = deep_back * gelu_slope(dnormed)
    pd_ref[...] = dfactor * (v - dnormed * jnp.mean(v * dnormed, axis=1, keepdims=True)) / 128.0

    fdp[0:8, :] = zero8
    fdp[EXT + 8 : EXT + 16, :] = zero8

    def fine_step(i):
        r0 = pl.multiple_of(i * 16, 16)
        row = pd_ref[pl.ds((r0 + 112) // 128 + 1, 1), :]
        fine = (mixed[pl.ds(r0, 16), :] * row).astype(BF).astype(F32)
        fdp[pl.ds(r0 + 8, 16), :] = fine

    loop(EXT // 16, fine_step, unroll=2)
    for i in range(4):
        block = fdp[OFF + 8 + 128 * i : OFF + 136 + 128 * i, :]
        fdt[0, :, 128 * i : 128 * i + 128] = block.T.astype(BF)
    send(fdt.at[0], fdt.at[1], s_g.at[0, 0], r_g.at[0, 0], dp=sib)

    def back_shift(i):
        r0 = pl.multiple_of(i * 32, 32)
        block = fdp[pl.ds(r0, 48), :]
        for t in range(SPAN):
            fdc[t, pl.ds(r0, 32), :] = block[10 - t : 42 - t].astype(BF)

    loop(EXT // 32, back_shift)
    for copy in local:
        copy.wait()
    for t in range(SPAN):
        wait(ah.at[pl.ds(ROWS, ROWS), pl.ds(384 * t, 384)], r_d.at[4, t])
    wait(fdt.at[1], r_g.at[0, 0])

    def grad_chunk(low):
        cols = pl.ds(pl.multiple_of(low, 256), 256)
        return dot(fdt[0], ah[pl.ds(0, ROWS), cols]) + dot(fdt[1], ah[pl.ds(ROWS, ROWS), cols])

    def by_x(total, xx):
        return jnp.concatenate(
            [total[24 * (4 * zz + xx) : 24 * (4 * zz + xx) + 24] for zz in range(NZ)], axis=0
        ).astype(BF)

    def beta_step(i):
        total = grad_chunk(512 * i + 256)
        for xx in range(NX):
            gb[xx, i] = by_x(total, xx)

    loop(NY, beta_step)
    for i in range(1, NX):
        send(gb.at[xp(i)], gbr.at[i], s_g.at[1, i], r_g.at[1, i], **to_x(i))

    def alpha_step(i):
        yy = lax.rem(y + i + 1, NY)
        total = grad_chunk(512 * yy)
        for xx in range(NX):
            ga[yy, xx] = by_x(total, xx)

    for i in range(NY):
        alpha_step(i)
        if i < NY - 1:
            send(ga.at[yp(i + 1)], gar.at[i + 1], s_g.at[2, i + 1], r_g.at[2, i + 1], dp=2 * yp(i + 1) + k)

    def back_step(i):
        cols = 256 * i
        total = dot(fdc[0], wf[:, cols : cols + 256])
        for t in range(1, SPAN):
            total = total + dot(fdc[t], wf[:, WIDTH * t + cols : WIDTH * t + cols + 256])
        fdp[0:EXT, cols : cols + 256] = total

    for i in range(3):
        back_step(i)

    fhl[0, EXT:WIDE, :] = jnp.zeros((WIDE - EXT, WIDTH), BF)
    fhl[1, EXT:WIDE, :] = jnp.zeros((WIDE - EXT, WIDTH), BF)

    def delta_step(i):
        r0 = pl.multiple_of(i * 16, 16)
        row = pd_ref[pl.ds((r0 + 112) // 128 + 1, 1), :]
        normed = nm_ref[pl.ds(r0, 16), :]
        w = fdp[pl.ds(r0, 16), :] * gn_ref[pl.ds(r0, 16), :]
        factor = fac_ref[pl.ds(r0, 16), :][:, :1]
        value = row + factor * (w - normed * jnp.mean(w * normed, axis=1, keepdims=True))
        value = jnp.where(jnp.logical_and(r0 >= OFF, r0 < OFF + ROWS), value, 0.0)
        fdl[pl.ds(r0, 16), :] = value
        high = value.astype(BF)
        fhl[0, pl.ds(r0, 16), :] = high
        fhl[1, pl.ds(r0, 16), :] = (value - high.astype(F32)).astype(BF)

    loop(EXT // 16, delta_step, unroll=2)
    out_copy = pltpu.make_async_copy(fdl.at[pl.ds(OFF, ROWS)], o_fd, s_o.at[5])
    out_copy.start()
    ep[...] = (dot(e_ref[...], fhl[0]) + dot(e_ref[...], fhl[1])).reshape(NZ, 8, WIDTH)
    for i in range(1, NZ):
        send(ep.at[zp(i)], er.at[i], s_e.at[0, i], r_e.at[0, i], **to_z(i))

    def sum_pieces(count, step_rows, own, got, put):
        def body(i):
            rows = pl.ds(pl.multiple_of(i * step_rows, 16), step_rows)
            total = own(rows).astype(F32)
            for j in range(1, 4):
                total = total + got(j, rows).astype(F32)
            put(rows, total)

        loop(count, body)

    for i in range(1, NY):
        wait(gar.at[i], r_g.at[2, i])
    for xx in range(NX):
        def put_a(rows, total, xx=xx):
            ha[xx, rows, :] = total.astype(BF)

        sum_pieces(4, 48, lambda rows, xx=xx: ga[y, xx, rows, :], lambda j, rows, xx=xx: gar[j, xx, rows, :], put_a)
    for i in range(1, NX):
        send(ha.at[xp(i)], har.at[i], s_g.at[3, i], r_g.at[3, i], **to_x(i))
    for i in range(1, NX):
        wait(gbr.at[i], r_g.at[1, i])
    for yy in range(NY):
        def put_b(rows, total, yy=yy):
            hb[yy, rows, :] = total.astype(BF)

        sum_pieces(4, 48, lambda rows, yy=yy: gb[x, yy, rows, :], lambda j, rows, yy=yy: gbr[j, yy, rows, :], put_b)
    for i in range(1, NY):
        send(hb.at[yp(i)], hbr.at[i], s_g.at[4, i], r_g.at[4, i], dp=2 * yp(i) + k)

    total = ep[z]
    for i in range(1, NZ):
        wait(er.at[i], r_e.at[0, i])
    for i in range(1, NZ):
        total = total + er[i]
    ex[x] = total
    for i in range(1, NX):
        send(ex.at[x], ex.at[x], s_e.at[1, i], r_e.at[1, i], **to_x(i))

    for i in range(1, ND):
        wait(dp_slot(dax, dpp(-i), 128), r_d.at[0, i])
        wait(fdx.at[dpp(-i)], r_d.at[3, i])
    for i in range(ND):
        fkx[:, 128 * i : 128 * i + 128] = shifted(fdx[i])
    deep_total = dot(fkx[...], dax[...])
    for t in range(SPAN):
        o_gd[:, WIDTH * t : WIDTH * (t + 1)] = deep_total[48 * t : 48 * t + 48]
    store(o_gd, q_gd)

    for i in range(1, NX):
        wait(ex.at[xp(-i)], r_e.at[1, i])
    ey[d] = (ex[0] + ex[1]) + (ex[2] + ex[3])
    for i in range(1, ND):
        send(ey.at[d], ey.at[d], s_e.at[2, i], r_e.at[2, i], dp=dpp(i))

    for i in range(1, NX):
        wait(har.at[i], r_g.at[3, i])
    for i in range(1, NY):
        wait(hbr.at[i], r_g.at[4, i])

    def third_step(i):
        rows = pl.ds(pl.multiple_of(i * 48, 16), 48)
        left_half = ha[x, rows, :].astype(F32)
        right_half = hb[y, rows, :].astype(F32)
        for j in range(1, 4):
            left_half = left_half + har[j, rows, :].astype(F32)
            right_half = right_half + hbr[j, rows, :].astype(F32)
        zs[2 * i] = jnp.concatenate([left_half[:24], right_half[:24]], axis=0).astype(BF)
        zs[2 * i + 1] = jnp.concatenate([left_half[24:], right_half[24:]], axis=0).astype(BF)

    loop(4, third_step)
    for i in range(1, NZ):
        send(zs.at[zp(i)], zr.at[i], s_g.at[5, i], r_g.at[5, i], **to_z(i))

    total = ey[d]
    for i in range(1, ND):
        wait(ey.at[dpp(-i)], r_e.at[2, i])
    total = ey[0]
    for i in range(1, ND):
        total = total + ey[i]
    eg[z] = total
    for i in range(1, NZ):
        send(eg.at[z], eg.at[z], s_e.at[3, i], r_e.at[3, i], **to_z(i))

    total = zs[z].astype(F32)
    for i in range(1, NZ):
        wait(zr.at[i], r_g.at[5, i])
    for i in range(1, NZ):
        total = total + zr[i].astype(F32)
    fin[d] = total.astype(BF)
    for i in range(1, ND):
        send(fin.at[d], fin.at[d], s_g.at[6, i], r_g.at[6, i], dp=dpp(i))
    for i in range(1, NZ):
        wait(eg.at[zp(-i)], r_e.at[3, i])
    for t in range(15):
        for j in range(4):
            o_ge[4 * t + j : 4 * t + j + 1, :] = eg[2 * j + (15 - t) // 8, (15 - t) % 8 : (15 - t) % 8 + 1, :]
    store(o_ge, q_ge)
    for i in range(1, ND):
        wait(fin.at[dpp(-i)], r_g.at[6, i])
    for i in range(ND):
        for t in range(4):
            tile = 4 * (i // 2) + t
            if tile >= 15:
                continue
            column = 128 * (6 * (tile // 3) + 3 * (i % 2) + tile % 3)
            part = fin[i, 24 * (t // 2) : 24 * (t // 2) + 24, 128 * (t % 2) : 128 * (t % 2) + 128]
            o_gc[:, column : column + 128] = part.astype(F32)
    store(o_gc, q_gc)

    out_copy.wait()
    for out in stores:
        out.wait()
    for copy in sends:
        copy.wait_send()


def shards(bases, organism, embed_weight, conv_weight, deep_weight, human_head, mouse_head, human_cotangent, mouse_cotangent):
    vmem, dma = pltpu.VMEM, pltpu.SemaphoreType.DMA
    scratch = [
        vmem((1, ROWS), jnp.int32), vmem((60, WIDTH), BF), vmem((48, 3840), BF), vmem((184, 1536), BF),
        vmem((32, 1536), BF), vmem((184, 128), BF), vmem((32, 128), BF),
        vmem((60, WIDTH), F32), vmem((24, 3840), F32), vmem((48, 3840), F32), vmem((184, 192), F32), vmem((32, 192), F32),
        vmem((1536, 256), BF), vmem((256, 1536), BF), vmem((256, 128), F32),
        vmem((1, 128), jnp.int32), vmem((1, 128), jnp.int32),
        vmem((64, WIDE), BF), vmem((WIDE, 64), BF), vmem((64, WIDTH), BF),
        vmem((EXT + 16, WIDTH), F32), vmem((EXT, WIDTH), BF), vmem((EXT, WIDTH), F32),
        vmem((EXT, WIDTH), F32), vmem((EXT, 128), F32), vmem((SPAN, EXT, WIDTH), BF),
        vmem((NZ, NX, 24, 3840), BF), vmem((WIDTH, 3840), BF), vmem((EXT, WIDTH), F32),
        vmem((2 * ROWS, 2048), BF),
        vmem((NZ, NX, 16, 256), BF), vmem((144, WIDTH), F32), vmem((144, WIDTH), F32), vmem((144, 128), F32),
        vmem((SPAN, 128, WIDTH), BF), vmem((NZ, NX, 48, 128), BF),
        vmem((ND, 256, 128), BF), vmem((ND, 4, 48, 128), BF),
        vmem((NZ, NX, 48, 128), BF), vmem((4, NZ, 48, 128), BF), vmem((NZ, 48, 128), BF), vmem((NZ, 48, 128), BF),
        vmem((ND, 48, 128), BF), vmem((240, 1024), BF), vmem((240, WIDTH), BF), vmem((144, WIDTH), F32),
        vmem((NZ, NX, 16, 384), BF), vmem((4, NZ, 16, 384), BF), vmem((NZ, 16, 384), BF), vmem((NZ, 16, 384), BF),
        vmem((1024, WIDTH), BF), vmem((8, WIDTH), F32),
        vmem((EXT + 16, WIDTH), F32), vmem((SPAN, EXT, WIDTH), BF), vmem((2, WIDTH, ROWS), BF),
        vmem((NY, NX, 192, 256), BF), vmem((NX, NY, 192, 256), BF),
        vmem((4, NX, 192, 256), BF), vmem((4, NY, 192, 256), BF),
        vmem((NX, 192, 256), BF), vmem((NY, 192, 256), BF), vmem((4, 192, 256), BF), vmem((4, 192, 256), BF),
        vmem((NZ, 48, 256), BF), vmem((NZ, 48, 256), BF), vmem((ND, 48, 256), BF),
        vmem((EXT, WIDTH), F32), vmem((2, WIDE, WIDTH), BF),
        vmem((NZ, 8, WIDTH), F32), vmem((NZ, 8, WIDTH), F32), vmem((NX, 8, WIDTH), F32),
        vmem((ND, 8, WIDTH), F32), vmem((NZ, 8, WIDTH), F32),
        dma((2,)), dma((2,)), dma((24, 8)), dma((24, 8)), dma((4, 8)), dma((4, 8)), dma((4, 8)), dma((4, 8)),
        dma((4, 8)), dma((4, 8)), dma((4, 8)), dma((4, 8)), dma((5, 8)), dma((5, 8)), dma((7, 8)), dma((7, 8)),
        dma((4, 8)), dma((4, 8)), dma((6,)), dma((13,)),
    ]
    spec = pl.BlockSpec(memory_space=pl.ANY)
    ge, gc, gd, gh, gm, fd = pl.pallas_call(
        kernel,
        out_shape=(
            jax.ShapeDtypeStruct((60, WIDTH), F32),
            jax.ShapeDtypeStruct((24, 3840), F32),
            jax.ShapeDtypeStruct((48, 3840), F32),
            jax.ShapeDtypeStruct((184, 192), F32),
            jax.ShapeDtypeStruct((32, 192), F32),
            jax.ShapeDtypeStruct((ROWS, WIDTH), F32),
        ),
        in_specs=[spec, pl.BlockSpec(memory_space=pltpu.SMEM)] + [spec] * 7,
        out_specs=(spec,) * 6,
        scratch_shapes=scratch,
        compiler_params=pltpu.CompilerParams(
            collective_id=0, has_side_effects=True, vmem_limit_bytes=60 * 1024 * 1024
        ),
        cost_estimate=pl.CostEstimate(flops=10_000_000_000, bytes_accessed=8_000_000, transcendentals=2_000_000),
    )(
        bases, organism, embed_weight, conv_weight, deep_weight,
        human_head.T, mouse_head.T, human_cotangent[0].T, mouse_cotangent[0].T,
    )
    return ge, gc, gd, gh.T, gm.T, fd[None]


def solution(mesh):
    return jax.shard_map(
        shards,
        mesh=mesh,
        in_specs=(
            P("dp", "context"),
            P("dp"),
            P(),
            P("context", None),
            P("context", None),
            P(None, "context"),
            P(None, "context"),
            P("dp", None, "context"),
            P("dp", None, "context"),
        ),
        out_specs=(
            P(),
            P("context", None),
            P("context", None),
            P("dp", "context"),
            P("dp", "context"),
            P("dp", "context", None),
        ),
        check_vma=False,
    )
```

```python
import jax
import jax.numpy as jnp
from jax import lax
from jax.experimental import pallas as pl
from jax.experimental.pallas import tpu as pltpu
from jax.sharding import PartitionSpec as P

F32 = jnp.float32
BF = jnp.bfloat16
MESH = pl.DeviceIdType.MESH

WIDTH = 768
SPAN = 5
NZ, NX, NY = 8, 4, 4
ND = 8
ROWS = 512
OFF = 16
EXT = ROWS + 2 * OFF
WIDE = 640
HALF = 1920
SPLIT = 1024

SLOPE = 0.7978845608028654
CUBIC = 0.044715
EPSILON = 1e-06


def gelu_both(value):
    square = value * value
    tangent = jnp.tanh(SLOPE * (value + CUBIC * square * value))
    half = 0.5 * (1.0 + tangent)
    slope = half + 0.5 * value * (1.0 - tangent * tangent) * SLOPE * (1.0 + 3.0 * CUBIC * square)
    return value * half, slope


def gelu_value(value):
    return 0.5 * value * (1.0 + jnp.tanh(SLOPE * (value + CUBIC * value * value * value)))


def gelu_slope(value):
    return gelu_both(value)[1]


def dot(a, b, ca=1, cb=0):
    return lax.dot_general(a, b, (((ca,), (cb,)), ((), ())), preferred_element_type=F32)


def loop(count, body, unroll=1):
    def step(i, carry):
        body(i)
        return carry

    lax.fori_loop(0, count, step, 0, unroll=unroll)


def kernel(
    i_bases, organism, i_embed, i_cw, i_dw, i_head_h, i_head_m, i_cot_h, i_cot_m,
    q_ge, q_gc, q_gd, q_gh, q_gm, o_fd,
    bases, embed, dw, head_h, head_m, cot_h, cot_m, o_ge, o_gc, o_gd, o_gh, o_gm,
    hm, hmt, cot, hl, hr, e_ref, et_ref, embp, fpad, first, nm_ref, gn_ref, fac_ref, acols, wg, wf, mixed, ah,
    pbuf, dn_ref, dpad, df_ref, dcols, ft, dtx, fxs, fbs, fxr, fzs, fzr, fdx, fkx, dw2, dbp, dbs, dxr, dzs, dzr,
    dax, pd_ref, fdp, fdc, fdt,
    ga, gb, gar, gbr, ha, hb, har, hbr, zs, zr, fin,
    fdl, fhl, ep, es, er, ex, ey, eg,
    s_all, r_h, r_w, r_p, r_f, r_rf, r_rd, r_d, r_g, r_e, s_o, s_i,
):
    c = lax.axis_index("context")
    d = lax.axis_index("dp")
    z, x = c // NX, c % NX
    y, k = d // 2, d % 2

    def zp(i):
        return lax.rem(z + i + NZ, NZ)

    def xp(i):
        return lax.rem(x + i + NX, NX)

    def dpp(i):
        return lax.rem(d + i + ND, ND)

    def yp(i):
        return lax.rem(y + i + NY, NY)

    sent = [0] * 11

    def count(group, ref):
        size = ref.dtype.itemsize
        for n in ref.shape:
            size *= n
        sent[group] += size

    def send(src, dst, group, rs, **to):
        pltpu.make_async_remote_copy(
            src_ref=src, dst_ref=dst, send_sem=s_all.at[group], recv_sem=rs, device_id=to, device_id_type=MESH
        ).start()
        count(group, src)

    def wait(dst, rs):
        pltpu.make_async_remote_copy(
            src_ref=dst, dst_ref=dst, send_sem=rs, recv_sem=rs, device_id={"context": zp(1) * NX + x}, device_id_type=MESH
        ).wait_recv()

    def wait_sends(group):
        cells = sent[group] // 2
        parts = []
        for r in range(768, 0, -16):
            if cells % (r * 128) == 0 and cells // r <= 3840:
                parts.append(wf.at[pl.ds(0, r), pl.ds(0, cells // r)])
        for a in range(1, NZ + 1):
            for b in range(1, NX + 1):
                if cells % (a * b * 24 * 128) == 0 and cells // (a * b * 24) <= 3840:
                    parts.append(wg.at[pl.ds(0, a), pl.ds(0, b), :, pl.ds(0, cells // (a * b * 24))])
        pltpu.make_async_copy(parts[0], parts[0], s_all.at[group]).wait()

    barrier = pltpu.get_barrier_semaphore()
    for i in range(1, NZ):
        pl.semaphore_signal(barrier, inc=1, device_id={"context": zp(i) * NX + x}, device_id_type=MESH)
    for i in range(1, NX):
        pl.semaphore_signal(barrier, inc=1, device_id={"context": z * NX + xp(i)}, device_id_type=MESH)
    for i in range(1, ND):
        pl.semaphore_signal(barrier, inc=1, device_id={"dp": dpp(i)}, device_id_type=MESH)
    right, left = lax.rem(c + 1, NZ * NX), lax.rem(c + NZ * NX - 1, NZ * NX)
    pl.semaphore_signal(barrier, inc=1, device_id={"context": right}, device_id_type=MESH)
    pl.semaphore_signal(barrier, inc=1, device_id={"context": left}, device_id_type=MESH)
    loads = []
    for i, (src, dst) in enumerate(
        (
            (i_cw, wg.at[z, x]), (i_bases, bases), (i_embed, embed), (i_head_h, head_h),
            (i_head_m, head_m), (i_cot_h, cot_h), (i_cot_m, cot_m), (i_dw, dw),
        )
    ):
        load = pltpu.make_async_copy(src, dst, s_i.at[i])
        load.start()
        loads.append(load)
    stores = []

    def store(src, dst):
        out = pltpu.make_async_copy(src, dst, s_i.at[8 + len(stores)])
        out.start()
        stores.append(out)

    loads[0].wait()
    loads[1].wait()
    pl.semaphore_wait(barrier, NZ - 1 + NX - 1 + ND - 1 + 2)

    mine = pl.multiple_of(HALF * k, 128)
    other = pl.multiple_of(HALF * (1 - k), 128)
    c0 = pl.ds(mine, SPLIT)
    c1 = pl.ds(pl.multiple_of(mine + SPLIT, 128), HALF - SPLIT)
    o0 = pl.ds(other, SPLIT)
    o1 = pl.ds(pl.multiple_of(other + SPLIT, 128), HALF - SPLIT)
    sib = 2 * y + 1 - k

    def blk1(q):
        return wg.at[zp(-q), x, :, c1]

    def to_z(i):
        return dict(context=zp(i) * NX + x)

    def to_x(i):
        return dict(context=z * NX + xp(i))

    send(bases.at[:, pl.ds(ROWS - 128, 128)], hl, 0, r_h.at[0], context=right)
    send(bases.at[:, pl.ds(0, 128)], hr, 0, r_h.at[1], context=left)
    for i in range(1, NX):
        send(wg.at[z, x, :, c0], wg.at[z, x, :, c0], 9, r_w.at[0], **to_x(i))
    send(blk1(0), blk1(0), 10, r_w.at[3], **to_z(1))
    send(blk1(0), blk1(0), 10, r_w.at[9], **to_z(-1))
    for i in range(1, NX):
        send(blk1(0), blk1(0), 8, r_w.at[10], **to_x(i))

    rows60 = lax.broadcasted_iota(jnp.int32, (64, 60), 0)
    cols60 = lax.broadcasted_iota(jnp.int32, (64, 60), 1)
    place = jnp.where(cols60 == 4 * (15 - rows60 % 16) + rows60 // 16, 1.0, 0.0).astype(BF)
    loads[2].wait()
    embp[...] = dot(place, embed[...]).astype(BF)
    wait(hl, r_h.at[0])
    wait(hr, r_h.at[1])
    before = jnp.where(c == 0, -1, hl[...])
    after = jnp.where(c == NZ * NX - 1, -1, hr[...])
    line = jnp.concatenate([before, bases[...], after], axis=1)
    rolled = pltpu.roll(jnp.broadcast_to(line, (16, ROWS + 256)), 648, 1, stride=1, stride_axis=0)
    for j in range(4):
        e_ref[16 * j : 16 * j + 16, :] = jnp.where(rolled[:, :WIDE] == j, 1.0, 0.0).astype(BF)
    for i in range(WIDE // 128):
        block = e_ref[:, 128 * i : 128 * i + 128].astype(F32)
        et_ref[128 * i : 128 * i + 128, :] = block.T.astype(BF)
    fpad[0:8, :] = jnp.zeros((8, WIDTH), F32)
    fpad[EXT + 8 : EXT + 16, :] = jnp.zeros((8, WIDTH), F32)

    def embed_step(i):
        r0 = pl.multiple_of(i * 32, 32)
        values = dot(et_ref[pl.ds(r0, 32), :], embp[...]).astype(BF)
        first[pl.ds(r0, 32), :] = values
        values = values.astype(F32)
        factor = lax.rsqrt(jnp.mean(values * values, axis=1, keepdims=True) + EPSILON)
        normed = values * factor
        value, slope = gelu_both(normed)
        spot = lax.broadcasted_iota(jnp.int32, (32, WIDTH), 0) + (c * ROWS + r0 - OFF)
        inside = jnp.logical_and(spot >= 0, spot < ROWS * NZ * NX)
        value = jnp.where(inside, value, 0.0)
        fpad[pl.ds(r0 + 8, 32), :] = value.astype(BF).astype(F32)
        nm_ref[pl.ds(r0, 32), :] = normed
        gn_ref[pl.ds(r0, 32), :] = slope
        fac_ref[pl.ds(r0, 32), :] = jnp.broadcast_to(factor, (32, 128))

    def head_rows():
        for load in loads[3:]:
            load.wait()
        hmt[0:176, :] = head_h[0:176, :]
        last = jnp.concatenate([head_h[176:184, :].astype(F32), jnp.zeros((8, 1536), F32)], axis=0)
        hmt[176:192, :] = last.astype(BF)
        hmt[192:224, :] = head_m[...]
        hmt[224:256, :] = jnp.zeros((32, 1536), BF)
        human = (organism[0] == 0).astype(F32)
        cot[0:184, :] = cot_h[...].astype(F32) * human
        cot[184:192, :] = jnp.zeros((8, 128), F32)
        cot[192:224, :] = cot_m[...].astype(F32) * (1.0 - human)
        cot[224:256, :] = jnp.zeros((32, 128), F32)

    def head_turn(i):
        cols = pl.ds(pl.multiple_of(128 * i, 128), 128)
        hm[cols, :] = hmt[:, cols].astype(F32).T.astype(BF)

    def ring1_up(s):
        wait(blk1(s), r_w.at[2 + s])
        if s < 4:
            send(blk1(s), blk1(s), 10, r_w.at[3 + s], **to_z(1))
        spread1(s)

    def ring1_down(s):
        q = NZ - s
        wait(blk1(q), r_w.at[2 + q])
        if s < 3:
            send(blk1(q), blk1(q), 10, r_w.at[1 + q], **to_z(-1))
        spread1(q)

    def spread1(q):
        for i in range(1, NX):
            send(blk1(q), blk1(q), 8, r_w.at[10 + q], **to_x(i))

    def blk0(q, cols):
        return wg.at[zp(-q), :, :, cols]

    def chunk(low, h):
        return pl.ds(pl.multiple_of(low + 256 * h, 128), 256)

    def ring0(s, h):
        for down in range(2):
            if s == 4 and down != h // 2:
                continue
            q = NZ - s if down else s
            part = blk0(q, chunk(mine, h))
            wait(part, r_w.at[34 + 8 * h + q])
            if s < 3 or (s == 3 and down == h // 2):
                step = -1 if down else 1
                send(part, part, 1, r_w.at[34 + 8 * h + q + step], **to_z(step))
            send(part, part, 2, r_w.at[26 + q], dp=sib)

    def pass_on(q):
        wait(wg.at[zp(-q), pl.ds(0, 3), :, c1], r_w.at[10 + q])
        if q:
            here = wg.at[zp(-q), :, :, c1]
            send(here, here, 10, r_w.at[18 + q], dp=sib)
        else:
            for i in range(1, NX):
                here = wg.at[z, xp(-i), :, c1]
                send(here, here, 10, r_w.at[18], dp=sib)

    def pack(q):
        if q:
            wait(wg.at[zp(-q), :, :, o1], r_w.at[18 + q])
            wait(wg.at[zp(-q), :, :, o0], r_w.at[26 + q])
        else:
            wait(wg.at[z, pl.ds(0, 3), :, o1], r_w.at[18])
            wait(wg.at[z, pl.ds(0, 3), :, o0], r_w.at[1])
        zz = zp(-q)

        def pack_step(i):
            pair = jnp.concatenate([wg[zz, 2 * i].astype(F32), wg[zz, 2 * i + 1].astype(F32)], axis=0)
            wf[pl.ds(pl.multiple_of(96 * zz + 48 * i, 16), 48), :] = pair.astype(BF)

        loop(2, pack_step)

    def embed_some(low, high):
        def body(i):
            embed_step(i + low)

        loop(high - low, body)

    def shift_step(i):
        r0 = pl.multiple_of(i * 32, 32)
        block = fpad[pl.ds(r0, 48), :]
        for t in range(SPAN):
            acols[t, pl.ds(r0, 32), :] = block[t + 6 : t + 38].astype(BF)

    ring1_up(1)
    ring1_down(1)
    wait(wg.at[z, pl.ds(0, 3), :, c0], r_w.at[0])
    for i in range(1, NX):
        here = wg.at[z, xp(-i), :, c0]
        send(here, here, 9, r_w.at[1], dp=sib)
    for h in range(4):
        part = blk0(0, chunk(mine, h))
        send(part, part, 1, r_w.at[34 + 8 * h + 1], **to_z(1))
        send(part, part, 1, r_w.at[34 + 8 * h + 7], **to_z(-1))
    embed_some(0, 4)
    ring1_up(2)
    ring1_down(2)
    embed_step(4)
    for s in range(1, 4):
        for h in range(4):
            ring0(s, h)
            embed_step(1 + 4 * s + h)
            if s == 1 and h == 1:
                ring1_up(3)
                ring1_down(3)
            if s == 2 and h == 1:
                ring1_up(4)
        if s == 2:
            pass_on(0)
        if s == 3:
            pass_on(1)
            pass_on(7)
    head_rows()
    loop(EXT // 32, shift_step)
    pass_on(2)
    pass_on(6)
    pack(0)
    for h in (0, 2, 1, 3):
        ring0(4, h)
        if h == 0:
            pack(1)
            pack(7)
    for q in (3, 5, 4):
        pass_on(q)
    loop(12, head_turn)
    for q in (2, 6, 3, 5, 4):
        pack(q)

    own_cols = pl.ds(pl.multiple_of((WIDTH // 2) * k, 128), WIDTH // 2)
    sib_cols = pl.ds(pl.multiple_of((WIDTH // 2) * (1 - k), 128), WIDTH // 2)
    local = []
    for t in range(SPAN):
        dst = ah.at[pl.ds(0, ROWS), pl.ds(384 * t, 384)]
        copy = pltpu.make_async_copy(acols.at[t, pl.ds(OFF, ROWS), own_cols], dst, s_o.at[t])
        copy.start()
        local.append(copy)
        send(
            acols.at[t, pl.ds(OFF, ROWS), sib_cols], ah.at[pl.ds(ROWS, ROWS), pl.ds(384 * t, 384)],
            9, r_d.at[4], dp=sib,
        )
    ah[:, pl.ds(HALF, 128)] = jnp.zeros((2 * ROWS, 128), BF)
    def conv_step(i):
        o0_ = pl.multiple_of(i * 256, 256)
        total = dot(acols[0], wf[pl.ds(o0_, 256), 0:WIDTH], 1, 1)
        for t in range(1, SPAN):
            total = total + dot(acols[t], wf[pl.ds(o0_, 256), WIDTH * t : WIDTH * (t + 1)], 1, 1)
        mixed[:, pl.ds(o0_, 256)] = total

    loop(3, conv_step)

    pooled = []
    for t in range(4):
        def pool_step(i, total):
            r0 = pl.multiple_of(OFF + 128 * t + 32 * i, 16)
            part = first[pl.ds(r0, 32), :].astype(F32) + gelu_value(mixed[pl.ds(r0, 32), :])
            return total + part.reshape(4, 8, WIDTH).sum(axis=0)

        total = lax.fori_loop(0, 4, pool_step, jnp.zeros((8, WIDTH), F32))
        row = jnp.sum(total, axis=0, keepdims=True) / 128.0
        pooled.append(row)

    pieces = [row[:, 256 * m : 256 * m + 256] for m in range(3) for row in pooled]
    pbuf[z, x] = jnp.concatenate(pieces + [jnp.zeros((4, 256), F32)], axis=0).astype(BF)
    near = (1, 7, 2, 6, 3, 5, 4)
    far = (4, 3, 5, 2, 6, 1, 7, 0)

    def relay_gather(buf, group, rs, between=None):
        own = buf.at[z, x]
        for q in near:
            send(own, own, group, rs.at[q], **to_z(q))
        for i in range(1, NX):
            send(own, own, group, rs.at[0], **to_x(i))
        if between is not None:
            between()
        for q in near:
            here = buf.at[zp(-q), x]
            wait(here, rs.at[q])
            for i in range(1, NX):
                send(here, here, group, rs.at[0], **to_x(i))

    def relay_finish(buf, rs):
        wait(buf.at[:, pl.ds(0, 3)], rs.at[0])

    def scatter_start(src, got, group, rs):
        for q in far:
            for i in range(1, NX):
                send(src.at[zp(q), xp(i)], got.at[i, q], group, rs.at[q], **to_x(i))

    def scatter_turn(src, got, zsrc, zgot, group, rs):
        for q in far:
            total = src[zp(q), x].astype(F32)
            wait(got.at[pl.ds(1, 3), q], rs.at[q])
            for i in range(1, NX):
                total = total + got[i, q].astype(F32)
            if q:
                zsrc[q] = total.astype(BF)
                send(zsrc.at[q], zgot.at[q], group, rs.at[NZ], **to_z(q))
        return total

    def scatter_finish(total, zgot, rs):
        wait(zgot.at[pl.ds(1, 7)], rs.at[NZ])
        for q in near:
            total = total + zgot[q].astype(F32)
        return total

    relay_gather(pbuf, 3, r_p)

    def slope_step(i):
        r0 = pl.multiple_of(i * 32, 32)
        mixed[pl.ds(r0, 32), :] = gelu_slope(mixed[pl.ds(r0, 32), :])

    loop(EXT // 32, slope_step)
    for t in range(SPAN):
        dw2[48 * t : 48 * t + 48, :] = dw[:, WIDTH * t : WIDTH * (t + 1)]
    zero8 = jnp.zeros((8, WIDTH), F32)
    dn_ref[0:8, :] = zero8
    dn_ref[136:144, :] = zero8
    dpad[0:8, :] = zero8
    dpad[136:144, :] = zero8
    dbp[0:8, :] = zero8
    dbp[136:144, :] = zero8
    df_ref[...] = jnp.ones((144, 128), F32)
    relay_finish(pbuf, r_p)

    def coarse_step(i):
        zz, half = i // 2, 2 * (i % 2)
        v0, v1 = pbuf[zz, half].astype(F32), pbuf[zz, half + 1].astype(F32)
        parts = [jnp.concatenate([v0[4 * m : 4 * m + 4], v1[4 * m : 4 * m + 4]], axis=0) for m in range(3)]
        values = jnp.concatenate(parts, axis=1)
        factor = lax.rsqrt(jnp.mean(values * values, axis=1, keepdims=True) + EPSILON)
        normed = values * factor
        r0 = pl.multiple_of(8 * i + 8, 8)
        dn_ref[pl.ds(r0, 8), :] = normed
        df_ref[pl.ds(r0, 8), :] = jnp.broadcast_to(factor, (8, 128))
        dpad[pl.ds(r0, 8), :] = gelu_value(normed).astype(BF).astype(F32)

    loop(16, coarse_step, unroll=4)
    block = dpad[...]
    for t in range(SPAN):
        dcols[t] = block[t + 6 : t + 134].astype(BF)
    total = dot(dw[:, 0:WIDTH], dcols[0], 1, 1)
    for t in range(1, SPAN):
        total = total + dot(dw[:, WIDTH * t : WIDTH * (t + 1)], dcols[t], 1, 1)
    ft[z, x] = total.astype(BF)
    dax[pl.ds(pl.multiple_of(d * 128, 128), 128), :] = dcols[2]

    def dp_slot(ref, i, size):
        return ref.at[pl.ds(pl.multiple_of(i * size, 16), size)]

    def coarse_background():
        for i in range(1, ND):
            send(dcols.at[2], dp_slot(dax, d, 128), 8, r_d.at[0], dp=dpp(i))

    relay_gather(ft, 4, r_f, coarse_background)
    relay_finish(ft, r_f)

    feats = ft[...].reshape(1536, 128)
    logit = dot(hmt[...], feats)
    delta = (cot[...] * jax.nn.sigmoid(logit)).astype(BF)
    dtx[d] = delta
    fbs[...] = dot(hm[...], delta).astype(BF).reshape(NZ, NX, 48, 128)
    scatter_start(fbs, fxr, 5, r_rf)
    for i in range(1, ND):
        send(dtx.at[d], dtx.at[d], 4, r_d.at[1], dp=dpp(i))
        send(ft.at[dpp(i)], fxs.at[d], 4, r_d.at[2], dp=dpp(i))
    fxs[d] = ft[d]

    own_part = scatter_turn(fbs, fxr, fzs, fzr, 5, r_rf)
    fdelta = scatter_finish(own_part, fzr, r_rf).astype(BF)
    fdx[d] = fdelta

    lanes = lax.broadcasted_iota(jnp.int32, (48, 128), 1)

    def shifted(values):
        wide = values.astype(F32)
        parts = []
        for t in range(SPAN):
            move = t - 2
            if move == 0:
                parts.append(wide)
                continue
            turned = pltpu.roll(wide, move % 128, 1)
            keep = lanes >= move if move > 0 else lanes < 128 + move
            parts.append(jnp.where(keep, turned, 0.0))
        return jnp.concatenate(parts, axis=0).astype(BF)

    back = dot(shifted(fdelta), dw2[...], 0, 0)
    dbp[8:136, :] = back

    def piece_step(i):
        block = dbp[pl.ds(pl.multiple_of(8 * i, 8), 24), :]
        zz, half = i // 2, 2 * (i % 2)
        for j, low in ((0, 6), (1, 10)):
            rows = block[low : low + 8]
            dbs[zz, half + j] = jnp.concatenate([rows[:, :384], rows[:, 384:]], axis=0).astype(BF)

    loop(16, piece_step, unroll=4)
    scatter_start(dbs, dxr, 5, r_rd)
    for i in range(1, ND):
        send(fdx.at[d], fdx.at[d], 4, r_d.at[3], dp=dpp(i))
    own_part = scatter_turn(dbs, dxr, dzs, dzr, 5, r_rd)

    wait(dtx.at[pl.ds(0, 7)], r_d.at[1])
    wait(fxs.at[pl.ds(0, 7)], r_d.at[2])
    total = jnp.zeros((256, 192), F32)
    for i in range(ND):
        total = total + dot(dtx[i], fxs[i].reshape(192, 128), 1, 1)
    o_gh[...] = total[:184]
    o_gm[...] = total[192:224]
    store(o_gh, q_gh)
    store(o_gm, q_gm)

    deep_back = scatter_finish(own_part, dzr, r_rd)
    deep_back = jnp.concatenate([deep_back[:8], deep_back[8:]], axis=1)
    r0 = pl.multiple_of(8 * (c // 2), 8)

    def own_rows(ref):
        block = ref[pl.ds(r0, 24), :]
        return jnp.where(c % 2 == 0, block[6:14], block[10:18])

    dnormed = own_rows(dn_ref)
    dfactor = own_rows(df_ref)[:, :1]
    v = deep_back * gelu_slope(dnormed)
    pd_ref[...] = dfactor * (v - dnormed * jnp.mean(v * dnormed, axis=1, keepdims=True)) / 128.0

    fdp[0:8, :] = zero8
    fdp[EXT + 8 : EXT + 16, :] = zero8

    def fine_step(i):
        r0 = pl.multiple_of(i * 16, 16)
        row = pd_ref[pl.ds((r0 + 112) // 128 + 1, 1), :]
        fine = (mixed[pl.ds(r0, 16), :] * row).astype(BF).astype(F32)
        fdp[pl.ds(r0 + 8, 16), :] = fine

    loop(EXT // 16, fine_step, unroll=2)
    for i in range(4):
        block = fdp[OFF + 8 + 128 * i : OFF + 136 + 128 * i, :]
        fdt[0, :, 128 * i : 128 * i + 128] = block.T.astype(BF)
    send(fdt.at[0], fdt.at[1], 6, r_g.at[0], dp=sib)

    def back_shift(i):
        r0 = pl.multiple_of(i * 32, 32)
        block = fdp[pl.ds(r0, 48), :]
        for t in range(SPAN):
            fdc[t, pl.ds(r0, 32), :] = block[10 - t : 42 - t].astype(BF)

    loop(EXT // 32, back_shift)
    for copy in local:
        copy.wait()
    wait(ah.at[pl.ds(ROWS, ROWS), pl.ds(0, HALF)], r_d.at[4])
    wait(fdt.at[1], r_g.at[0])

    def grad_chunk(low):
        cols = pl.ds(pl.multiple_of(low, 256), 256)
        return dot(fdt[0], ah[pl.ds(0, ROWS), cols]) + dot(fdt[1], ah[pl.ds(ROWS, ROWS), cols])

    def by_x(total, xx):
        return jnp.concatenate(
            [total[24 * (4 * zz + xx) : 24 * (4 * zz + xx) + 24] for zz in range(NZ)], axis=0
        ).astype(BF)

    halves = (pl.ds(0, 96), pl.ds(96, 96))

    def alpha_send(i, h):
        send(
            ga.at[yp(i), :, halves[h]], gar.at[i, :, halves[h]],
            6, r_g.at[1 + h], dp=2 * yp(i) + k,
        )

    def beta_send(yy, i, h):
        send(
            gb.at[xp(i), yy, halves[h]], gbr.at[i, yy, halves[h]],
            6, r_g.at[3 + h], **to_x(i),
        )

    for n in range(NY):
        total = grad_chunk(512 * n + 256)
        for xx in range(NX):
            gb[xx, n] = by_x(total, xx)
        for i in range(1, NX):
            beta_send(n, i, 0)
        yy = yp(n + 1)
        total = grad_chunk(512 * yy)
        for xx in range(NX):
            ga[yy, xx] = by_x(total, xx)
        if n < NY - 1:
            alpha_send(n + 1, 0)
    for n in range(NY):
        for i in range(1, NX):
            beta_send(n, i, 1)
        if n < NY - 1:
            alpha_send(n + 1, 1)

    def second_phase(h):
        wait(gar.at[pl.ds(1, 3), :, halves[h]], r_g.at[1 + h])
        for xx in range(NX):
            for low in (96 * h, 96 * h + 48):
                rows = pl.ds(low, 48)
                total = ga[y, xx, rows, :].astype(F32)
                for i in range(1, NY):
                    total = total + gar[i, xx, rows, :].astype(F32)
                ha[xx, rows, :] = total.astype(BF)
        for i in range(1, NX):
            send(ha.at[xp(i), halves[h]], har.at[i, halves[h]], 7, r_g.at[5 + h], **to_x(i))
        wait(gbr.at[pl.ds(1, 3), :, halves[h]], r_g.at[3 + h])
        for yy in range(NY):
            for low in (96 * h, 96 * h + 48):
                rows = pl.ds(low, 48)
                total = gb[x, yy, rows, :].astype(F32)
                for i in range(1, NX):
                    total = total + gbr[i, yy, rows, :].astype(F32)
                hb[yy, rows, :] = total.astype(BF)
        for i in range(1, NY):
            send(
                hb.at[yp(i), halves[h]], hbr.at[i, halves[h]],
                7, r_g.at[7 + h], dp=2 * yp(i) + k,
            )

    def third_copy(zz):
        return pltpu.make_async_remote_copy(
            src_ref=zs.at[zz], dst_ref=zr.at[z], send_sem=s_all.at[7], recv_sem=r_g.at[9],
            device_id={"context": zz * NX + x}, device_id_type=MESH,
        )

    def third_phase(h):
        wait(har.at[pl.ds(1, 3), halves[h]], r_g.at[5 + h])
        wait(hbr.at[pl.ds(1, 3), halves[h]], r_g.at[7 + h])
        for m in range(2):
            rows = pl.ds(96 * h + 48 * m, 48)
            left_half = ha[x, rows, :].astype(F32)
            right_half = hb[y, rows, :].astype(F32)
            for i in range(1, 4):
                left_half = left_half + har[i, rows, :].astype(F32)
                right_half = right_half + hbr[i, rows, :].astype(F32)
            zz = 4 * h + 2 * m
            zs[zz] = jnp.concatenate([left_half[:24], right_half[:24]], axis=0).astype(BF)
            zs[zz + 1] = jnp.concatenate([left_half[24:], right_half[24:]], axis=0).astype(BF)
            for to in (zz, zz + 1):

                @pl.when(z != to)
                def _(to=to):
                    third_copy(to).start()

    def back_step(i):
        cols = 256 * i
        total = dot(fdc[0], wf[:, cols : cols + 256])
        for t in range(1, SPAN):
            total = total + dot(fdc[t], wf[:, WIDTH * t + cols : WIDTH * t + cols + 256])
        fdp[0:EXT, cols : cols + 256] = total

    for i in range(3):
        back_step(i)

    second_phase(0)
    fhl[0, EXT:WIDE, :] = jnp.zeros((WIDE - EXT, WIDTH), BF)
    fhl[1, EXT:WIDE, :] = jnp.zeros((WIDE - EXT, WIDTH), BF)

    def delta_step(i):
        r0 = pl.multiple_of(i * 16, 16)
        row = pd_ref[pl.ds((r0 + 112) // 128 + 1, 1), :]
        normed = nm_ref[pl.ds(r0, 16), :]
        w = fdp[pl.ds(r0, 16), :] * gn_ref[pl.ds(r0, 16), :]
        factor = fac_ref[pl.ds(r0, 16), :][:, :1]
        value = row + factor * (w - normed * jnp.mean(w * normed, axis=1, keepdims=True))
        value = jnp.where(jnp.logical_and(r0 >= OFF, r0 < OFF + ROWS), value, 0.0)
        fdl[pl.ds(r0, 16), :] = value
        high = value.astype(BF)
        fhl[0, pl.ds(r0, 16), :] = high
        fhl[1, pl.ds(r0, 16), :] = (value - high.astype(F32)).astype(BF)

    loop(EXT // 16, delta_step, unroll=2)
    out_copy = pltpu.make_async_copy(fdl.at[pl.ds(OFF, ROWS)], o_fd, s_o.at[5])
    out_copy.start()
    ep[...] = (dot(e_ref[...], fhl[0]) + dot(e_ref[...], fhl[1])).reshape(NZ, 8, WIDTH)
    for q in far[:7]:
        part = ep[zp(q)]
        es[q] = jnp.concatenate([part[:, :384], part[:, 384:]], axis=0).astype(BF)
        send(es.at[q], er.at[q], 7, r_e.at[0], **to_z(q))

    wait(dax.at[pl.ds(0, 896)], r_d.at[0])
    wait(fdx.at[pl.ds(0, 7)], r_d.at[3])
    for i in range(ND):
        fkx[:, 128 * i : 128 * i + 128] = shifted(fdx[i])
    deep_total = dot(fkx[...], dax[...])
    for t in range(SPAN):
        o_gd[:, WIDTH * t : WIDTH * (t + 1)] = deep_total[48 * t : 48 * t + 48]
    store(o_gd, q_gd)

    third_phase(0)

    wait(er.at[pl.ds(1, 7)], r_e.at[0])
    total = er[1].astype(F32)
    for q in near[1:]:
        total = total + er[q].astype(F32)
    ex[x] = ep[z] + jnp.concatenate([total[:8], total[8:]], axis=1)
    for i in range(1, NX):
        send(ex.at[x], ex.at[x], 7, r_e.at[1], **to_x(i))
    second_phase(1)
    wait(ex.at[pl.ds(0, 3)], r_e.at[1])
    ey[d] = (ex[0] + ex[1]) + (ex[2] + ex[3])
    for i in range(1, ND):
        send(ey.at[d], ey.at[d], 7, r_e.at[2], dp=dpp(i))
    third_phase(1)
    wait(ey.at[pl.ds(0, 7)], r_e.at[2])
    total = ey[0]
    for i in range(1, ND):
        total = total + ey[i]
    eg[z] = jnp.concatenate([total[:, :384], total[:, 384:]], axis=0).astype(BF)
    for i in range(1, NZ):
        send(eg.at[z], eg.at[z], 7, r_e.at[3], **to_z(i))

    total = zs[z].astype(F32)
    wait(zr.at[pl.ds(0, 7)], r_g.at[9])
    for i in range(1, NZ):
        total = total + zr[zp(i)].astype(F32)
    fin[d] = total.astype(BF)
    for i in range(1, NZ):
        count(7, zs.at[i])
    for i in range(1, ND):
        send(fin.at[d], fin.at[d], 7, r_g.at[10], dp=dpp(i))
    wait(eg.at[pl.ds(0, 7)], r_e.at[3])
    blocks = []
    for i in range(NZ):
        block = eg[i].astype(F32)
        blocks.append(jnp.concatenate([block[:8], block[8:]], axis=1))
    for t in range(15):
        for j in range(4):
            row = (15 - t) % 8
            o_ge[4 * t + j : 4 * t + j + 1, :] = blocks[2 * j + (15 - t) // 8][row : row + 1, :]
    store(o_ge, q_ge)
    wait(fin.at[pl.ds(0, 7)], r_g.at[10])
    for i in range(ND):
        for t in range(4):
            tile = 4 * (i // 2) + t
            if tile >= 15:
                continue
            column = 128 * (6 * (tile // 3) + 3 * (i % 2) + tile % 3)
            part = fin[i, 24 * (t // 2) : 24 * (t // 2) + 24, 128 * (t % 2) : 128 * (t % 2) + 128]
            o_gc[:, column : column + 128] = part.astype(F32)
    store(o_gc, q_gc)

    out_copy.wait()
    for out in stores:
        out.wait()
    both = bases.at[:, pl.ds(0, 256)]
    pltpu.make_async_copy(both, both, s_all.at[0]).wait()
    for group in range(1, 11):
        wait_sends(group)


def place(*refs):
    count = 6
    held, sems = refs[2 * count : 3 * count], refs[-1]
    loads = [pltpu.make_async_copy(refs[i], held[i], sems.at[0, i]) for i in range(count)]
    stores = [pltpu.make_async_copy(held[i], refs[count + i], sems.at[1, i]) for i in range(count)]
    for load in loads:
        load.start()
    for load, out in zip(loads, stores):
        load.wait()
        out.start()
    for out in stores:
        out.wait()


def shards(bases, organism, embed_weight, conv_weight, deep_weight, human_head, mouse_head, human_cotangent, mouse_cotangent):
    vmem, dma = pltpu.VMEM, pltpu.SemaphoreType.DMA
    scratch = [
        vmem((1, ROWS), jnp.int32), vmem((60, WIDTH), BF), vmem((48, 3840), BF), vmem((184, 1536), BF),
        vmem((32, 1536), BF), vmem((184, 128), BF), vmem((32, 128), BF),
        vmem((60, WIDTH), F32), vmem((24, 3840), F32), vmem((48, 3840), F32), vmem((184, 192), F32), vmem((32, 192), F32),
        vmem((1536, 256), BF), vmem((256, 1536), BF), vmem((256, 128), F32),
        vmem((1, 128), jnp.int32), vmem((1, 128), jnp.int32),
        vmem((64, WIDE), BF), vmem((WIDE, 64), BF), vmem((64, WIDTH), BF),
        vmem((EXT + 16, WIDTH), F32), vmem((EXT, WIDTH), BF), vmem((EXT, WIDTH), F32),
        vmem((EXT, WIDTH), F32), vmem((EXT, 128), F32), vmem((SPAN, EXT, WIDTH), BF),
        vmem((NZ, NX, 24, 3840), BF), vmem((WIDTH, 3840), BF), vmem((EXT, WIDTH), F32),
        vmem((2 * ROWS, 2048), BF),
        vmem((NZ, NX, 16, 256), BF), vmem((144, WIDTH), F32), vmem((144, WIDTH), F32), vmem((144, 128), F32),
        vmem((SPAN, 128, WIDTH), BF), vmem((NZ, NX, 48, 128), BF),
        vmem((ND, 256, 128), BF), vmem((ND, 4, 48, 128), BF),
        vmem((NZ, NX, 48, 128), BF), vmem((4, NZ, 48, 128), BF), vmem((NZ, 48, 128), BF), vmem((NZ, 48, 128), BF),
        vmem((ND, 48, 128), BF), vmem((240, 1024), BF), vmem((240, WIDTH), BF), vmem((144, WIDTH), F32),
        vmem((NZ, NX, 16, 384), BF), vmem((4, NZ, 16, 384), BF), vmem((NZ, 16, 384), BF), vmem((NZ, 16, 384), BF),
        vmem((1024, WIDTH), BF), vmem((8, WIDTH), F32),
        vmem((EXT + 16, WIDTH), F32), vmem((SPAN, EXT, WIDTH), BF), vmem((2, WIDTH, ROWS), BF),
        vmem((NY, NX, 192, 256), BF), vmem((NX, NY, 192, 256), BF),
        vmem((4, NX, 192, 256), BF), vmem((4, NY, 192, 256), BF),
        vmem((NX, 192, 256), BF), vmem((NY, 192, 256), BF), vmem((4, 192, 256), BF), vmem((4, 192, 256), BF),
        vmem((NZ, 48, 256), BF), vmem((NZ, 48, 256), BF), vmem((ND, 48, 256), BF),
        vmem((EXT, WIDTH), F32), vmem((2, WIDE, WIDTH), BF),
        vmem((NZ, 8, WIDTH), F32), vmem((NZ, 16, 384), BF), vmem((NZ, 16, 384), BF), vmem((NX, 8, WIDTH), F32),
        vmem((ND, 8, WIDTH), F32), vmem((NZ, 16, 384), BF),
        dma((11,)), dma((2,)), dma((66,)), dma((8,)), dma((8,)), dma((9,)), dma((9,)), dma((5,)), dma((11,)), dma((4,)),
        dma((6,)), dma((13,)),
    ]
    spec = pl.BlockSpec(memory_space=pl.ANY)
    ge, gc, gd, gh, gm, fd = pl.pallas_call(
        kernel,
        out_shape=(
            jax.ShapeDtypeStruct((60, WIDTH), F32),
            jax.ShapeDtypeStruct((24, 3840), F32),
            jax.ShapeDtypeStruct((48, 3840), F32),
            jax.ShapeDtypeStruct((184, 192), F32),
            jax.ShapeDtypeStruct((32, 192), F32),
            jax.ShapeDtypeStruct((ROWS, WIDTH), F32),
        ),
        in_specs=[spec, pl.BlockSpec(memory_space=pltpu.SMEM)] + [spec] * 7,
        out_specs=(spec,) * 6,
        scratch_shapes=scratch,
        compiler_params=pltpu.CompilerParams(
            collective_id=0, has_side_effects=True, vmem_limit_bytes=60 * 1024 * 1024
        ),
        cost_estimate=pl.CostEstimate(flops=10_000_000_000, bytes_accessed=8_000_000, transcendentals=2_000_000),
    )(
        bases, organism, embed_weight, conv_weight, deep_weight,
        human_head.T, mouse_head.T, human_cotangent[0].T, mouse_cotangent[0].T,
    )
    results = (ge, gc, gd, gh, gm, fd)
    ge, gc, gd, gh, gm, fd = pl.pallas_call(
        place,
        out_shape=tuple(jax.ShapeDtypeStruct(a.shape, a.dtype) for a in results),
        in_specs=[spec] * 6,
        out_specs=(spec,) * 6,
        scratch_shapes=[vmem(a.shape, a.dtype) for a in results] + [dma((2, 6))],
        compiler_params=pltpu.CompilerParams(vmem_limit_bytes=60 * 1024 * 1024),
    )(*results)
    return ge, gc, gd, gh.T, gm.T, fd[None]


def solution(mesh):
    return jax.shard_map(
        shards,
        mesh=mesh,
        in_specs=(
            P("dp", "context"),
            P("dp"),
            P(),
            P("context", None),
            P("context", None),
            P(None, "context"),
            P(None, "context"),
            P("dp", None, "context"),
            P("dp", None, "context"),
        ),
        out_specs=(
            P(),
            P("context", None),
            P("context", None),
            P("dp", "context"),
            P("dp", "context"),
            P("dp", "context", None),
        ),
        check_vma=False,
    )
```

```python
import jax
import jax.numpy as jnp
from jax import lax
from jax.experimental import pallas as pl
from jax.experimental.pallas import tpu as pltpu
from jax.sharding import PartitionSpec as P

F32 = jnp.float32
BF = jnp.bfloat16
MESH = pl.DeviceIdType.MESH

WIDTH = 768
SPAN = 5
NZ, NX, NY = 8, 4, 4
ND = 8
ROWS = 512
OFF = 16
EXT = ROWS + 2 * OFF
WIDE = 640
HALF = 1920
SPLIT = 896

SLOPE = 0.7978845608028654
CUBIC = 0.044715
EPSILON = 1e-06


def gelu_both(value):
    square = value * value
    tangent = jnp.tanh(SLOPE * (value + CUBIC * square * value))
    half = 0.5 * (1.0 + tangent)
    slope = half + 0.5 * value * (1.0 - tangent * tangent) * SLOPE * (1.0 + 3.0 * CUBIC * square)
    return value * half, slope


def gelu_value(value):
    return 0.5 * value * (1.0 + jnp.tanh(SLOPE * (value + CUBIC * value * value * value)))


def gelu_slope(value):
    return gelu_both(value)[1]


def dot(a, b, ca=1, cb=0):
    return lax.dot_general(a, b, (((ca,), (cb,)), ((), ())), preferred_element_type=F32)


def loop(count, body, unroll=1):
    def step(i, carry):
        body(i)
        return carry

    lax.fori_loop(0, count, step, 0, unroll=unroll)


def kernel(
    i_bases, organism, i_embed, i_cw, i_dw, i_head_h, i_head_m, i_cot_h, i_cot_m,
    q_ge, q_gc, q_gd, q_gh, q_gm, o_fd,
    bases, embed, dw, head_h, head_m, cot_h, cot_m, o_ge, o_gc, o_gd, o_gh, o_gm,
    hm, hmt, cot, hl, hr, e_ref, et_ref, embp, fpad, first, nm_ref, gn_ref, fac_ref, acols, wg, wf, mixed, ah,
    pbuf, dn_ref, dpad, df_ref, dcols, ft, dtx, fxs, fbs, fxr, fzs, fzr, fdx, fkx, dw2, dbp, dbs, dxr, dzs, dzr,
    dax, pd_ref, fdp, fdc, fdt,
    ga, gb, gar, gbr, ha, hb, har, hbr, zs, zr, fin,
    fdl, fhl, ep, es, er, ex, ey, eg,
    s_all, r_h, r_w, r_p, r_f, r_rf, r_rd, r_d, r_g, r_e, s_o, s_i,
):
    c = lax.axis_index("context")
    d = lax.axis_index("dp")
    z, x = c // NX, c % NX
    y, k = d // 2, d % 2

    def zp(i):
        return lax.rem(z + i + NZ, NZ)

    def xp(i):
        return lax.rem(x + i + NX, NX)

    def dpp(i):
        return lax.rem(d + i + ND, ND)

    def yp(i):
        return lax.rem(y + i + NY, NY)

    sent = [0] * 11

    def count(group, ref):
        size = ref.dtype.itemsize
        for n in ref.shape:
            size *= n
        sent[group] += size

    def send(src, dst, group, rs, **to):
        pltpu.make_async_remote_copy(
            src_ref=src, dst_ref=dst, send_sem=s_all.at[group], recv_sem=rs, device_id=to, device_id_type=MESH
        ).start()
        count(group, src)

    def wait(dst, rs):
        pltpu.make_async_remote_copy(
            src_ref=dst, dst_ref=dst, send_sem=rs, recv_sem=rs, device_id={"context": zp(1) * NX + x}, device_id_type=MESH
        ).wait_recv()

    def wait_sends(group):
        cells = sent[group] // 2
        parts = []
        for r in range(768, 0, -16):
            if cells % (r * 128) == 0 and cells // r <= 3840:
                parts.append(wf.at[pl.ds(0, r), pl.ds(0, cells // r)])
        for a in range(1, NZ + 1):
            for b in range(1, NX + 1):
                if cells % (a * b * 24 * 128) == 0 and cells // (a * b * 24) <= 3840:
                    parts.append(wg.at[pl.ds(0, a), pl.ds(0, b), :, pl.ds(0, cells // (a * b * 24))])
        pltpu.make_async_copy(parts[0], parts[0], s_all.at[group]).wait()

    barrier = pltpu.get_barrier_semaphore()
    for i in range(1, NZ):
        pl.semaphore_signal(barrier, inc=1, device_id={"context": zp(i) * NX + x}, device_id_type=MESH)
    for i in range(1, NX):
        pl.semaphore_signal(barrier, inc=1, device_id={"context": z * NX + xp(i)}, device_id_type=MESH)
    for i in range(1, ND):
        pl.semaphore_signal(barrier, inc=1, device_id={"dp": dpp(i)}, device_id_type=MESH)
    right, left = lax.rem(c + 1, NZ * NX), lax.rem(c + NZ * NX - 1, NZ * NX)
    pl.semaphore_signal(barrier, inc=1, device_id={"context": right}, device_id_type=MESH)
    pl.semaphore_signal(barrier, inc=1, device_id={"context": left}, device_id_type=MESH)
    loads = []
    for i, (src, dst) in enumerate(
        (
            (i_cw, wg.at[z, x]), (i_bases, bases), (i_embed, embed), (i_head_h, head_h),
            (i_head_m, head_m), (i_cot_h, cot_h), (i_cot_m, cot_m), (i_dw, dw),
        )
    ):
        load = pltpu.make_async_copy(src, dst, s_i.at[i])
        load.start()
        loads.append(load)
    stores = []

    def store(src, dst):
        out = pltpu.make_async_copy(src, dst, s_i.at[8 + len(stores)])
        out.start()
        stores.append(out)

    loads[0].wait()
    loads[1].wait()
    pl.semaphore_wait(barrier, NZ - 1 + NX - 1 + ND - 1 + 2)

    mine = pl.multiple_of(HALF * k, 128)
    other = pl.multiple_of(HALF * (1 - k), 128)
    c0 = pl.ds(mine, SPLIT)
    c1 = pl.ds(pl.multiple_of(mine + SPLIT, 128), HALF - SPLIT)
    o0 = pl.ds(other, SPLIT)
    o1 = pl.ds(pl.multiple_of(other + SPLIT, 128), HALF - SPLIT)
    sib = 2 * y + 1 - k

    def blk1(q):
        return wg.at[zp(-q), x, :, c1]

    def to_z(i):
        return dict(context=zp(i) * NX + x)

    def to_x(i):
        return dict(context=z * NX + xp(i))

    send(bases.at[:, pl.ds(ROWS - 128, 128)], hl, 0, r_h.at[0], context=right)
    send(bases.at[:, pl.ds(0, 128)], hr, 0, r_h.at[1], context=left)
    for i in range(1, NX):
        send(wg.at[z, x, :, c0], wg.at[z, x, :, c0], 9, r_w.at[0], **to_x(i))
    send(blk1(0), blk1(0), 10, r_w.at[3], **to_z(1))
    send(blk1(0), blk1(0), 10, r_w.at[9], **to_z(-1))
    for i in range(1, NX):
        send(blk1(0), blk1(0), 8, r_w.at[10], **to_x(i))

    rows60 = lax.broadcasted_iota(jnp.int32, (64, 60), 0)
    cols60 = lax.broadcasted_iota(jnp.int32, (64, 60), 1)
    place = jnp.where(cols60 == 4 * (15 - rows60 % 16) + rows60 // 16, 1.0, 0.0).astype(BF)
    loads[2].wait()
    embp[...] = dot(place, embed[...]).astype(BF)
    wait(hl, r_h.at[0])
    wait(hr, r_h.at[1])
    before = jnp.where(c == 0, -1, hl[...])
    after = jnp.where(c == NZ * NX - 1, -1, hr[...])
    line = jnp.concatenate([before, bases[...], after], axis=1)
    rolled = pltpu.roll(jnp.broadcast_to(line, (16, ROWS + 256)), 648, 1, stride=1, stride_axis=0)
    for j in range(4):
        e_ref[16 * j : 16 * j + 16, :] = jnp.where(rolled[:, :WIDE] == j, 1.0, 0.0).astype(BF)
    for i in range(WIDE // 128):
        block = e_ref[:, 128 * i : 128 * i + 128].astype(F32)
        et_ref[128 * i : 128 * i + 128, :] = block.T.astype(BF)
    fpad[0:8, :] = jnp.zeros((8, WIDTH), F32)
    fpad[EXT + 8 : EXT + 16, :] = jnp.zeros((8, WIDTH), F32)

    def embed_step(i):
        r0 = pl.multiple_of(i * 32, 32)
        values = dot(et_ref[pl.ds(r0, 32), :], embp[...]).astype(BF)
        first[pl.ds(r0, 32), :] = values
        values = values.astype(F32)
        factor = lax.rsqrt(jnp.mean(values * values, axis=1, keepdims=True) + EPSILON)
        normed = values * factor
        value, slope = gelu_both(normed)
        spot = lax.broadcasted_iota(jnp.int32, (32, WIDTH), 0) + (c * ROWS + r0 - OFF)
        inside = jnp.logical_and(spot >= 0, spot < ROWS * NZ * NX)
        value = jnp.where(inside, value, 0.0)
        fpad[pl.ds(r0 + 8, 32), :] = value.astype(BF).astype(F32)
        nm_ref[pl.ds(r0, 32), :] = normed
        gn_ref[pl.ds(r0, 32), :] = slope
        fac_ref[pl.ds(r0, 32), :] = jnp.broadcast_to(factor, (32, 128))

    def head_rows():
        for load in loads[3:]:
            load.wait()
        hmt[0:176, :] = head_h[0:176, :]
        last = jnp.concatenate([head_h[176:184, :].astype(F32), jnp.zeros((8, 1536), F32)], axis=0)
        hmt[176:192, :] = last.astype(BF)
        hmt[192:224, :] = head_m[...]
        hmt[224:256, :] = jnp.zeros((32, 1536), BF)
        human = (organism[0] == 0).astype(F32)
        cot[0:184, :] = cot_h[...].astype(F32) * human
        cot[184:192, :] = jnp.zeros((8, 128), F32)
        cot[192:224, :] = cot_m[...].astype(F32) * (1.0 - human)
        cot[224:256, :] = jnp.zeros((32, 128), F32)

    def head_turn(i):
        cols = pl.ds(pl.multiple_of(128 * i, 128), 128)
        hm[cols, :] = hmt[:, cols].astype(F32).T.astype(BF)

    def ring1_up(s):
        wait(blk1(s), r_w.at[2 + s])
        if s < 4:
            send(blk1(s), blk1(s), 10, r_w.at[3 + s], **to_z(1))
        spread1(s)

    def ring1_down(s):
        q = NZ - s
        wait(blk1(q), r_w.at[2 + q])
        if s < 3:
            send(blk1(q), blk1(q), 10, r_w.at[1 + q], **to_z(-1))
        spread1(q)

    def spread1(q):
        for i in range(1, NX):
            send(blk1(q), blk1(q), 8, r_w.at[10 + q], **to_x(i))

    def blk0(q, cols):
        return wg.at[zp(-q), :, :, cols]

    def chunk(low, h):
        return pl.ds(pl.multiple_of(low + 256 * h, 128), min(256, SPLIT - 256 * h))

    def ring0(s, h):
        for down in range(2):
            if s == 4 and down != 1 - h // 2:
                continue
            q = NZ - s if down else s
            part = blk0(q, chunk(mine, h))
            wait(part, r_w.at[34 + 8 * h + q])
            if s < 3 or (s == 3 and down == 1 - h // 2):
                step = -1 if down else 1
                send(part, part, 1, r_w.at[34 + 8 * h + q + step], **to_z(step))
            send(part, part, 2, r_w.at[26 + q], dp=sib)

    def pass_on(q):
        wait(wg.at[zp(-q), pl.ds(0, 3), :, c1], r_w.at[10 + q])
        if q:
            here = wg.at[zp(-q), :, :, c1]
            send(here, here, 10, r_w.at[18 + q], dp=sib)
        else:
            for i in range(1, NX):
                here = wg.at[z, xp(-i), :, c1]
                send(here, here, 10, r_w.at[18], dp=sib)

    def pack(q):
        if q:
            wait(wg.at[zp(-q), :, :, o1], r_w.at[18 + q])
            wait(wg.at[zp(-q), :, :, o0], r_w.at[26 + q])
        else:
            wait(wg.at[z, pl.ds(0, 3), :, o1], r_w.at[18])
            wait(wg.at[z, pl.ds(0, 3), :, o0], r_w.at[1])
        zz = zp(-q)

        def pack_step(i):
            pair = jnp.concatenate([wg[zz, 2 * i].astype(F32), wg[zz, 2 * i + 1].astype(F32)], axis=0)
            wf[pl.ds(pl.multiple_of(96 * zz + 48 * i, 16), 48), :] = pair.astype(BF)

        loop(2, pack_step)

    def embed_some(low, high):
        def body(i):
            embed_step(i + low)

        loop(high - low, body)

    def shift_step(i):
        r0 = pl.multiple_of(i * 32, 32)
        block = fpad[pl.ds(r0, 48), :]
        for t in range(SPAN):
            acols[t, pl.ds(r0, 32), :] = block[t + 6 : t + 38].astype(BF)

    ring1_up(1)
    ring1_down(1)
    wait(wg.at[z, pl.ds(0, 3), :, c0], r_w.at[0])
    for i in range(1, NX):
        here = wg.at[z, xp(-i), :, c0]
        send(here, here, 9, r_w.at[1], dp=sib)
    for h in range(4):
        part = blk0(0, chunk(mine, h))
        send(part, part, 1, r_w.at[34 + 8 * h + 1], **to_z(1))
        send(part, part, 1, r_w.at[34 + 8 * h + 7], **to_z(-1))
    embed_some(0, 4)
    ring1_up(2)
    ring1_down(2)
    embed_step(4)
    for s in range(1, 4):
        for h in range(4):
            ring0(s, h)
            embed_step(1 + 4 * s + h)
            if s == 1 and h == 1:
                ring1_up(3)
                ring1_down(3)
            if s == 2 and h == 1:
                ring1_up(4)
        if s == 2:
            pass_on(0)
        if s == 3:
            pass_on(1)
            pass_on(7)
    head_rows()
    loop(EXT // 32, shift_step)
    pass_on(2)
    pass_on(6)
    pack(0)
    for h in (0, 2, 1, 3):
        ring0(4, h)
        if h == 0:
            pack(1)
            pack(7)
    for q in (3, 5, 4):
        pass_on(q)
    loop(12, head_turn)
    for q in (2, 6, 3, 5, 4):
        pack(q)

    own_cols = pl.ds(pl.multiple_of((WIDTH // 2) * k, 128), WIDTH // 2)
    sib_cols = pl.ds(pl.multiple_of((WIDTH // 2) * (1 - k), 128), WIDTH // 2)
    local = []
    for t in range(SPAN):
        dst = ah.at[pl.ds(0, ROWS), pl.ds(384 * t, 384)]
        copy = pltpu.make_async_copy(acols.at[t, pl.ds(OFF, ROWS), own_cols], dst, s_o.at[t])
        copy.start()
        local.append(copy)
        send(
            acols.at[t, pl.ds(OFF, ROWS), sib_cols], ah.at[pl.ds(ROWS, ROWS), pl.ds(384 * t, 384)],
            2, r_d.at[4], dp=sib,
        )
    ah[:, pl.ds(HALF, 128)] = jnp.zeros((2 * ROWS, 128), BF)
    def conv_step(i):
        o0_ = pl.multiple_of(i * 256, 256)
        total = dot(acols[0], wf[pl.ds(o0_, 256), 0:WIDTH], 1, 1)
        for t in range(1, SPAN):
            total = total + dot(acols[t], wf[pl.ds(o0_, 256), WIDTH * t : WIDTH * (t + 1)], 1, 1)
        mixed[:, pl.ds(o0_, 256)] = total

    loop(3, conv_step)

    pooled = []
    for t in range(4):
        def pool_step(i, total):
            r0 = pl.multiple_of(OFF + 128 * t + 32 * i, 16)
            part = first[pl.ds(r0, 32), :].astype(F32) + gelu_value(mixed[pl.ds(r0, 32), :])
            return total + part.reshape(4, 8, WIDTH).sum(axis=0)

        total = lax.fori_loop(0, 4, pool_step, jnp.zeros((8, WIDTH), F32))
        row = jnp.sum(total, axis=0, keepdims=True) / 128.0
        pooled.append(row)

    pieces = [row[:, 256 * m : 256 * m + 256] for m in range(3) for row in pooled]
    pbuf[z, x] = jnp.concatenate(pieces + [jnp.zeros((4, 256), F32)], axis=0).astype(BF)
    near = (1, 7, 2, 6, 3, 5, 4)
    far = (4, 3, 5, 2, 6, 1, 7, 0)

    def relay_gather(buf, group, rs, between=None):
        own = buf.at[z, x]
        for q in near:
            send(own, own, group, rs.at[q], **to_z(q))
        for i in range(1, NX):
            send(own, own, group, rs.at[0], **to_x(i))
        if between is not None:
            between()
        for q in near:
            here = buf.at[zp(-q), x]
            wait(here, rs.at[q])
            for i in range(1, NX):
                send(here, here, group, rs.at[0], **to_x(i))

    def relay_finish(buf, rs):
        wait(buf.at[:, pl.ds(0, 3)], rs.at[0])

    def scatter_start(src, got, group, rs):
        for q in far:
            for i in range(1, NX):
                send(src.at[zp(q), xp(i)], got.at[i, q], group, rs.at[q], **to_x(i))

    def scatter_turn(src, got, zsrc, zgot, group, rs):
        for q in far:
            total = src[zp(q), x].astype(F32)
            wait(got.at[pl.ds(1, 3), q], rs.at[q])
            for i in range(1, NX):
                total = total + got[i, q].astype(F32)
            if q:
                zsrc[q] = total.astype(BF)
                send(zsrc.at[q], zgot.at[q], group, rs.at[NZ], **to_z(q))
        return total

    def scatter_finish(total, zgot, rs):
        wait(zgot.at[pl.ds(1, 7)], rs.at[NZ])
        for q in near:
            total = total + zgot[q].astype(F32)
        return total

    relay_gather(pbuf, 3, r_p)

    def slope_step(i):
        r0 = pl.multiple_of(i * 32, 32)
        mixed[pl.ds(r0, 32), :] = gelu_slope(mixed[pl.ds(r0, 32), :])

    loop(EXT // 32, slope_step)
    for t in range(SPAN):
        dw2[48 * t : 48 * t + 48, :] = dw[:, WIDTH * t : WIDTH * (t + 1)]
    zero8 = jnp.zeros((8, WIDTH), F32)
    dn_ref[0:8, :] = zero8
    dn_ref[136:144, :] = zero8
    dpad[0:8, :] = zero8
    dpad[136:144, :] = zero8
    dbp[0:8, :] = zero8
    dbp[136:144, :] = zero8
    df_ref[...] = jnp.ones((144, 128), F32)
    relay_finish(pbuf, r_p)

    def coarse_step(i):
        zz, half = i // 2, 2 * (i % 2)
        v0, v1 = pbuf[zz, half].astype(F32), pbuf[zz, half + 1].astype(F32)
        parts = [jnp.concatenate([v0[4 * m : 4 * m + 4], v1[4 * m : 4 * m + 4]], axis=0) for m in range(3)]
        values = jnp.concatenate(parts, axis=1)
        factor = lax.rsqrt(jnp.mean(values * values, axis=1, keepdims=True) + EPSILON)
        normed = values * factor
        r0 = pl.multiple_of(8 * i + 8, 8)
        dn_ref[pl.ds(r0, 8), :] = normed
        df_ref[pl.ds(r0, 8), :] = jnp.broadcast_to(factor, (8, 128))
        dpad[pl.ds(r0, 8), :] = gelu_value(normed).astype(BF).astype(F32)

    loop(16, coarse_step, unroll=4)
    block = dpad[...]
    for t in range(SPAN):
        dcols[t] = block[t + 6 : t + 134].astype(BF)
    total = dot(dw[:, 0:WIDTH], dcols[0], 1, 1)
    for t in range(1, SPAN):
        total = total + dot(dw[:, WIDTH * t : WIDTH * (t + 1)], dcols[t], 1, 1)
    ft[z, x] = total.astype(BF)
    dax[pl.ds(pl.multiple_of(d * 128, 128), 128), :] = dcols[2]

    def dp_slot(ref, i, size):
        return ref.at[pl.ds(pl.multiple_of(i * size, 16), size)]

    def coarse_background():
        for i in range(1, ND):
            send(dcols.at[2], dp_slot(dax, d, 128), 8, r_d.at[0], dp=dpp(i))

    relay_gather(ft, 4, r_f, coarse_background)
    relay_finish(ft, r_f)

    feats = ft[...].reshape(1536, 128)
    logit = dot(hmt[...], feats)
    delta = (cot[...] * jax.nn.sigmoid(logit)).astype(BF)
    dtx[d] = delta
    fbs[...] = dot(hm[...], delta).astype(BF).reshape(NZ, NX, 48, 128)
    scatter_start(fbs, fxr, 5, r_rf)
    for i in range(1, ND):
        send(dtx.at[d], dtx.at[d], 4, r_d.at[1], dp=dpp(i))
        send(ft.at[dpp(i)], fxs.at[d], 4, r_d.at[2], dp=dpp(i))
    fxs[d] = ft[d]

    own_part = scatter_turn(fbs, fxr, fzs, fzr, 5, r_rf)
    fdelta = scatter_finish(own_part, fzr, r_rf).astype(BF)
    fdx[d] = fdelta

    lanes = lax.broadcasted_iota(jnp.int32, (48, 128), 1)

    def shifted(values):
        wide = values.astype(F32)
        parts = []
        for t in range(SPAN):
            move = t - 2
            if move == 0:
                parts.append(wide)
                continue
            turned = pltpu.roll(wide, move % 128, 1)
            keep = lanes >= move if move > 0 else lanes < 128 + move
            parts.append(jnp.where(keep, turned, 0.0))
        return jnp.concatenate(parts, axis=0).astype(BF)

    back = dot(shifted(fdelta), dw2[...], 0, 0)
    dbp[8:136, :] = back

    def piece_step(i):
        block = dbp[pl.ds(pl.multiple_of(8 * i, 8), 24), :]
        zz, half = i // 2, 2 * (i % 2)
        for j, low in ((0, 6), (1, 10)):
            rows = block[low : low + 8]
            dbs[zz, half + j] = jnp.concatenate([rows[:, :384], rows[:, 384:]], axis=0).astype(BF)

    loop(16, piece_step, unroll=4)
    scatter_start(dbs, dxr, 5, r_rd)
    for i in range(1, ND):
        send(fdx.at[d], fdx.at[d], 4, r_d.at[3], dp=dpp(i))
    own_part = scatter_turn(dbs, dxr, dzs, dzr, 5, r_rd)

    wait(dtx.at[pl.ds(0, 7)], r_d.at[1])
    wait(fxs.at[pl.ds(0, 7)], r_d.at[2])
    total = jnp.zeros((256, 192), F32)
    for i in range(ND):
        total = total + dot(dtx[i], fxs[i].reshape(192, 128), 1, 1)
    o_gh[...] = total[:184]
    o_gm[...] = total[192:224]
    store(o_gh, q_gh)
    store(o_gm, q_gm)

    deep_back = scatter_finish(own_part, dzr, r_rd)
    deep_back = jnp.concatenate([deep_back[:8], deep_back[8:]], axis=1)
    r0 = pl.multiple_of(8 * (c // 2), 8)

    def own_rows(ref):
        block = ref[pl.ds(r0, 24), :]
        return jnp.where(c % 2 == 0, block[6:14], block[10:18])

    dnormed = own_rows(dn_ref)
    dfactor = own_rows(df_ref)[:, :1]
    v = deep_back * gelu_slope(dnormed)
    pd_ref[...] = dfactor * (v - dnormed * jnp.mean(v * dnormed, axis=1, keepdims=True)) / 128.0

    fdp[0:8, :] = zero8
    fdp[EXT + 8 : EXT + 16, :] = zero8

    def fine_step(i):
        r0 = pl.multiple_of(i * 16, 16)
        row = pd_ref[pl.ds((r0 + 112) // 128 + 1, 1), :]
        fine = (mixed[pl.ds(r0, 16), :] * row).astype(BF).astype(F32)
        fdp[pl.ds(r0 + 8, 16), :] = fine

    for i in range(4):
        def fine_block(n, i=i):
            fine_step(n + 8 * i + 1)

        loop(8, fine_block, unroll=4)
        block = fdp[OFF + 8 + 128 * i : OFF + 136 + 128 * i, :]
        fdt[0, :, 128 * i : 128 * i + 128] = block.T.astype(BF)
        part = fdt.at[:, :, pl.ds(128 * i, 128)]
        send(part.at[0], part.at[1], 6, r_g.at[0], dp=sib)
    fine_step(0)
    fine_step(EXT // 16 - 1)

    def back_shift(i):
        r0 = pl.multiple_of(i * 32, 32)
        block = fdp[pl.ds(r0, 48), :]
        for t in range(SPAN):
            fdc[t, pl.ds(r0, 32), :] = block[10 - t : 42 - t].astype(BF)

    loop(EXT // 32, back_shift)
    for copy in local:
        copy.wait()
    wait(ah.at[pl.ds(ROWS, ROWS), pl.ds(0, HALF)], r_d.at[4])
    wait(fdt.at[1], r_g.at[0])

    def grad_chunk(low):
        cols = pl.ds(pl.multiple_of(low, 256), 256)
        return dot(fdt[0], ah[pl.ds(0, ROWS), cols]) + dot(fdt[1], ah[pl.ds(ROWS, ROWS), cols])

    def by_x(total, xx):
        return jnp.concatenate(
            [total[24 * (4 * zz + xx) : 24 * (4 * zz + xx) + 24] for zz in range(NZ)], axis=0
        ).astype(BF)

    halves = (pl.ds(0, 144), pl.ds(144, 48))
    pairs = (range(3), range(3, 4))

    def alpha_send(i, h):
        send(
            ga.at[yp(i), :, halves[h]], gar.at[i, :, halves[h]],
            6, r_g.at[1 + h], dp=2 * yp(i) + k,
        )

    def beta_send(yy, i, h):
        send(
            gb.at[xp(i), yy, halves[h]], gbr.at[i, yy, halves[h]],
            6, r_g.at[3 + h], **to_x(i),
        )

    for n in range(NY):
        total = grad_chunk(512 * n + 256)
        for xx in range(NX):
            gb[xx, n] = by_x(total, xx)
        for i in range(1, NX):
            beta_send(n, i, 0)
        yy = yp(n + 1)
        total = grad_chunk(512 * yy)
        for xx in range(NX):
            ga[yy, xx] = by_x(total, xx)
        if n < NY - 1:
            alpha_send(n + 1, 0)
    for n in range(NY):
        for i in range(1, NX):
            beta_send(n, i, 1)
        if n < NY - 1:
            alpha_send(n + 1, 1)

    def second_phase(h):
        wait(gar.at[pl.ds(1, 3), :, halves[h]], r_g.at[1 + h])
        for xx in range(NX):
            for m in pairs[h]:
                rows = pl.ds(48 * m, 48)
                total = ga[y, xx, rows, :].astype(F32)
                for i in range(1, NY):
                    total = total + gar[i, xx, rows, :].astype(F32)
                ha[xx, rows, :] = total.astype(BF)
        for i in range(1, NX):
            send(ha.at[xp(i), halves[h]], har.at[i, halves[h]], 7, r_g.at[5 + h], **to_x(i))
        wait(gbr.at[pl.ds(1, 3), :, halves[h]], r_g.at[3 + h])
        for yy in range(NY):
            for m in pairs[h]:
                rows = pl.ds(48 * m, 48)
                total = gb[x, yy, rows, :].astype(F32)
                for i in range(1, NX):
                    total = total + gbr[i, yy, rows, :].astype(F32)
                hb[yy, rows, :] = total.astype(BF)
        for i in range(1, NY):
            send(
                hb.at[yp(i), halves[h]], hbr.at[i, halves[h]],
                7, r_g.at[7 + h], dp=2 * yp(i) + k,
            )

    def third_copy(zz):
        return pltpu.make_async_remote_copy(
            src_ref=zs.at[zz], dst_ref=zr.at[z], send_sem=s_all.at[7], recv_sem=r_g.at[9],
            device_id={"context": zz * NX + x}, device_id_type=MESH,
        )

    def third_phase(h):
        wait(har.at[pl.ds(1, 3), halves[h]], r_g.at[5 + h])
        wait(hbr.at[pl.ds(1, 3), halves[h]], r_g.at[7 + h])
        for m in pairs[h]:
            rows = pl.ds(48 * m, 48)
            left_half = ha[x, rows, :].astype(F32)
            right_half = hb[y, rows, :].astype(F32)
            for i in range(1, 4):
                left_half = left_half + har[i, rows, :].astype(F32)
                right_half = right_half + hbr[i, rows, :].astype(F32)
            zz = 2 * m
            zs[zz] = jnp.concatenate([left_half[:24], right_half[:24]], axis=0).astype(BF)
            zs[zz + 1] = jnp.concatenate([left_half[24:], right_half[24:]], axis=0).astype(BF)
            for to in (zz, zz + 1):

                @pl.when(z != to)
                def _(to=to):
                    third_copy(to).start()

    def back_step(i):
        cols = 256 * i
        total = dot(fdc[0], wf[:, cols : cols + 256])
        for t in range(1, SPAN):
            total = total + dot(fdc[t], wf[:, WIDTH * t + cols : WIDTH * t + cols + 256])
        fdp[0:EXT, cols : cols + 256] = total

    for i in range(3):
        back_step(i)

    fhl[0, EXT:WIDE, :] = jnp.zeros((WIDE - EXT, WIDTH), BF)
    fhl[1, EXT:WIDE, :] = jnp.zeros((WIDE - EXT, WIDTH), BF)

    def delta_step(i):
        r0 = pl.multiple_of(i * 16, 16)
        row = pd_ref[pl.ds((r0 + 112) // 128 + 1, 1), :]
        normed = nm_ref[pl.ds(r0, 16), :]
        w = fdp[pl.ds(r0, 16), :] * gn_ref[pl.ds(r0, 16), :]
        factor = fac_ref[pl.ds(r0, 16), :][:, :1]
        value = row + factor * (w - normed * jnp.mean(w * normed, axis=1, keepdims=True))
        value = jnp.where(jnp.logical_and(r0 >= OFF, r0 < OFF + ROWS), value, 0.0)
        fdl[pl.ds(r0, 16), :] = value
        high = value.astype(BF)
        fhl[0, pl.ds(r0, 16), :] = high
        fhl[1, pl.ds(r0, 16), :] = (value - high.astype(F32)).astype(BF)

    loop(EXT // 16, delta_step, unroll=2)
    out_copy = pltpu.make_async_copy(fdl.at[pl.ds(OFF, ROWS)], o_fd, s_o.at[5])
    out_copy.start()
    ep[...] = (dot(e_ref[...], fhl[0]) + dot(e_ref[...], fhl[1])).reshape(NZ, 8, WIDTH)
    for q in far[:7]:
        part = ep[zp(q)]
        es[q] = jnp.concatenate([part[:, :384], part[:, 384:]], axis=0).astype(BF)
        send(es.at[q], er.at[q], 7, r_e.at[0], **to_z(q))

    second_phase(0)

    wait(dax.at[pl.ds(0, 896)], r_d.at[0])
    wait(fdx.at[pl.ds(0, 7)], r_d.at[3])
    for i in range(ND):
        fkx[:, 128 * i : 128 * i + 128] = shifted(fdx[i])
    deep_total = dot(fkx[...], dax[...])
    for t in range(SPAN):
        o_gd[:, WIDTH * t : WIDTH * (t + 1)] = deep_total[48 * t : 48 * t + 48]
    store(o_gd, q_gd)

    wait(er.at[pl.ds(1, 7)], r_e.at[0])
    total = er[1].astype(F32)
    for q in near[1:]:
        total = total + er[q].astype(F32)
    ex[x] = ep[z] + jnp.concatenate([total[:8], total[8:]], axis=1)
    for i in range(1, NX):
        send(ex.at[x], ex.at[x], 7, r_e.at[1], **to_x(i))
    second_phase(1)
    third_phase(0)
    wait(ex.at[pl.ds(0, 3)], r_e.at[1])
    ey[d] = (ex[0] + ex[1]) + (ex[2] + ex[3])
    for i in range(1, ND):
        send(ey.at[d], ey.at[d], 7, r_e.at[2], dp=dpp(i))
    third_phase(1)
    wait(ey.at[pl.ds(0, 7)], r_e.at[2])
    total = ey[0]
    for i in range(1, ND):
        total = total + ey[i]
    eg[z] = jnp.concatenate([total[:, :384], total[:, 384:]], axis=0).astype(BF)
    for i in range(1, NZ):
        send(eg.at[z], eg.at[z], 7, r_e.at[3], **to_z(i))

    total = zs[z].astype(F32)
    wait(zr.at[pl.ds(0, 7)], r_g.at[9])
    for i in range(1, NZ):
        total = total + zr[zp(i)].astype(F32)
    fin[d] = total.astype(BF)
    for i in range(1, NZ):
        count(7, zs.at[i])
    for i in range(1, ND):
        send(fin.at[d], fin.at[d], 7, r_g.at[10], dp=dpp(i))
    wait(eg.at[pl.ds(0, 7)], r_e.at[3])
    blocks = []
    for i in range(NZ):
        block = eg[i].astype(F32)
        blocks.append(jnp.concatenate([block[:8], block[8:]], axis=1))
    for t in range(15):
        for j in range(4):
            row = (15 - t) % 8
            o_ge[4 * t + j : 4 * t + j + 1, :] = blocks[2 * j + (15 - t) // 8][row : row + 1, :]
    store(o_ge, q_ge)
    wait(fin.at[pl.ds(0, 7)], r_g.at[10])
    for i in range(ND):
        for t in range(4):
            tile = 4 * (i // 2) + t
            if tile >= 15:
                continue
            column = 128 * (6 * (tile // 3) + 3 * (i % 2) + tile % 3)
            part = fin[i, 24 * (t // 2) : 24 * (t // 2) + 24, 128 * (t % 2) : 128 * (t % 2) + 128]
            o_gc[:, column : column + 128] = part.astype(F32)
    store(o_gc, q_gc)

    out_copy.wait()
    for out in stores:
        out.wait()
    both = bases.at[:, pl.ds(0, 256)]
    pltpu.make_async_copy(both, both, s_all.at[0]).wait()
    for group in range(1, 11):
        wait_sends(group)


def place(*refs):
    count = 6
    held, sems = refs[2 * count : 3 * count], refs[-1]
    pieces = []
    for i, size in ((5, 128), (2, 24), (1, 24), (0, 60), (3, 184), (4, 32)):
        for low in range(0, held[i].shape[0], size):
            pieces.append((i, pl.ds(low, size)))
    loads, stores = [], []
    for n, (i, rows) in enumerate(pieces):
        loads.append(pltpu.make_async_copy(refs[i].at[rows], held[i].at[rows], sems.at[0, n]))
        stores.append(pltpu.make_async_copy(held[i].at[rows], refs[count + i].at[rows], sems.at[1, n]))
    for load in loads:
        load.start()
    for load, out in zip(loads, stores):
        load.wait()
        out.start()
    for out in stores:
        out.wait()


def shards(bases, organism, embed_weight, conv_weight, deep_weight, human_head, mouse_head, human_cotangent, mouse_cotangent):
    vmem, dma = pltpu.VMEM, pltpu.SemaphoreType.DMA
    scratch = [
        vmem((1, ROWS), jnp.int32), vmem((60, WIDTH), BF), vmem((48, 3840), BF), vmem((184, 1536), BF),
        vmem((32, 1536), BF), vmem((184, 128), BF), vmem((32, 128), BF),
        vmem((60, WIDTH), F32), vmem((24, 3840), F32), vmem((48, 3840), F32), vmem((184, 192), F32), vmem((32, 192), F32),
        vmem((1536, 256), BF), vmem((256, 1536), BF), vmem((256, 128), F32),
        vmem((1, 128), jnp.int32), vmem((1, 128), jnp.int32),
        vmem((64, WIDE), BF), vmem((WIDE, 64), BF), vmem((64, WIDTH), BF),
        vmem((EXT + 16, WIDTH), F32), vmem((EXT, WIDTH), BF), vmem((EXT, WIDTH), F32),
        vmem((EXT, WIDTH), F32), vmem((EXT, 128), F32), vmem((SPAN, EXT, WIDTH), BF),
        vmem((NZ, NX, 24, 3840), BF), vmem((WIDTH, 3840), BF), vmem((EXT, WIDTH), F32),
        vmem((2 * ROWS, 2048), BF),
        vmem((NZ, NX, 16, 256), BF), vmem((144, WIDTH), F32), vmem((144, WIDTH), F32), vmem((144, 128), F32),
        vmem((SPAN, 128, WIDTH), BF), vmem((NZ, NX, 48, 128), BF),
        vmem((ND, 256, 128), BF), vmem((ND, 4, 48, 128), BF),
        vmem((NZ, NX, 48, 128), BF), vmem((4, NZ, 48, 128), BF), vmem((NZ, 48, 128), BF), vmem((NZ, 48, 128), BF),
        vmem((ND, 48, 128), BF), vmem((240, 1024), BF), vmem((240, WIDTH), BF), vmem((144, WIDTH), F32),
        vmem((NZ, NX, 16, 384), BF), vmem((4, NZ, 16, 384), BF), vmem((NZ, 16, 384), BF), vmem((NZ, 16, 384), BF),
        vmem((1024, WIDTH), BF), vmem((8, WIDTH), F32),
        vmem((EXT + 16, WIDTH), F32), vmem((SPAN, EXT, WIDTH), BF), vmem((2, WIDTH, ROWS), BF),
        vmem((NY, NX, 192, 256), BF), vmem((NX, NY, 192, 256), BF),
        vmem((4, NX, 192, 256), BF), vmem((4, NY, 192, 256), BF),
        vmem((NX, 192, 256), BF), vmem((NY, 192, 256), BF), vmem((4, 192, 256), BF), vmem((4, 192, 256), BF),
        vmem((NZ, 48, 256), BF), vmem((NZ, 48, 256), BF), vmem((ND, 48, 256), BF),
        vmem((EXT, WIDTH), F32), vmem((2, WIDE, WIDTH), BF),
        vmem((NZ, 8, WIDTH), F32), vmem((NZ, 16, 384), BF), vmem((NZ, 16, 384), BF), vmem((NX, 8, WIDTH), F32),
        vmem((ND, 8, WIDTH), F32), vmem((NZ, 16, 384), BF),
        dma((11,)), dma((2,)), dma((66,)), dma((8,)), dma((8,)), dma((9,)), dma((9,)), dma((5,)), dma((11,)), dma((4,)),
        dma((6,)), dma((13,)),
    ]
    spec = pl.BlockSpec(memory_space=pl.ANY)
    ge, gc, gd, gh, gm, fd = pl.pallas_call(
        kernel,
        out_shape=(
            jax.ShapeDtypeStruct((60, WIDTH), F32),
            jax.ShapeDtypeStruct((24, 3840), F32),
            jax.ShapeDtypeStruct((48, 3840), F32),
            jax.ShapeDtypeStruct((184, 192), F32),
            jax.ShapeDtypeStruct((32, 192), F32),
            jax.ShapeDtypeStruct((ROWS, WIDTH), F32),
        ),
        in_specs=[spec, pl.BlockSpec(memory_space=pltpu.SMEM)] + [spec] * 7,
        out_specs=(spec,) * 6,
        scratch_shapes=scratch,
        compiler_params=pltpu.CompilerParams(
            collective_id=0, has_side_effects=True, vmem_limit_bytes=60 * 1024 * 1024
        ),
        cost_estimate=pl.CostEstimate(flops=10_000_000_000, bytes_accessed=8_000_000, transcendentals=2_000_000),
    )(
        bases, organism, embed_weight, conv_weight, deep_weight,
        human_head.T, mouse_head.T, human_cotangent[0].T, mouse_cotangent[0].T,
    )
    results = (ge, gc, gd, gh, gm, fd)
    ge, gc, gd, gh, gm, fd = pl.pallas_call(
        place,
        out_shape=tuple(jax.ShapeDtypeStruct(a.shape, a.dtype) for a in results),
        in_specs=[spec] * 6,
        out_specs=(spec,) * 6,
        scratch_shapes=[vmem(a.shape, a.dtype) for a in results] + [dma((2, 10))],
        compiler_params=pltpu.CompilerParams(vmem_limit_bytes=60 * 1024 * 1024),
    )(*results)
    return ge, gc, gd, gh.T, gm.T, fd[None]


def solution(mesh):
    return jax.shard_map(
        shards,
        mesh=mesh,
        in_specs=(
            P("dp", "context"),
            P("dp"),
            P(),
            P("context", None),
            P("context", None),
            P(None, "context"),
            P(None, "context"),
            P("dp", None, "context"),
            P("dp", None, "context"),
        ),
        out_specs=(
            P(),
            P("context", None),
            P("context", None),
            P("dp", "context"),
            P("dp", "context"),
            P("dp", "context", None),
        ),
        check_vma=False,
    )
```

```python
import jax
import jax.numpy as jnp
from jax import lax
from jax.experimental import pallas as pl
from jax.experimental.pallas import tpu as pltpu
from jax.sharding import PartitionSpec as P

F32 = jnp.float32
BF = jnp.bfloat16
MESH = pl.DeviceIdType.MESH

WIDTH = 768
SPAN = 5
NZ, NX, NY = 8, 4, 4
ND = 8
ROWS = 512
OFF = 16
EXT = ROWS + 2 * OFF
WIDE = 640
HALF = 1920
SPLIT = 896

SLOPE = 0.7978845608028654
CUBIC = 0.044715
EPSILON = 1e-06


def gelu_both(value):
    square = value * value
    tangent = jnp.tanh(SLOPE * (value + CUBIC * square * value))
    half = 0.5 * (1.0 + tangent)
    slope = half + 0.5 * value * (1.0 - tangent * tangent) * SLOPE * (1.0 + 3.0 * CUBIC * square)
    return value * half, slope


def gelu_value(value):
    return 0.5 * value * (1.0 + jnp.tanh(SLOPE * (value + CUBIC * value * value * value)))


def gelu_slope(value):
    return gelu_both(value)[1]


def dot(a, b, ca=1, cb=0):
    return lax.dot_general(a, b, (((ca,), (cb,)), ((), ())), preferred_element_type=F32)


def loop(count, body, unroll=1):
    def step(i, carry):
        body(i)
        return carry

    lax.fori_loop(0, count, step, 0, unroll=unroll)


def kernel(
    i_bases, organism, i_embed, i_cw, i_dw, i_head_h, i_head_m, i_cot_h, i_cot_m,
    q_ge, q_gc, q_gd, q_gh, q_gm, o_fd,
    bases, embed, dw, head_h, head_m, cot_h, cot_m, o_ge, o_gc, o_gd, o_gh, o_gm,
    hm, hmt, cot, hl, hr, e_ref, et_ref, embp, fpad, first, nm_ref, gn_ref, fac_ref, acols, wg, wf, mixed, ah,
    pbuf, dn_ref, dpad, df_ref, dcols, ft, dtx, fxs, fbs, fxr, fzs, fzr, fdx, fkx, dw2, dbp, dbs, dxr, dzs, dzr,
    dax, pd_ref, fdp, fdc, fdt,
    ga, gb, gar, gbr, ha, hb, har, hbr, zs, zr, fin,
    fdl, fhl, ep, es, er, ex, ey, eg,
    s_all, r_h, r_w, r_p, r_f, r_rf, r_rd, r_d, r_g, r_e, s_o, s_i,
):
    c = lax.axis_index("context")
    d = lax.axis_index("dp")
    z, x = c // NX, c % NX
    y, k = d // 2, d % 2

    def zp(i):
        return lax.rem(z + i + NZ, NZ)

    def xp(i):
        return lax.rem(x + i + NX, NX)

    def dpp(i):
        return lax.rem(d + i + ND, ND)

    def yp(i):
        return lax.rem(y + i + NY, NY)

    sent = [0] * 11

    def count(group, ref):
        size = ref.dtype.itemsize
        for n in ref.shape:
            size *= n
        sent[group] += size

    def send(src, dst, group, rs, **to):
        pltpu.make_async_remote_copy(
            src_ref=src, dst_ref=dst, send_sem=s_all.at[group], recv_sem=rs, device_id=to, device_id_type=MESH
        ).start()
        count(group, src)

    def wait(dst, rs):
        pltpu.make_async_remote_copy(
            src_ref=dst, dst_ref=dst, send_sem=rs, recv_sem=rs, device_id={"context": zp(1) * NX + x}, device_id_type=MESH
        ).wait_recv()

    def wait_sends(group):
        cells = sent[group] // 2
        parts = []
        for r in range(768, 0, -16):
            if cells % (r * 128) == 0 and cells // r <= 3840:
                parts.append(wf.at[pl.ds(0, r), pl.ds(0, cells // r)])
        for a in range(1, NZ + 1):
            for b in range(1, NX + 1):
                if cells % (a * b * 24 * 128) == 0 and cells // (a * b * 24) <= 3840:
                    parts.append(wg.at[pl.ds(0, a), pl.ds(0, b), :, pl.ds(0, cells // (a * b * 24))])
        pltpu.make_async_copy(parts[0], parts[0], s_all.at[group]).wait()

    barrier = pltpu.get_barrier_semaphore()
    for i in range(1, NZ):
        pl.semaphore_signal(barrier, inc=1, device_id={"context": zp(i) * NX + x}, device_id_type=MESH)
    for i in range(1, NX):
        pl.semaphore_signal(barrier, inc=1, device_id={"context": z * NX + xp(i)}, device_id_type=MESH)
    for i in range(1, ND):
        pl.semaphore_signal(barrier, inc=1, device_id={"dp": dpp(i)}, device_id_type=MESH)
    right, left = lax.rem(c + 1, NZ * NX), lax.rem(c + NZ * NX - 1, NZ * NX)
    pl.semaphore_signal(barrier, inc=1, device_id={"context": right}, device_id_type=MESH)
    pl.semaphore_signal(barrier, inc=1, device_id={"context": left}, device_id_type=MESH)
    loads = []
    for i, (src, dst) in enumerate(
        (
            (i_cw, wg.at[z, x]), (i_bases, bases), (i_embed, embed), (i_head_h, head_h),
            (i_head_m, head_m), (i_cot_h, cot_h), (i_cot_m, cot_m), (i_dw, dw),
        )
    ):
        load = pltpu.make_async_copy(src, dst, s_i.at[i])
        load.start()
        loads.append(load)
    stores = []

    def store(src, dst):
        out = pltpu.make_async_copy(src, dst, s_i.at[8 + len(stores)])
        out.start()
        stores.append(out)

    loads[0].wait()
    loads[1].wait()
    pl.semaphore_wait(barrier, NZ - 1 + NX - 1 + ND - 1 + 2)

    mine = pl.multiple_of(HALF * k, 128)
    other = pl.multiple_of(HALF * (1 - k), 128)
    c0 = pl.ds(mine, SPLIT)
    c1 = pl.ds(pl.multiple_of(mine + SPLIT, 128), HALF - SPLIT)
    o0 = pl.ds(other, SPLIT)
    o1 = pl.ds(pl.multiple_of(other + SPLIT, 128), HALF - SPLIT)
    sib = 2 * y + 1 - k

    def blk1(q):
        return wg.at[zp(-q), x, :, c1]

    def to_z(i):
        return dict(context=zp(i) * NX + x)

    def to_x(i):
        return dict(context=z * NX + xp(i))

    send(bases.at[:, pl.ds(ROWS - 128, 128)], hl, 0, r_h.at[0], context=right)
    send(bases.at[:, pl.ds(0, 128)], hr, 0, r_h.at[1], context=left)
    for i in range(1, NX):
        send(wg.at[z, x, :, c0], wg.at[z, x, :, c0], 9, r_w.at[0], **to_x(i))
    send(blk1(0), blk1(0), 10, r_w.at[3], **to_z(1))
    send(blk1(0), blk1(0), 10, r_w.at[9], **to_z(-1))
    for i in range(1, NX):
        send(blk1(0), blk1(0), 8, r_w.at[10], **to_x(i))

    rows60 = lax.broadcasted_iota(jnp.int32, (64, 60), 0)
    cols60 = lax.broadcasted_iota(jnp.int32, (64, 60), 1)
    place = jnp.where(cols60 == 4 * (15 - rows60 % 16) + rows60 // 16, 1.0, 0.0).astype(BF)
    loads[2].wait()
    embp[...] = dot(place, embed[...]).astype(BF)
    wait(hl, r_h.at[0])
    wait(hr, r_h.at[1])
    before = jnp.where(c == 0, -1, hl[...])
    after = jnp.where(c == NZ * NX - 1, -1, hr[...])
    line = jnp.concatenate([before, bases[...], after], axis=1)
    rolled = pltpu.roll(jnp.broadcast_to(line, (16, ROWS + 256)), 648, 1, stride=1, stride_axis=0)
    for j in range(4):
        e_ref[16 * j : 16 * j + 16, :] = jnp.where(rolled[:, :WIDE] == j, 1.0, 0.0).astype(BF)
    for i in range(WIDE // 128):
        block = e_ref[:, 128 * i : 128 * i + 128].astype(F32)
        et_ref[128 * i : 128 * i + 128, :] = block.T.astype(BF)
    fpad[0:8, :] = jnp.zeros((8, WIDTH), F32)
    fpad[EXT + 8 : EXT + 16, :] = jnp.zeros((8, WIDTH), F32)

    def embed_step(i):
        r0 = pl.multiple_of(i * 32, 32)
        values = dot(et_ref[pl.ds(r0, 32), :], embp[...]).astype(BF)
        first[pl.ds(r0, 32), :] = values
        values = values.astype(F32)
        factor = lax.rsqrt(jnp.mean(values * values, axis=1, keepdims=True) + EPSILON)
        normed = values * factor
        value, slope = gelu_both(normed)
        spot = lax.broadcasted_iota(jnp.int32, (32, WIDTH), 0) + (c * ROWS + r0 - OFF)
        inside = jnp.logical_and(spot >= 0, spot < ROWS * NZ * NX)
        value = jnp.where(inside, value, 0.0)
        fpad[pl.ds(r0 + 8, 32), :] = value.astype(BF).astype(F32)
        nm_ref[pl.ds(r0, 32), :] = normed
        gn_ref[pl.ds(r0, 32), :] = slope
        fac_ref[pl.ds(r0, 32), :] = jnp.broadcast_to(factor, (32, 128))

    def head_rows():
        for load in loads[3:]:
            load.wait()
        hmt[0:176, :] = head_h[0:176, :]
        last = jnp.concatenate([head_h[176:184, :].astype(F32), jnp.zeros((8, 1536), F32)], axis=0)
        hmt[176:192, :] = last.astype(BF)
        hmt[192:224, :] = head_m[...]
        hmt[224:256, :] = jnp.zeros((32, 1536), BF)
        human = (organism[0] == 0).astype(F32)
        cot[0:184, :] = cot_h[...].astype(F32) * human
        cot[184:192, :] = jnp.zeros((8, 128), F32)
        cot[192:224, :] = cot_m[...].astype(F32) * (1.0 - human)
        cot[224:256, :] = jnp.zeros((32, 128), F32)

    def head_turn(i):
        cols = pl.ds(pl.multiple_of(128 * i, 128), 128)
        hm[cols, :] = hmt[:, cols].astype(F32).T.astype(BF)

    def ring1_up(s):
        wait(blk1(s), r_w.at[2 + s])
        if s < 4:
            send(blk1(s), blk1(s), 10, r_w.at[3 + s], **to_z(1))
        spread1(s)

    def ring1_down(s):
        q = NZ - s
        wait(blk1(q), r_w.at[2 + q])
        if s < 3:
            send(blk1(q), blk1(q), 10, r_w.at[1 + q], **to_z(-1))
        spread1(q)

    def spread1(q):
        for i in range(1, NX):
            send(blk1(q), blk1(q), 8, r_w.at[10 + q], **to_x(i))

    def blk0(q, cols):
        return wg.at[zp(-q), :, :, cols]

    def chunk(low, h):
        return pl.ds(pl.multiple_of(low + 256 * h, 128), min(256, SPLIT - 256 * h))

    def ring0(s, h):
        for down in range(2):
            if s == 4 and down != 1 - h // 2:
                continue
            q = NZ - s if down else s
            part = blk0(q, chunk(mine, h))
            wait(part, r_w.at[34 + 8 * h + q])
            if s < 3 or (s == 3 and down == 1 - h // 2):
                step = -1 if down else 1
                send(part, part, 1, r_w.at[34 + 8 * h + q + step], **to_z(step))
            send(part, part, 2, r_w.at[26 + q], dp=sib)

    def pass_on(q):
        wait(wg.at[zp(-q), pl.ds(0, 3), :, c1], r_w.at[10 + q])
        if q:
            here = wg.at[zp(-q), :, :, c1]
            send(here, here, 10, r_w.at[18 + q], dp=sib)
        else:
            for i in range(1, NX):
                here = wg.at[z, xp(-i), :, c1]
                send(here, here, 10, r_w.at[18], dp=sib)

    def pack(q):
        if q:
            wait(wg.at[zp(-q), :, :, o1], r_w.at[18 + q])
            wait(wg.at[zp(-q), :, :, o0], r_w.at[26 + q])
        else:
            wait(wg.at[z, pl.ds(0, 3), :, o1], r_w.at[18])
            wait(wg.at[z, pl.ds(0, 3), :, o0], r_w.at[1])
        zz = zp(-q)

        def pack_step(i):
            pair = jnp.concatenate([wg[zz, 2 * i].astype(F32), wg[zz, 2 * i + 1].astype(F32)], axis=0)
            wf[pl.ds(pl.multiple_of(96 * zz + 48 * i, 16), 48), :] = pair.astype(BF)

        loop(2, pack_step)

    def embed_some(low, high):
        def body(i):
            embed_step(i + low)

        loop(high - low, body)

    def shift_step(i):
        r0 = pl.multiple_of(i * 32, 32)
        block = fpad[pl.ds(r0, 48), :]
        for t in range(SPAN):
            acols[t, pl.ds(r0, 32), :] = block[t + 6 : t + 38].astype(BF)

    ring1_up(1)
    ring1_down(1)
    wait(wg.at[z, pl.ds(0, 3), :, c0], r_w.at[0])
    for i in range(1, NX):
        here = wg.at[z, xp(-i), :, c0]
        send(here, here, 9, r_w.at[1], dp=sib)
    for h in range(4):
        part = blk0(0, chunk(mine, h))
        send(part, part, 1, r_w.at[34 + 8 * h + 1], **to_z(1))
        send(part, part, 1, r_w.at[34 + 8 * h + 7], **to_z(-1))
    embed_some(0, 4)
    ring1_up(2)
    ring1_down(2)
    embed_step(4)
    for s in range(1, 4):
        for h in range(4):
            ring0(s, h)
            embed_step(1 + 4 * s + h)
            if s == 1 and h == 1:
                ring1_up(3)
                ring1_down(3)
            if s == 2 and h == 1:
                ring1_up(4)
        if s == 2:
            pass_on(0)
        if s == 3:
            pass_on(1)
            pass_on(7)
    head_rows()
    loop(EXT // 32, shift_step)
    pass_on(2)
    pass_on(6)
    pack(0)
    for h in (0, 2, 1, 3):
        ring0(4, h)
        if h == 0:
            pack(1)
            pack(7)
    for q in (3, 5, 4):
        pass_on(q)
    loop(12, head_turn)
    for q in (2, 6, 3, 5, 4):
        pack(q)

    own_cols = pl.ds(pl.multiple_of((WIDTH // 2) * k, 128), WIDTH // 2)
    sib_cols = pl.ds(pl.multiple_of((WIDTH // 2) * (1 - k), 128), WIDTH // 2)
    local = []
    for t in range(SPAN):
        dst = ah.at[pl.ds(0, ROWS), pl.ds(384 * t, 384)]
        copy = pltpu.make_async_copy(acols.at[t, pl.ds(OFF, ROWS), own_cols], dst, s_o.at[t])
        copy.start()
        local.append(copy)
        send(
            acols.at[t, pl.ds(OFF, ROWS), sib_cols], ah.at[pl.ds(ROWS, ROWS), pl.ds(384 * t, 384)],
            2, r_d.at[4], dp=sib,
        )
    ah[:, pl.ds(HALF, 128)] = jnp.zeros((2 * ROWS, 128), BF)
    def conv_step(i):
        o0_ = pl.multiple_of(i * 256, 256)
        total = dot(acols[0], wf[pl.ds(o0_, 256), 0:WIDTH], 1, 1)
        for t in range(1, SPAN):
            total = total + dot(acols[t], wf[pl.ds(o0_, 256), WIDTH * t : WIDTH * (t + 1)], 1, 1)
        mixed[:, pl.ds(o0_, 256)] = total

    loop(3, conv_step, unroll=3)

    pooled = []
    for t in range(4):
        def pool_step(i, total):
            r0 = pl.multiple_of(OFF + 128 * t + 32 * i, 16)
            part = first[pl.ds(r0, 32), :].astype(F32) + gelu_value(mixed[pl.ds(r0, 32), :])
            return total + part.reshape(4, 8, WIDTH).sum(axis=0)

        total = lax.fori_loop(0, 4, pool_step, jnp.zeros((8, WIDTH), F32))
        row = jnp.sum(total, axis=0, keepdims=True) / 128.0
        pooled.append(row)

    pieces = [row[:, 256 * m : 256 * m + 256] for m in range(3) for row in pooled]
    pbuf[z, x] = jnp.concatenate(pieces + [jnp.zeros((4, 256), F32)], axis=0).astype(BF)
    near = (1, 7, 2, 6, 3, 5, 4)
    far = (4, 3, 5, 2, 6, 1, 7, 0)

    def relay_gather(buf, group, rs, between=None):
        own = buf.at[z, x]
        for q in near:
            send(own, own, group, rs.at[q], **to_z(q))
        for i in range(1, NX):
            send(own, own, group, rs.at[0], **to_x(i))
        if between is not None:
            between()
        for q in near:
            here = buf.at[zp(-q), x]
            wait(here, rs.at[q])
            for i in range(1, NX):
                send(here, here, group, rs.at[0], **to_x(i))

    def relay_finish(buf, rs):
        wait(buf.at[:, pl.ds(0, 3)], rs.at[0])

    def scatter_start(src, got, group, rs):
        for q in far:
            for i in range(1, NX):
                send(src.at[zp(q), xp(i)], got.at[i, q], group, rs.at[q], **to_x(i))

    def scatter_turn(src, got, zsrc, zgot, group, rs):
        for q in far:
            total = src[zp(q), x].astype(F32)
            wait(got.at[pl.ds(1, 3), q], rs.at[q])
            for i in range(1, NX):
                total = total + got[i, q].astype(F32)
            if q:
                zsrc[q] = total.astype(BF)
                send(zsrc.at[q], zgot.at[q], group, rs.at[NZ], **to_z(q))
        return total

    def scatter_finish(total, zgot, rs):
        wait(zgot.at[pl.ds(1, 7)], rs.at[NZ])
        for q in near:
            total = total + zgot[q].astype(F32)
        return total

    relay_gather(pbuf, 3, r_p)

    def slope_step(i):
        r0 = pl.multiple_of(i * 32, 32)
        mixed[pl.ds(r0, 32), :] = gelu_slope(mixed[pl.ds(r0, 32), :])

    loop(EXT // 32, slope_step)
    for t in range(SPAN):
        dw2[48 * t : 48 * t + 48, :] = dw[:, WIDTH * t : WIDTH * (t + 1)]
    zero8 = jnp.zeros((8, WIDTH), F32)
    dn_ref[0:8, :] = zero8
    dn_ref[136:144, :] = zero8
    dpad[0:8, :] = zero8
    dpad[136:144, :] = zero8
    dbp[0:8, :] = zero8
    dbp[136:144, :] = zero8
    df_ref[...] = jnp.ones((144, 128), F32)
    relay_finish(pbuf, r_p)

    def coarse_step(i):
        zz, half = i // 2, 2 * (i % 2)
        v0, v1 = pbuf[zz, half].astype(F32), pbuf[zz, half + 1].astype(F32)
        parts = [jnp.concatenate([v0[4 * m : 4 * m + 4], v1[4 * m : 4 * m + 4]], axis=0) for m in range(3)]
        values = jnp.concatenate(parts, axis=1)
        factor = lax.rsqrt(jnp.mean(values * values, axis=1, keepdims=True) + EPSILON)
        normed = values * factor
        r0 = pl.multiple_of(8 * i + 8, 8)
        dn_ref[pl.ds(r0, 8), :] = normed
        df_ref[pl.ds(r0, 8), :] = jnp.broadcast_to(factor, (8, 128))
        dpad[pl.ds(r0, 8), :] = gelu_value(normed).astype(BF).astype(F32)

    loop(16, coarse_step, unroll=4)
    block = dpad[...]
    for t in range(SPAN):
        dcols[t] = block[t + 6 : t + 134].astype(BF)
    total = dot(dw[:, 0:WIDTH], dcols[0], 1, 1)
    for t in range(1, SPAN):
        total = total + dot(dw[:, WIDTH * t : WIDTH * (t + 1)], dcols[t], 1, 1)
    ft[z, x] = total.astype(BF)
    dax[pl.ds(pl.multiple_of(d * 128, 128), 128), :] = dcols[2]

    def dp_slot(ref, i, size):
        return ref.at[pl.ds(pl.multiple_of(i * size, 16), size)]

    def coarse_background():
        for i in range(1, ND):
            send(dcols.at[2], dp_slot(dax, d, 128), 8, r_d.at[0], dp=dpp(i))

    relay_gather(ft, 4, r_f, coarse_background)
    relay_finish(ft, r_f)

    feats = ft[...].reshape(1536, 128)
    logit = dot(hmt[...], feats)
    delta = (cot[...] * jax.nn.sigmoid(logit)).astype(BF)
    dtx[d] = delta
    fbs[...] = dot(hm[...], delta).astype(BF).reshape(NZ, NX, 48, 128)
    scatter_start(fbs, fxr, 5, r_rf)
    for i in range(1, ND):
        send(dtx.at[d], dtx.at[d], 4, r_d.at[1], dp=dpp(i))
        send(ft.at[dpp(i)], fxs.at[d], 4, r_d.at[2], dp=dpp(i))
    fxs[d] = ft[d]

    own_part = scatter_turn(fbs, fxr, fzs, fzr, 5, r_rf)
    fdelta = scatter_finish(own_part, fzr, r_rf).astype(BF)
    fdx[d] = fdelta

    lanes = lax.broadcasted_iota(jnp.int32, (48, 128), 1)

    def shifted(values):
        wide = values.astype(F32)
        parts = []
        for t in range(SPAN):
            move = t - 2
            if move == 0:
                parts.append(wide)
                continue
            turned = pltpu.roll(wide, move % 128, 1)
            keep = lanes >= move if move > 0 else lanes < 128 + move
            parts.append(jnp.where(keep, turned, 0.0))
        return jnp.concatenate(parts, axis=0).astype(BF)

    back = dot(shifted(fdelta), dw2[...], 0, 0)
    dbp[8:136, :] = back

    def piece_step(i):
        block = dbp[pl.ds(pl.multiple_of(8 * i, 8), 24), :]
        zz, half = i // 2, 2 * (i % 2)
        for j, low in ((0, 6), (1, 10)):
            rows = block[low : low + 8]
            dbs[zz, half + j] = jnp.concatenate([rows[:, :384], rows[:, 384:]], axis=0).astype(BF)

    loop(16, piece_step, unroll=4)
    scatter_start(dbs, dxr, 5, r_rd)
    for i in range(1, ND):
        send(fdx.at[d], fdx.at[d], 4, r_d.at[3], dp=dpp(i))
    own_part = scatter_turn(dbs, dxr, dzs, dzr, 5, r_rd)

    wait(dtx.at[pl.ds(0, 7)], r_d.at[1])
    wait(fxs.at[pl.ds(0, 7)], r_d.at[2])
    total = jnp.zeros((256, 192), F32)
    for i in range(ND):
        total = total + dot(dtx[i], fxs[i].reshape(192, 128), 1, 1)
    o_gh[...] = total[:184]
    o_gm[...] = total[192:224]
    store(o_gh, q_gh)
    store(o_gm, q_gm)

    deep_back = scatter_finish(own_part, dzr, r_rd)
    deep_back = jnp.concatenate([deep_back[:8], deep_back[8:]], axis=1)
    r0 = pl.multiple_of(8 * (c // 2), 8)

    def own_rows(ref):
        block = ref[pl.ds(r0, 24), :]
        return jnp.where(c % 2 == 0, block[6:14], block[10:18])

    dnormed = own_rows(dn_ref)
    dfactor = own_rows(df_ref)[:, :1]
    v = deep_back * gelu_slope(dnormed)
    pd_ref[...] = dfactor * (v - dnormed * jnp.mean(v * dnormed, axis=1, keepdims=True)) / 128.0

    fdp[0:8, :] = zero8
    fdp[EXT + 8 : EXT + 16, :] = zero8

    def fine_step(i):
        r0 = pl.multiple_of(i * 16, 16)
        row = pd_ref[pl.ds((r0 + 112) // 128 + 1, 1), :]
        fine = (mixed[pl.ds(r0, 16), :] * row).astype(BF).astype(F32)
        fdp[pl.ds(r0 + 8, 16), :] = fine

    for i in range(4):
        def fine_block(n, i=i):
            fine_step(n + 8 * i + 1)

        loop(8, fine_block, unroll=4)
        block = fdp[OFF + 8 + 128 * i : OFF + 136 + 128 * i, :]
        fdt[0, :, 128 * i : 128 * i + 128] = block.T.astype(BF)
        part = fdt.at[:, :, pl.ds(128 * i, 128)]
        send(part.at[0], part.at[1], 6, r_g.at[0], dp=sib)
    fine_step(0)
    fine_step(EXT // 16 - 1)

    def back_shift(i):
        r0 = pl.multiple_of(i * 32, 32)
        block = fdp[pl.ds(r0, 48), :]
        for t in range(SPAN):
            fdc[t, pl.ds(r0, 32), :] = block[10 - t : 42 - t].astype(BF)

    loop(EXT // 32, back_shift)
    for copy in local:
        copy.wait()
    wait(ah.at[pl.ds(ROWS, ROWS), pl.ds(0, HALF)], r_d.at[4])
    wait(fdt.at[1], r_g.at[0])

    def grad_chunk(low):
        cols = pl.ds(pl.multiple_of(low, 256), 256)
        return dot(fdt[0], ah[pl.ds(0, ROWS), cols]) + dot(fdt[1], ah[pl.ds(ROWS, ROWS), cols])

    def by_x(total, xx):
        return jnp.concatenate(
            [total[24 * (4 * zz + xx) : 24 * (4 * zz + xx) + 24] for zz in range(NZ)], axis=0
        ).astype(BF)

    halves = (pl.ds(0, 144), pl.ds(144, 48))
    pairs = (range(3), range(3, 4))

    def alpha_send(i, h):
        send(
            ga.at[yp(i), :, halves[h]], gar.at[i, :, halves[h]],
            6, r_g.at[1 + h], dp=2 * yp(i) + k,
        )

    def beta_send(yy, i, h):
        send(
            gb.at[xp(i), yy, halves[h]], gbr.at[i, yy, halves[h]],
            6, r_g.at[3 + h], **to_x(i),
        )

    for n in range(NY):
        total = grad_chunk(512 * n + 256)
        for xx in range(NX):
            gb[xx, n] = by_x(total, xx)
        for i in range(1, NX):
            beta_send(n, i, 0)
        yy = yp(n + 1)
        total = grad_chunk(512 * yy)
        for xx in range(NX):
            ga[yy, xx] = by_x(total, xx)
        if n < NY - 1:
            alpha_send(n + 1, 0)
    for n in range(NY):
        for i in range(1, NX):
            beta_send(n, i, 1)
        if n < NY - 1:
            alpha_send(n + 1, 1)

    def second_phase(h):
        wait(gar.at[pl.ds(1, 3), :, halves[h]], r_g.at[1 + h])
        for xx in range(NX):
            for m in pairs[h]:
                rows = pl.ds(48 * m, 48)
                total = ga[y, xx, rows, :].astype(F32)
                for i in range(1, NY):
                    total = total + gar[i, xx, rows, :].astype(F32)
                ha[xx, rows, :] = total.astype(BF)
        for i in range(1, NX):
            send(ha.at[xp(i), halves[h]], har.at[i, halves[h]], 7, r_g.at[5 + h], **to_x(i))
        wait(gbr.at[pl.ds(1, 3), :, halves[h]], r_g.at[3 + h])
        for yy in range(NY):
            for m in pairs[h]:
                rows = pl.ds(48 * m, 48)
                total = gb[x, yy, rows, :].astype(F32)
                for i in range(1, NX):
                    total = total + gbr[i, yy, rows, :].astype(F32)
                hb[yy, rows, :] = total.astype(BF)
        for i in range(1, NY):
            send(
                hb.at[yp(i), halves[h]], hbr.at[i, halves[h]],
                7, r_g.at[7 + h], dp=2 * yp(i) + k,
            )

    def third_copy(zz):
        return pltpu.make_async_remote_copy(
            src_ref=zs.at[zz], dst_ref=zr.at[z], send_sem=s_all.at[7], recv_sem=r_g.at[9],
            device_id={"context": zz * NX + x}, device_id_type=MESH,
        )

    def third_phase(h):
        wait(har.at[pl.ds(1, 3), halves[h]], r_g.at[5 + h])
        wait(hbr.at[pl.ds(1, 3), halves[h]], r_g.at[7 + h])
        for m in pairs[h]:
            rows = pl.ds(48 * m, 48)
            left_half = ha[x, rows, :].astype(F32)
            right_half = hb[y, rows, :].astype(F32)
            for i in range(1, 4):
                left_half = left_half + har[i, rows, :].astype(F32)
                right_half = right_half + hbr[i, rows, :].astype(F32)
            zz = 2 * m
            zs[zz] = jnp.concatenate([left_half[:24], right_half[:24]], axis=0).astype(BF)
            zs[zz + 1] = jnp.concatenate([left_half[24:], right_half[24:]], axis=0).astype(BF)
            for to in (zz, zz + 1):

                @pl.when(z != to)
                def _(to=to):
                    third_copy(to).start()

    def back_step(i):
        cols = 256 * i
        total = dot(fdc[0], wf[:, cols : cols + 256])
        for t in range(1, SPAN):
            total = total + dot(fdc[t], wf[:, WIDTH * t + cols : WIDTH * t + cols + 256])
        fdp[0:EXT, cols : cols + 256] = total

    for i in range(3):
        back_step(i)

    fhl[0, EXT:WIDE, :] = jnp.zeros((WIDE - EXT, WIDTH), BF)
    fhl[1, EXT:WIDE, :] = jnp.zeros((WIDE - EXT, WIDTH), BF)

    def delta_step(i):
        r0 = pl.multiple_of(i * 16, 16)
        row = pd_ref[pl.ds((r0 + 112) // 128 + 1, 1), :]
        normed = nm_ref[pl.ds(r0, 16), :]
        w = fdp[pl.ds(r0, 16), :] * gn_ref[pl.ds(r0, 16), :]
        factor = fac_ref[pl.ds(r0, 16), :][:, :1]
        value = row + factor * (w - normed * jnp.mean(w * normed, axis=1, keepdims=True))
        value = jnp.where(jnp.logical_and(r0 >= OFF, r0 < OFF + ROWS), value, 0.0)
        fdl[pl.ds(r0, 16), :] = value
        high = value.astype(BF)
        fhl[0, pl.ds(r0, 16), :] = high
        fhl[1, pl.ds(r0, 16), :] = (value - high.astype(F32)).astype(BF)

    loop(EXT // 16, delta_step, unroll=2)
    out_copy = pltpu.make_async_copy(fdl.at[pl.ds(OFF, ROWS)], o_fd, s_o.at[5])
    out_copy.start()
    ep[...] = (dot(e_ref[...], fhl[0]) + dot(e_ref[...], fhl[1])).reshape(NZ, 8, WIDTH)
    for q in far[:7]:
        part = ep[zp(q)]
        es[q] = jnp.concatenate([part[:, :384], part[:, 384:]], axis=0).astype(BF)
        send(es.at[q], er.at[q], 7, r_e.at[0], **to_z(q))

    second_phase(0)

    wait(dax.at[pl.ds(0, 896)], r_d.at[0])
    wait(fdx.at[pl.ds(0, 7)], r_d.at[3])
    for i in range(ND):
        fkx[:, 128 * i : 128 * i + 128] = shifted(fdx[i])
    deep_total = dot(fkx[...], dax[...])
    for t in range(SPAN):
        o_gd[:, WIDTH * t : WIDTH * (t + 1)] = deep_total[48 * t : 48 * t + 48]
    store(o_gd, q_gd)

    wait(er.at[pl.ds(1, 7)], r_e.at[0])
    total = er[1].astype(F32)
    for q in near[1:]:
        total = total + er[q].astype(F32)
    own = ep[z]
    ex[x] = (total + jnp.concatenate([own[:, :384], own[:, 384:]], axis=0)).astype(BF)
    for i in range(1, NX):
        send(ex.at[x], ex.at[x], 7, r_e.at[1], **to_x(i))
    second_phase(1)
    third_phase(0)
    wait(ex.at[pl.ds(0, 3)], r_e.at[1])
    total = ex[0].astype(F32)
    for i in range(1, NX):
        total = total + ex[i].astype(F32)
    ey[d] = total.astype(BF)
    for i in range(1, ND):
        send(ey.at[d], ey.at[d], 7, r_e.at[2], dp=dpp(i))
    third_phase(1)
    wait(ey.at[pl.ds(0, 7)], r_e.at[2])
    total = ey[0].astype(F32)
    for i in range(1, ND):
        total = total + ey[i].astype(F32)
    eg[z] = total.astype(BF)
    for i in range(1, NZ):
        send(eg.at[z], eg.at[z], 7, r_e.at[3], **to_z(i))

    total = zs[z].astype(F32)
    wait(zr.at[pl.ds(0, 7)], r_g.at[9])
    for i in range(1, NZ):
        total = total + zr[zp(i)].astype(F32)
    fin[d] = total.astype(BF)
    for i in range(1, NZ):
        count(7, zs.at[i])
    for i in range(1, ND):
        send(fin.at[d], fin.at[d], 7, r_g.at[10], dp=dpp(i))
    wait(eg.at[pl.ds(0, 7)], r_e.at[3])
    blocks = []
    for i in range(NZ):
        block = eg[i].astype(F32)
        blocks.append(jnp.concatenate([block[:8], block[8:]], axis=1))
    for t in range(15):
        for j in range(4):
            row = (15 - t) % 8
            o_ge[4 * t + j : 4 * t + j + 1, :] = blocks[2 * j + (15 - t) // 8][row : row + 1, :]
    store(o_ge, q_ge)
    wait(fin.at[pl.ds(0, 7)], r_g.at[10])
    for i in range(ND):
        for t in range(4):
            tile = 4 * (i // 2) + t
            if tile >= 15:
                continue
            column = 128 * (6 * (tile // 3) + 3 * (i % 2) + tile % 3)
            part = fin[i, 24 * (t // 2) : 24 * (t // 2) + 24, 128 * (t % 2) : 128 * (t % 2) + 128]
            o_gc[:, column : column + 128] = part.astype(F32)
    store(o_gc, q_gc)

    out_copy.wait()
    for out in stores:
        out.wait()
    both = bases.at[:, pl.ds(0, 256)]
    pltpu.make_async_copy(both, both, s_all.at[0]).wait()
    for group in range(1, 11):
        wait_sends(group)


def place(*refs):
    count = 6
    held, sems = refs[2 * count : 3 * count], refs[-1]
    pieces = []
    for i, size in ((5, 128), (2, 24), (1, 24), (0, 60), (3, 184), (4, 32)):
        for low in range(0, held[i].shape[0], size):
            pieces.append((i, pl.ds(low, size)))
    loads, stores = [], []
    for n, (i, rows) in enumerate(pieces):
        loads.append(pltpu.make_async_copy(refs[i].at[rows], held[i].at[rows], sems.at[0, n]))
        stores.append(pltpu.make_async_copy(held[i].at[rows], refs[count + i].at[rows], sems.at[1, n]))
    for load in loads:
        load.start()
    for load, out in zip(loads, stores):
        load.wait()
        out.start()
    for out in stores:
        out.wait()


def shards(bases, organism, embed_weight, conv_weight, deep_weight, human_head, mouse_head, human_cotangent, mouse_cotangent):
    vmem, dma = pltpu.VMEM, pltpu.SemaphoreType.DMA
    scratch = [
        vmem((1, ROWS), jnp.int32), vmem((60, WIDTH), BF), vmem((48, 3840), BF), vmem((184, 1536), BF),
        vmem((32, 1536), BF), vmem((184, 128), BF), vmem((32, 128), BF),
        vmem((60, WIDTH), F32), vmem((24, 3840), F32), vmem((48, 3840), F32), vmem((184, 192), F32), vmem((32, 192), F32),
        vmem((1536, 256), BF), vmem((256, 1536), BF), vmem((256, 128), F32),
        vmem((1, 128), jnp.int32), vmem((1, 128), jnp.int32),
        vmem((64, WIDE), BF), vmem((WIDE, 64), BF), vmem((64, WIDTH), BF),
        vmem((EXT + 16, WIDTH), F32), vmem((EXT, WIDTH), BF), vmem((EXT, WIDTH), F32),
        vmem((EXT, WIDTH), F32), vmem((EXT, 128), F32), vmem((SPAN, EXT, WIDTH), BF),
        vmem((NZ, NX, 24, 3840), BF), vmem((WIDTH, 3840), BF), vmem((EXT, WIDTH), F32),
        vmem((2 * ROWS, 2048), BF),
        vmem((NZ, NX, 16, 256), BF), vmem((144, WIDTH), F32), vmem((144, WIDTH), F32), vmem((144, 128), F32),
        vmem((SPAN, 128, WIDTH), BF), vmem((NZ, NX, 48, 128), BF),
        vmem((ND, 256, 128), BF), vmem((ND, 4, 48, 128), BF),
        vmem((NZ, NX, 48, 128), BF), vmem((4, NZ, 48, 128), BF), vmem((NZ, 48, 128), BF), vmem((NZ, 48, 128), BF),
        vmem((ND, 48, 128), BF), vmem((240, 1024), BF), vmem((240, WIDTH), BF), vmem((144, WIDTH), F32),
        vmem((NZ, NX, 16, 384), BF), vmem((4, NZ, 16, 384), BF), vmem((NZ, 16, 384), BF), vmem((NZ, 16, 384), BF),
        vmem((1024, WIDTH), BF), vmem((8, WIDTH), F32),
        vmem((EXT + 16, WIDTH), F32), vmem((SPAN, EXT, WIDTH), BF), vmem((2, WIDTH, ROWS), BF),
        vmem((NY, NX, 192, 256), BF), vmem((NX, NY, 192, 256), BF),
        vmem((4, NX, 192, 256), BF), vmem((4, NY, 192, 256), BF),
        vmem((NX, 192, 256), BF), vmem((NY, 192, 256), BF), vmem((4, 192, 256), BF), vmem((4, 192, 256), BF),
        vmem((NZ, 48, 256), BF), vmem((NZ, 48, 256), BF), vmem((ND, 48, 256), BF),
        vmem((EXT, WIDTH), F32), vmem((2, WIDE, WIDTH), BF),
        vmem((NZ, 8, WIDTH), F32), vmem((NZ, 16, 384), BF), vmem((NZ, 16, 384), BF), vmem((NX, 16, 384), BF),
        vmem((ND, 16, 384), BF), vmem((NZ, 16, 384), BF),
        dma((11,)), dma((2,)), dma((66,)), dma((8,)), dma((8,)), dma((9,)), dma((9,)), dma((5,)), dma((11,)), dma((4,)),
        dma((6,)), dma((13,)),
    ]
    spec = pl.BlockSpec(memory_space=pl.ANY)
    ge, gc, gd, gh, gm, fd = pl.pallas_call(
        kernel,
        out_shape=(
            jax.ShapeDtypeStruct((60, WIDTH), F32),
            jax.ShapeDtypeStruct((24, 3840), F32),
            jax.ShapeDtypeStruct((48, 3840), F32),
            jax.ShapeDtypeStruct((184, 192), F32),
            jax.ShapeDtypeStruct((32, 192), F32),
            jax.ShapeDtypeStruct((ROWS, WIDTH), F32),
        ),
        in_specs=[spec, pl.BlockSpec(memory_space=pltpu.SMEM)] + [spec] * 7,
        out_specs=(spec,) * 6,
        scratch_shapes=scratch,
        compiler_params=pltpu.CompilerParams(
            collective_id=0, has_side_effects=True, vmem_limit_bytes=60 * 1024 * 1024
        ),
        cost_estimate=pl.CostEstimate(flops=10_000_000_000, bytes_accessed=8_000_000, transcendentals=2_000_000),
    )(
        bases, organism, embed_weight, conv_weight, deep_weight,
        human_head.T, mouse_head.T, human_cotangent[0].T, mouse_cotangent[0].T,
    )
    results = (ge, gc, gd, gh, gm, fd)
    ge, gc, gd, gh, gm, fd = pl.pallas_call(
        place,
        out_shape=tuple(jax.ShapeDtypeStruct(a.shape, a.dtype) for a in results),
        in_specs=[spec] * 6,
        out_specs=(spec,) * 6,
        scratch_shapes=[vmem(a.shape, a.dtype) for a in results] + [dma((2, 10))],
        compiler_params=pltpu.CompilerParams(vmem_limit_bytes=60 * 1024 * 1024),
    )(*results)
    return ge, gc, gd, gh.T, gm.T, fd[None]


def solution(mesh):
    return jax.shard_map(
        shards,
        mesh=mesh,
        in_specs=(
            P("dp", "context"),
            P("dp"),
            P(),
            P("context", None),
            P("context", None),
            P(None, "context"),
            P(None, "context"),
            P("dp", None, "context"),
            P("dp", None, "context"),
        ),
        out_specs=(
            P(),
            P("context", None),
            P("context", None),
            P("dp", "context"),
            P("dp", "context"),
            P("dp", "context", None),
        ),
        check_vma=False,
    )
```
